512 devices in a mesh: space: 32 (over y, x, core), dp: 16 (over z).
Axes of the slice: x: 4, y: 4, z: 16, core: 2. Of those that a mesh axis runs over, the one named last changes fastest.
Arguments:
- features: bfloat16 [2, 128, 32, 128, 128], P(None, 'space', None, 'dp'), may hold values from -6 to 6
- cotangent: bfloat16 [2, 128, 32, 128, 128], P(None, 'space', None, 'dp'), may hold values from -6 to 6
- spectral_weight: bfloat16 [256, 2, 16, 1024], P('space', None, 'dp'), may hold values from -0.75 to 0.75
- mix_weight: bfloat16 [32, 32], replicated, may hold values from -1 to 1
- bias_term: float32 [32], replicated, may hold values from -3 to 3
Outputs:
- activated: bfloat16 [2, 128, 32, 128, 128], P(None, 'space', None, 'dp')
- grad_input: bfloat16 [2, 128, 32, 128, 128], P(None, 'space', None, 'dp')
- grad_spectral: float32 [256, 2, 16, 1024], P('space', None, 'dp')
- grad_mix: float32 [32, 32], replicated
- grad_bias: float32 [32], replicated
The draws below stay inside these ranges and needn't reach their ends.
All inputs are finite; a program needn't handle non-finite values.
Results may differ from the reference program's by a relative error of at most 0.008.
Values sent between devices are 32-bit elements; how exact they have to be, the bound alone decides.
No kernel may reach another device: no remote copies, remote signals or barrier semaphores. Data moves between devices by JAX's collectives and lax.ppermute only.
A program may use at most 64 MiB of HBM per device.

```python
import math
import jax
import jax.numpy as jnp
from jax import lax

C = 32
NZ = 128
KX = 16
KY = 16
KZ = 16
SAMPLES = 2
NX = 128
NY = 128


def level_of(rng, dims, pieces, smallest, top_value):
    factor_of = 1.0
    for position, blocks in pieces:
        steps = jax.random.uniform(jax.random.fold_in(jax.random.fold_in(rng, 6), position), (blocks,), jnp.float32, smallest / len(pieces), top_value / len(pieces))
        factor_of = factor_of * jnp.repeat(jnp.exp(steps), dims[position] // blocks).reshape((-1,) + (1,) * (len(dims) - 1 - position))
    return factor_of


def centred(own_key, dims, width, bound, cuts=(), kind=jnp.bfloat16):
    result = jax.random.normal(own_key, dims, jnp.float32) * width
    if len(cuts) > 0:
        result = level_of(own_key, dims, cuts, -0.22, 0.18) * result
    return jnp.clip(result, min=-bound, max=bound).astype(kind)


def setup_inputs(seed: int = 0) -> dict:
    arg_keys = jax.random.split(jax.random.key(seed), 6)
    return {
        "features": centred(arg_keys[0], (SAMPLES, NX, C, NY, NZ), 1.0, 6.0, ((1, 32), (3, 16))),
        "cotangent": centred(arg_keys[1], (SAMPLES, NX, C, NY, NZ), 1.0, 6.0, ((1, 32), (3, 16))),
        "spectral_weight": centred(arg_keys[2], (KX * KY, 2, KZ, C * C), (2 * C) ** -0.5, 0.75, ((0, 32), (2, 16))),
        "mix_weight": centred(arg_keys[3], (C, C), C ** -0.5, 1.0),
        "bias_term": centred(arg_keys[4], (C,), 0.5, 3.0, (), jnp.float32),
    }


HIGHEST = lax.Precision.HIGHEST
ROOT_HALF = 0.7071067811865476
INV_ROOT_TAU = 0.3989422804014327

def signed_modes(extent):
    indices = jnp.arange(extent, dtype=jnp.int32)
    return jnp.where(indices < extent // 2, indices, indices - extent)

def twiddle(frequencies, places, length):
    phases = frequencies[:, None] * places[None, :] % length
    angles = phases.astype(jnp.float32) * (2.0 * math.pi / length)
    return (jnp.cos(angles), jnp.sin(angles))

def blend(pattern, operand_a, operand_b):
    return jnp.einsum(pattern, operand_a, operand_b, precision=HIGHEST)

def all_tables():
    cosine_z, sine_z = twiddle(jnp.arange(KZ, dtype=jnp.int32), jnp.arange(NZ, dtype=jnp.int32), NZ)
    cosine_y, sine_y = twiddle(signed_modes(KY), jnp.arange(NY, dtype=jnp.int32), NY)
    cosine_x, sine_x = twiddle(signed_modes(KX), jnp.arange(NX, dtype=jnp.int32), NX)
    return (cosine_z, sine_z, cosine_y, sine_y, cosine_x, sine_x)

def analyse(volume):
    cosine_z, sine_z, cosine_y, sine_y, cosine_x, sine_x = all_tables()
    table_z = jnp.concatenate([cosine_z, -sine_z], 0).astype(jnp.bfloat16)
    table_z = lax.optimization_barrier(table_z).astype(jnp.float32)
    z_part = blend('kz,xcyz->kxcy', table_z, volume.astype(jnp.float32))
    z_real, z_imag = (z_part[:KZ], z_part[KZ:])
    y_real = blend('kxcy,by->bkxc', z_real, cosine_y) + blend('kxcy,by->bkxc', z_imag, sine_y)
    y_imag = blend('kxcy,by->bkxc', z_imag, cosine_y) - blend('kxcy,by->bkxc', z_real, sine_y)
    x_real = blend('bkxc,ax->abkc', y_real, cosine_x) + blend('bkxc,ax->abkc', y_imag, sine_x)
    x_imag = blend('bkxc,ax->abkc', y_imag, cosine_x) - blend('bkxc,ax->abkc', y_real, sine_x)
    return (x_real.reshape(KX * KY, KZ, C), x_imag.reshape(KX * KY, KZ, C))

def synthesize(spec_real, spec_imag):
    cosine_z, sine_z, cosine_y, sine_y, cosine_x, sine_x = all_tables()
    part_real = spec_real.reshape(KX, KY, KZ, C)
    part_imag = spec_imag.reshape(KX, KY, KZ, C)
    q_real = blend('abkc,ax->xbkc', part_real, cosine_x) - blend('abkc,ax->xbkc', part_imag, sine_x)
    q_imag = blend('abkc,ax->xbkc', part_imag, cosine_x) + blend('abkc,ax->xbkc', part_real, sine_x)
    r_real = blend('xbkc,by->xcyk', q_real, cosine_y) - blend('xbkc,by->xcyk', q_imag, sine_y)
    r_imag = blend('xbkc,by->xcyk', q_imag, cosine_y) + blend('xbkc,by->xcyk', q_real, sine_y)
    table_z = jnp.concatenate([cosine_z, -sine_z], 0)
    return blend('xcyk,kz->xcyz', jnp.concatenate([r_real, r_imag], -1), table_z)

def reference(features, cotangent, spectral_weight, mix_weight, bias_term):
    cell_count = NX * NY * NZ
    scale_cells = 1.0 / math.sqrt(cell_count)
    scale_modes = 1.0 / math.sqrt(KX * KY * KZ)
    scale_all = 1.0 / math.sqrt(cell_count * SAMPLES)
    weights = spectral_weight.astype(jnp.float32).reshape(KX * KY, 2, KZ, C, C)
    weight_real, weight_imag = (weights[:, 0], weights[:, 1])
    mixing = mix_weight.astype(jnp.float32)
    offsets = bias_term.astype(jnp.float32)[None, :, None, None]

    def one_sample(carry, pair):
        volume, cot_volume = pair
        coeff_real, coeff_imag = analyse(volume)
        coeff_real = coeff_real * scale_cells
        coeff_imag = coeff_imag * scale_cells
        mixed_real = blend('jkc,jkco->jko', coeff_real, weight_real) - blend('jkc,jkco->jko', coeff_imag, weight_imag)
        mixed_imag = blend('jkc,jkco->jko', coeff_real, weight_imag) + blend('jkc,jkco->jko', coeff_imag, weight_real)
        volume_wide = volume.astype(jnp.float32)
        preact = synthesize(mixed_real, mixed_imag) * scale_modes + blend('xcyz,co->xoyz', volume_wide, mixing) + offsets
        normal_cdf = 0.5 * (1.0 + lax.erf(preact * ROOT_HALF))
        activated = (preact * normal_cdf).astype(jnp.bfloat16)
        gelu_slope = normal_cdf + preact * jnp.exp(-0.5 * preact * preact) * INV_ROOT_TAU
        grad_pre = (cot_volume.astype(jnp.float32) * gelu_slope).astype(jnp.bfloat16)
        cot_real, cot_imag = analyse(grad_pre)
        cot_real = cot_real * scale_cells
        cot_imag = cot_imag * scale_cells
        back_real = blend('jko,jkco->jkc', cot_real, weight_real) + blend('jko,jkco->jkc', cot_imag, weight_imag)
        back_imag = blend('jko,jkco->jkc', cot_imag, weight_real) - blend('jko,jkco->jkc', cot_real, weight_imag)
        grad_wide = grad_pre.astype(jnp.float32)
        grad_input = (blend('xoyz,co->xcyz', grad_wide, mixing) + synthesize(back_real, back_imag) * scale_modes).astype(jnp.bfloat16)
        outer_real = blend('jkc,jko->jkco', coeff_real, cot_real) + blend('jkc,jko->jkco', coeff_imag, cot_imag)
        outer_imag = blend('jkc,jko->jkco', coeff_real, cot_imag) - blend('jkc,jko->jkco', coeff_imag, cot_real)
        moments = blend('xcyz,xoyz->co', volume_wide, grad_wide)
        totals = lax.optimization_barrier(jnp.sum(grad_wide, axis=(0, 2, 3)))
        sum_real, sum_imag, sum_mix, sum_bias = carry
        carry = (sum_real + outer_real, sum_imag + outer_imag, sum_mix + moments, sum_bias + totals)
        return (carry, (activated, grad_input))
    start = (jnp.zeros((KX * KY, KZ, C, C), jnp.float32), jnp.zeros((KX * KY, KZ, C, C), jnp.float32), jnp.zeros((C, C), jnp.float32), jnp.zeros((C,), jnp.float32))
    carry, outputs = lax.scan(one_sample, start, (features, cotangent))
    sum_real, sum_imag, sum_mix, sum_bias = carry
    activated, grad_input = outputs
    grad_spectral = jnp.stack([sum_real, sum_imag], 1).reshape(KX * KY, 2, KZ, C * C) / math.sqrt(SAMPLES)
    return (activated, grad_input, grad_spectral, sum_mix * scale_all, sum_bias * scale_all)
```

```python
import math

import jax
import jax.numpy as jnp
import ml_dtypes
import numpy as np
from jax import lax
from jax.experimental import pallas as pl
from jax.experimental.pallas import tpu as pltpu
from jax.sharding import PartitionSpec as P

S, C, N, M = 2, 32, 128, 16
PLANES, ROWS = 4, 8
SPACES, GROUPS = 32, 16
CY = C * ROWS
CO = C * C
BF16, F32 = jnp.bfloat16, jnp.float32
ROOT_HALF = 0.7071067811865476
INV_ROOT_TAU = 0.3989422804014327
SCALE_CELLS = 1.0 / math.sqrt(N * N * N)
SCALE_MODES = 1.0 / math.sqrt(M * M * M)
SCALE_ALL = 1.0 / math.sqrt(N * N * N * S)


def rotation(modes, places):
    phases = modes[:, None] * places[None, :] % N
    angles = phases.astype(np.float32) * np.float32(2.0 * math.pi / N)
    return np.cos(angles.astype(np.float64)), np.sin(angles.astype(np.float64))


def narrow(table):
    return table.astype(np.float32).astype(ml_dtypes.bfloat16)


def halves(table):
    high = narrow(table)
    return high, narrow(table.astype(np.float32) - high.astype(np.float32))


def triple(table):
    high, low = halves(table)
    return np.concatenate([high, high, low], 1)


DEPTH = np.arange(M)
SIGNED = np.where(DEPTH < M // 2, DEPTH, DEPTH - M)
PLACES = np.arange(N)
EYE_XL = np.eye(PLANES)


def z_tables():
    cosine, sine = rotation(DEPTH, PLACES)
    both = np.stack([cosine, -sine], 1).astype(np.float32)
    spread = lambda t: np.einsum("krz,xw->krxwz", t, EYE_XL).reshape(M * 2 * PLANES, PLANES * N)
    forward = spread(narrow(both).astype(np.float32)).astype(ml_dtypes.bfloat16)
    high, low = halves(spread(both))
    return forward, np.concatenate([high, high, low], 0)


def turn(cosine, sine, sign):
    return np.stack([np.stack([cosine, -sign * sine]), np.stack([sign * sine, cosine])])


EYE_CH = np.eye(2)


def x_tables():
    cosine, sine = rotation(SIGNED, PLACES)
    down = turn(cosine, sine, -1).reshape(2, 2, M, SPACES, PLANES) * SCALE_CELLS
    analyse = np.zeros((2, M, 4, 2, SPACES, 2, PLANES))
    for h in range(2):
        for q in range(2):
            analyse[h, :, 2 * q + h, 0] = np.transpose(down[q], (1, 2, 0, 3))
    analyse = analyse[:, :, :, 0].reshape(2, M, 4, SPACES * 2 * PLANES)
    wide = np.zeros((2, M, 8, SPACES * 2 * PLANES))
    wide[:, :, :4] = analyse
    wide = wide.reshape(2, M * 8, -1)
    analyse = np.concatenate([triple(wide[0]), triple(wide[1])], 1)
    up = turn(cosine, sine, 1).reshape(2, 2, M, SPACES, PLANES) * SCALE_MODES
    synth = np.zeros((2, SPACES, 2, PLANES, M, 8))
    for h in range(2):
        for r in range(2):
            synth[h, :, :, :, :, 2 * r + h] = np.transpose(up[:, r], (2, 0, 3, 1))
    synth = synth.reshape(2, SPACES * 2 * PLANES, M * 8)
    return analyse, triple(synth[0]), triple(synth[1])


def y_tables():
    cosine, sine = rotation(SIGNED, np.arange(GROUPS) * ROWS)
    down = turn(cosine, sine, -1)
    analyse = np.zeros((2, 2, M, GROUPS, 8))
    for h in range(2):
        for r in range(2):
            analyse[h, :, :, :, 2 * r + h] = down[:, r]
    analyse = triple(analyse.reshape(2 * 2 * M, GROUPS * 8))
    up = turn(cosine, sine, 1)
    synth = np.zeros((2, GROUPS, 8, 2, M))
    for h in range(2):
        for q in range(2):
            synth[h, :, 2 * q + h] = np.transpose(up[q], (2, 0, 1))
    synth = synth.reshape(2, GROUPS * 8, 2 * M)
    synth = np.concatenate([triple(synth[0]), triple(synth[1])], 1)
    cosine, sine = rotation(SIGNED, np.arange(CY) % ROWS)
    return analyse, synth, cosine.astype(np.float32), sine.astype(np.float32)


def channel_tables():
    first = np.repeat(np.arange(C), ROWS)
    pair_in = np.repeat(np.arange(C), C)
    pair_out = np.tile(np.arange(C), C)
    grow_in = narrow((first[:, None] == pair_in[None, :]).astype(np.float32))
    grow_out = narrow((first[:, None] == pair_out[None, :]).astype(np.float32))
    own = narrow((first[:, None] == np.arange(C)[None, :]).astype(np.float32))
    block = narrow((first[:, None] == first[None, :]).astype(np.float32))
    return grow_in, grow_out, own, block


Z_DOWN, Z_UP = z_tables()
X_DOWN, X_UP_A, X_UP_B = x_tables()
Y_DOWN, Y_UP, ROW_COS, ROW_SIN = y_tables()
GROW_IN, GROW_OUT, OWN, BLOCK = channel_tables()
SUM_IN = np.ascontiguousarray(GROW_IN.T)
SUM_OUT = np.ascontiguousarray(GROW_OUT.T)
OWN_T = np.ascontiguousarray(OWN.T)


def dot(a, b):
    return jnp.dot(a, b, preferred_element_type=F32)


def dot_nt(a, b):
    return lax.dot_general(a, b, (((1,), (1,)), ((), ())), preferred_element_type=F32)


def split(value):
    high = value.astype(BF16)
    return high, (value - high.astype(F32)).astype(BF16)


def stack3(value):
    high, low = split(value)
    return jnp.concatenate([high, low, high], 0)


def apply_exact(value, table):
    high, low = split(value)
    both = dot(jnp.concatenate([high, low], 0), table)
    rows = value.shape[0]
    return both[:rows] + both[rows:]


def row_ids(shape):
    return lax.broadcasted_iota(jnp.int32, shape, len(shape) - 2)


def lane_ids(shape):
    return lax.broadcasted_iota(jnp.int32, shape, len(shape) - 1)


def analyse_depth(planes, table, out_ref):
    for s in range(S):
        field = jnp.concatenate([planes(s, x) for x in range(PLANES)], 1)
        out_ref[:, s] = dot_nt(table, field).reshape(M, 2 * PLANES, CY)


def synth_depth(got_ref, s, table):
    rows = got_ref[:, s].reshape(M * 2 * PLANES, CY)
    high, low = split(rows.T)
    return dot(jnp.concatenate([high, low, high], 1), table)


def depth_kernel(field_ref, table_ref, out_ref):
    analyse_depth(lambda s, x: field_ref[s * PLANES + x], table_ref[...], out_ref)


def prepare_kernel(mix_ref, bias_ref, own_ref, own_t_ref, after_ref, forth_ref, back_ref, bias_out):
    del after_ref
    mix = mix_ref[...]
    own, own_t = own_ref[...], own_t_ref[...]
    same = row_ids((CY, CY)) % ROWS == lane_ids((CY, CY)) % ROWS
    back = dot(dot(own, mix).astype(BF16), own_t)
    forth = dot(dot_nt(own, mix).astype(BF16), own_t)
    back_ref[...] = jnp.where(same, back, 0.0).astype(BF16)
    forth_ref[...] = jnp.where(same, forth, 0.0).astype(BF16)
    bias = jnp.broadcast_to(bias_ref[...], (CY, C))
    picked = jnp.where(lane_ids((CY, C)) == row_ids((CY, C)) // ROWS, bias, 0.0)
    bias_out[...] = jnp.broadcast_to(jnp.sum(picked, 1, keepdims=True), (CY, N))


def plane_kernel(with_sums, got_ref, table_ref, out_ref):
    got = got_ref[...]
    data = got
    if with_sums:
        lead = lax.axis_index("space") < S
        spare = (row_ids(got.shape) % (2 * PLANES) >= PLANES) & lead
        data = jnp.where(spare, 0.0, got)
    half = N
    stacked = jnp.concatenate([stack3(data[:, :half]), stack3(data[:, half:])], 0)
    out = dot(table_ref[...], stacked)
    if with_sums:
        total = jnp.sum(got.reshape(SPACES, 2 * PLANES, CY), 0)
        rows = row_ids((8, half))
        pair = []
        for x in range(2):
            own = total[PLANES + x : PLANES + x + 1]
            pair.append(
                jnp.where(rows == 4, own[:, :half], 0.0) + jnp.where(rows == 5, own[:, half:], 0.0)
            )
        pair = jnp.concatenate(pair, 0)
        out = (out.reshape(GROUPS // 2, 16, half) + pair[None]).reshape(GROUPS * 8, half)
    out_ref[...] = out


def row_spectrum(got_ref, table_ref, cos_ref, sin_ref):
    flat = dot(table_ref[...], stack3(got_ref[...]))
    real = jnp.concatenate([flat[0:M], flat[2 * M : 3 * M]], 1)
    imag = jnp.concatenate([flat[M : 2 * M], flat[3 * M :]], 1)
    cosine, sine = cos_ref[...], sin_ref[...]
    return real * cosine + imag * sine, imag * cosine - real * sine


def weight_rows(mine_ref, other_ref):
    even = lax.axis_index("space") % 2 == 0
    mine, other = mine_ref[...], other_ref[...]
    first = jnp.where(even, mine, other)
    second = jnp.where(even, other, mine)
    whole = jnp.concatenate([first, second], 1)
    return whole[0], whole[1]


def row_synth(real, imag, table_ref, cos_ref, sin_ref):
    cosine, sine = cos_ref[...], sin_ref[...]
    turned = jnp.concatenate([real * cosine - imag * sine, imag * cosine + real * sine], 0)
    stacked = jnp.concatenate([stack3(turned[:, :N]), stack3(turned[:, N:])], 0)
    return dot(table_ref[...], stacked)


def mix_kernel(got_ref, mine_ref, other_ref, down_ref, up_ref, cos_ref, sin_ref, grow_ref, sum_ref, out_ref, coeff_ref):
    real, imag = row_spectrum(got_ref, down_ref, cos_ref, sin_ref)
    coeff = apply_exact(jnp.concatenate([real, imag], 0), grow_ref[...])
    coeff_ref[...] = coeff
    cr, ci = coeff[:M], coeff[M:]
    wr, wi = weight_rows(mine_ref, other_ref)
    mixed = apply_exact(jnp.concatenate([cr * wr - ci * wi, cr * wi + ci * wr], 0), sum_ref[...])
    out_ref[...] = row_synth(mixed[:M], mixed[M:], up_ref, cos_ref, sin_ref)


def back_kernel(got_ref, mine_ref, other_ref, coeff_ref, down_ref, up_ref, cos_ref, sin_ref, grow_ref, sum_ref, out_ref, keep_ref, send_ref):
    real, imag = row_spectrum(got_ref, down_ref, cos_ref, sin_ref)
    cot = apply_exact(jnp.concatenate([real, imag], 0), grow_ref[...])
    dr, di = cot[:M], cot[M:]
    wr, wi = weight_rows(mine_ref, other_ref)
    back = apply_exact(jnp.concatenate([dr * wr + di * wi, di * wr - dr * wi], 0), sum_ref[...])
    out = row_synth(back[:M], back[M:], up_ref, cos_ref, sin_ref)
    total = jnp.sum(got_ref[...].reshape(GROUPS, 8, N), 0)
    rows = row_ids((8, N))
    extra = jnp.where((rows == 4) | (rows == 5), total, 0.0)
    extra = extra + jnp.where(rows == 6, real[0:1, :N], 0.0) + jnp.where(rows == 7, real[0:1, N:], 0.0)
    out_ref[...] = (out.reshape(GROUPS, 8, N) + extra[None]).reshape(GROUPS * 8, N)
    cr, ci = coeff_ref[:M], coeff_ref[M:]
    scale = 1.0 / math.sqrt(S)
    outer_real = (cr * dr + ci * di) * scale
    outer_imag = (cr * di - ci * dr) * scale
    even = lax.axis_index("space") % 2 == 0
    for r, outer in enumerate((outer_real, outer_imag)):
        low, high = outer[: M // 2], outer[M // 2 :]
        keep_ref[r] = jnp.where(even, low, high)
        send_ref[r] = jnp.where(even, high, low)


def spread_kernel(with_sums, got_ref, table_a_ref, table_b_ref, out_ref):
    got = got_ref[...]
    stacked = stack3(got)
    out_a = dot(table_a_ref[...], stacked)
    out_b = dot(table_b_ref[...], stacked)
    if with_sums:
        lead = lax.axis_index("space") < S
        rows = row_ids((8, N))
        spare = (rows >= PLANES) & lead
        for h, out in enumerate((out_a, out_b)):
            slot = jnp.where(rows == 4, got[4 + h : 5 + h], 0.0)
            slot = slot + jnp.where(rows == 5, got[12 + h : 13 + h], 0.0)
            slot = slot + jnp.where(rows == 6, got[6 + h : 7 + h], 0.0)
            out = jnp.where(spare[None], slot[None], out.reshape(SPACES, 8, N))
            out_ref[:, h * N : (h + 1) * N] = out.reshape(SPACES * 8, N)
    else:
        out_ref[:, :N] = out_a
        out_ref[:, N:] = out_b


def gelu_kernel(got_ref, field_ref, cot_ref, forth_ref, bias_ref, up_ref, down_ref, block_ref, act_ref, grad_ref, out_ref):
    forth, bias, up = forth_ref[...], bias_ref[...], up_ref[...]
    moments = jnp.zeros((CY, CY), F32)
    for s in range(S):
        spectral = synth_depth(got_ref, s, up)
        for x in range(PLANES):
            at = s * PLANES + x
            field = field_ref[at]
            preact = spectral[:, x * N : (x + 1) * N] + dot(forth, field) + bias
            normal_cdf = 0.5 * (1.0 + lax.erf(preact * ROOT_HALF))
            act_ref[at] = (preact * normal_cdf).astype(BF16)
            slope = normal_cdf + preact * jnp.exp(-0.5 * preact * preact) * INV_ROOT_TAU
            grad = (cot_ref[at].astype(F32) * slope).astype(BF16)
            grad_ref[at] = grad
            moments = moments + dot_nt(field, grad)
    analyse_depth(lambda s, x: grad_ref[s * PLANES + x], down_ref[...], out_ref)
    same = row_ids((CY, CY)) % ROWS == lane_ids((CY, CY)) % ROWS
    moments = jnp.sum(jnp.where(same, moments, 0.0).reshape(C, ROWS, CY), 1)
    moments = apply_exact(moments, block_ref[...])
    same = row_ids((C, CY)) % ROWS == lane_ids((C, CY)) % ROWS
    moments = jnp.sum(jnp.where(same, moments, 0.0).reshape(C // 8, 8, CY), 1)
    for s in range(S):
        out_ref[0, s, PLANES : PLANES + 2, :] = moments[2 * s : 2 * s + 2]


def input_kernel(got_ref, grad_ref, back_ref, up_ref, own_ref, out_ref, mix_ref, bias_ref):
    back, up, own = back_ref[...], up_ref[...], own_ref[...]
    for s in range(S):
        spectral = synth_depth(got_ref, s, up)
        for x in range(PLANES):
            at = s * PLANES + x
            out_ref[at] = (spectral[:, x * N : (x + 1) * N] + dot(back, grad_ref[at])).astype(BF16)
    rows = []
    for s in range(S):
        for x in range(2):
            rows.append(jnp.broadcast_to(got_ref[0, s, PLANES + x : PLANES + x + 1, :], (8, CY)))
    wide = jnp.concatenate(rows, 0)
    same = row_ids((C, CY)) % ROWS == lane_ids((C, CY)) % ROWS
    mix_ref[...] = apply_exact(jnp.where(same, wide, 0.0), own) * SCALE_ALL
    lead = got_ref[0, 0, PLANES + 2 : PLANES + 3, :] + got_ref[0, 1, PLANES + 2 : PLANES + 3, :]
    lead = jnp.broadcast_to(lead, (16, CY))
    bias_ref[...] = apply_exact(lead, own)[0:8] * (SCALE_ALL / SCALE_CELLS)


def call(kernel, outs, *operands):
    shapes = [jax.ShapeDtypeStruct(shape, kind) for shape, kind in outs]
    operands = [jnp.asarray(x) for x in operands]
    size = sum(math.prod(x.shape) * x.dtype.itemsize for x in operands + shapes)
    return pl.pallas_call(
        kernel,
        out_shape=shapes,
        compiler_params=pltpu.CompilerParams(vmem_limit_bytes=24 * 1024 * 1024),
        cost_estimate=pl.CostEstimate(flops=50_000_000, bytes_accessed=size, transcendentals=0),
    )(*operands)


def swap(value, axis):
    return lax.all_to_all(value, axis, 0, 0, tiled=True)


def on_device(features, cotangent, spectral_weight, mix_weight, bias_term):
    planes = S * PLANES
    field = features.reshape(planes, CY, N)
    cot = cotangent.reshape(planes, CY, N)
    crossing = [
        ((2 * a + h) * GROUPS + b, (2 * b + h) * GROUPS + a)
        for a in range(M)
        for h in range(2)
        for b in range(M)
    ]
    pairing = [(i, i ^ 1) for i in range(SPACES)]
    cross = lambda v: lax.ppermute(v, ("space", "dp"), crossing)
    partner = lambda v: lax.ppermute(v, "space", pairing)

    depth_shape = ((M, S, 2 * PLANES, CY), F32)
    plane_shape = ((GROUPS * 8, N), F32)
    space_shape = ((SPACES * 2 * PLANES, CY), F32)
    flat = lambda v: v.reshape(SPACES * 2 * PLANES, CY)

    def over_space(v):
        return swap(v.reshape(SPACES, 2 * PLANES, CY), "space")

    def over_dp(v):
        return swap(v.reshape(GROUPS, 8, N), "dp").reshape(GROUPS * 8, N)

    (depth,) = call(depth_kernel, [depth_shape], field, Z_DOWN)
    weight = spectral_weight.reshape(M // 2, 2, CO).astype(F32).transpose(1, 0, 2)
    mine = cross(weight)
    forth, back, bias = call(
        prepare_kernel,
        [((CY, CY), BF16), ((CY, CY), BF16), ((CY, N), F32)],
        mix_weight, bias_term.reshape(1, C), OWN, OWN_T, depth[0, 0, :, :N],
    )
    got = flat(over_space(depth))
    (plane,) = call(lambda *r: plane_kernel(False, *r), [plane_shape], got, X_DOWN)
    other = partner(mine)
    got = over_dp(plane)
    mixed, coeff = call(
        mix_kernel, [plane_shape, ((2 * M, CO), F32)],
        got, mine, other, Y_DOWN, Y_UP, ROW_COS, ROW_SIN, GROW_IN, SUM_OUT,
    )
    got = over_dp(mixed)
    (spread,) = call(lambda *r: spread_kernel(False, *r), [space_shape], got, X_UP_A, X_UP_B)
    got = over_space(spread).reshape(M, S, 2 * PLANES, CY)
    wide = ((planes, CY, N), BF16)
    activated, grad, depth = call(
        gelu_kernel, [wide, wide, depth_shape],
        got, field, cot, forth, bias, Z_UP, Z_DOWN, BLOCK,
    )
    got = flat(over_space(depth))
    (plane,) = call(lambda *r: plane_kernel(True, *r), [plane_shape], got, X_DOWN)
    got = over_dp(plane)
    half = ((2, M // 2, CO), F32)
    mixed, keep, send = call(
        back_kernel, [plane_shape, half, half],
        got, mine, other, coeff, Y_DOWN, Y_UP, ROW_COS, ROW_SIN, GROW_OUT, SUM_IN,
    )
    grad_spectral = cross(keep + partner(send))
    got = over_dp(mixed)
    (spread,) = call(lambda *r: spread_kernel(True, *r), [space_shape], got, X_UP_A, X_UP_B)
    got = over_space(spread).reshape(M, S, 2 * PLANES, CY)
    grad_input, grad_mix, grad_bias = call(
        input_kernel, [wide, ((C, C), F32), ((8, C), F32)],
        got, grad, back, Z_UP, OWN,
    )
    return (
        activated.reshape(features.shape),
        grad_input.reshape(features.shape),
        grad_spectral.transpose(1, 0, 2).reshape(M // 2, 2, 1, CO),
        grad_mix,
        grad_bias[0],
    )


def solution(mesh):
    field = P(None, "space", None, "dp", None)
    modes = P("space", None, "dp", None)
    return jax.shard_map(
        on_device,
        mesh=mesh,
        in_specs=(field, field, modes, P(), P()),
        out_specs=(field, field, modes, P(), P()),
        check_vma=False,
    )
```

```python
import math

import jax
import jax.numpy as jnp
import ml_dtypes
import numpy as np
from jax import lax
from jax.experimental import pallas as pl
from jax.experimental.pallas import tpu as pltpu
from jax.sharding import PartitionSpec as P

S, C, N, M = 2, 32, 128, 16
PLANES, ROWS = 4, 8
SPACES, GROUPS = 32, 16
CY = C * ROWS
CO = C * C
BF16, F32 = jnp.bfloat16, jnp.float32
ROOT_HALF = 0.7071067811865476
INV_ROOT_TAU = 0.3989422804014327
SCALE_CELLS = 1.0 / math.sqrt(N * N * N)
SCALE_MODES = 1.0 / math.sqrt(M * M * M)
SCALE_ALL = 1.0 / math.sqrt(N * N * N * S)


def rotation(modes, places):
    phases = modes[:, None] * places[None, :] % N
    angles = phases.astype(np.float32) * np.float32(2.0 * math.pi / N)
    return np.cos(angles.astype(np.float64)), np.sin(angles.astype(np.float64))


def narrow(table):
    return table.astype(np.float32).astype(ml_dtypes.bfloat16)


def halves(table):
    high = narrow(table)
    return high, narrow(table.astype(np.float32) - high.astype(np.float32))


def triple(table):
    high, low = halves(table)
    return np.concatenate([high, high, low], 1)


DEPTH = np.arange(M)
SIGNED = np.where(DEPTH < M // 2, DEPTH, DEPTH - M)
PLACES = np.arange(N)
EYE_XL = np.eye(PLANES)


def z_tables():
    cosine, sine = rotation(DEPTH, PLACES)
    both = np.stack([cosine, -sine], 1).astype(np.float32)
    spread = lambda t: np.einsum("krz,xw->krxwz", t, EYE_XL).reshape(M * 2 * PLANES, PLANES * N)
    forward = spread(narrow(both).astype(np.float32)).astype(ml_dtypes.bfloat16)
    high, low = halves(spread(both))
    return forward, np.concatenate([high, high, low], 0)


def turn(cosine, sine, sign):
    return np.stack([np.stack([cosine, -sign * sine]), np.stack([sign * sine, cosine])])


EYE_CH = np.eye(2)


def x_tables():
    cosine, sine = rotation(SIGNED, PLACES)
    down = turn(cosine, sine, -1).reshape(2, 2, M, SPACES, PLANES) * SCALE_CELLS
    analyse = np.zeros((2, M, 4, 2, SPACES, 2, PLANES))
    for h in range(2):
        for q in range(2):
            analyse[h, :, 2 * q + h, 0] = np.transpose(down[q], (1, 2, 0, 3))
    analyse = analyse[:, :, :, 0].reshape(2, M, 4, SPACES * 2 * PLANES)
    wide = np.zeros((2, M, 8, SPACES * 2 * PLANES))
    wide[:, :, :4] = analyse
    wide = wide.reshape(2, M * 8, -1)
    analyse = np.concatenate([triple(wide[0]), triple(wide[1])], 1)
    up = turn(cosine, sine, 1).reshape(2, 2, M, SPACES, PLANES) * SCALE_MODES
    synth = np.zeros((2, SPACES, 2, PLANES, M, 8))
    for h in range(2):
        for r in range(2):
            synth[h, :, :, :, :, 2 * r + h] = np.transpose(up[:, r], (2, 0, 3, 1))
    synth = synth.reshape(2, SPACES * 2 * PLANES, M * 8)
    return analyse, triple(synth[0]), triple(synth[1])


def y_tables():
    cosine, sine = rotation(SIGNED, np.arange(GROUPS) * ROWS)
    down = turn(cosine, sine, -1)
    analyse = np.zeros((2, 2, M, GROUPS, 8))
    for h in range(2):
        for r in range(2):
            analyse[h, :, :, :, 2 * r + h] = down[:, r]
    analyse = triple(analyse.reshape(2 * 2 * M, GROUPS * 8))
    up = turn(cosine, sine, 1)
    synth = np.zeros((2, GROUPS, 8, 2, M))
    for h in range(2):
        for q in range(2):
            synth[h, :, 2 * q + h] = np.transpose(up[q], (2, 0, 1))
    synth = synth.reshape(2, GROUPS * 8, 2 * M)
    synth = np.concatenate([triple(synth[0]), triple(synth[1])], 1)
    cosine, sine = rotation(SIGNED, np.arange(CY) % ROWS)
    return analyse, synth, cosine.astype(np.float32), sine.astype(np.float32)


def channel_tables():
    first = np.repeat(np.arange(C), ROWS)
    pair_in = np.repeat(np.arange(C), C)
    pair_out = np.tile(np.arange(C), C)
    grow_in = narrow((first[:, None] == pair_in[None, :]).astype(np.float32))
    grow_out = narrow((first[:, None] == pair_out[None, :]).astype(np.float32))
    own = narrow((first[:, None] == np.arange(C)[None, :]).astype(np.float32))
    block = narrow((first[:, None] == first[None, :]).astype(np.float32))
    return grow_in, grow_out, own, block


Z_DOWN, Z_UP = z_tables()
X_DOWN, X_UP_A, X_UP_B = x_tables()
Y_DOWN, Y_UP, ROW_COS, ROW_SIN = y_tables()
GROW_IN, GROW_OUT, OWN, BLOCK = channel_tables()
SUM_IN = np.ascontiguousarray(GROW_IN.T)
SUM_OUT = np.ascontiguousarray(GROW_OUT.T)
OWN_T = np.ascontiguousarray(OWN.T)


def dot(a, b):
    return jnp.dot(a, b, preferred_element_type=F32)


def dot_nt(a, b):
    return lax.dot_general(a, b, (((1,), (1,)), ((), ())), preferred_element_type=F32)


def split(value):
    high = value.astype(BF16)
    return high, (value - high.astype(F32)).astype(BF16)


def stack3(value):
    high, low = split(value)
    return jnp.concatenate([high, low, high], 0)


def apply_exact(value, table):
    high, low = split(value)
    both = dot(jnp.concatenate([high, low], 0), table)
    rows = value.shape[0]
    return both[:rows] + both[rows:]


def row_ids(shape):
    return lax.broadcasted_iota(jnp.int32, shape, len(shape) - 2)


def lane_ids(shape):
    return lax.broadcasted_iota(jnp.int32, shape, len(shape) - 1)


def analyse_depth(planes, table, out_ref):
    for s in range(S):
        field = jnp.concatenate([planes(s, x) for x in range(PLANES)], 1)
        out_ref[:, s] = dot_nt(table, field).reshape(M, 2 * PLANES, CY)


def synth_depth(got_ref, s, table):
    rows = got_ref[:, s].reshape(M * 2 * PLANES, CY)
    high, low = split(rows.T)
    return dot(jnp.concatenate([high, low, high], 1), table)


def depth_kernel(field_ref, table_ref, out_ref):
    analyse_depth(lambda s, x: field_ref[s * PLANES + x], table_ref[...], out_ref)


def prepare_kernel(mix_ref, bias_ref, own_ref, own_t_ref, after_ref, forth_ref, back_ref, bias_out):
    del after_ref
    mix = mix_ref[...]
    own, own_t = own_ref[...], own_t_ref[...]
    same = row_ids((CY, CY)) % ROWS == lane_ids((CY, CY)) % ROWS
    back = dot(dot(own, mix).astype(BF16), own_t)
    forth = dot(dot_nt(own, mix).astype(BF16), own_t)
    back_ref[...] = jnp.where(same, back, 0.0).astype(BF16)
    forth_ref[...] = jnp.where(same, forth, 0.0).astype(BF16)
    bias = jnp.broadcast_to(bias_ref[...], (CY, C))
    picked = jnp.where(lane_ids((CY, C)) == row_ids((CY, C)) // ROWS, bias, 0.0)
    bias_out[...] = jnp.broadcast_to(jnp.sum(picked, 1, keepdims=True), (CY, N))


def plane_kernel(with_sums, got_ref, table_ref, out_ref):
    got = got_ref[...]
    data = got
    if with_sums:
        lead = lax.axis_index("space") < S
        spare = (row_ids(got.shape) % (2 * PLANES) >= PLANES) & lead
        data = jnp.where(spare, 0.0, got)
    half = N
    stacked = jnp.concatenate([stack3(data[:, :half]), stack3(data[:, half:])], 0)
    out = dot(table_ref[...], stacked)
    if with_sums:
        total = jnp.sum(got.reshape(SPACES, 2 * PLANES, CY), 0)
        rows = row_ids((8, half))
        pair = []
        for x in range(2):
            own = total[PLANES + x : PLANES + x + 1]
            pair.append(
                jnp.where(rows == 4, own[:, :half], 0.0) + jnp.where(rows == 5, own[:, half:], 0.0)
            )
        pair = jnp.concatenate(pair, 0)
        out = (out.reshape(GROUPS // 2, 16, half) + pair[None]).reshape(GROUPS * 8, half)
    out_ref[...] = out


def row_spectrum(got_ref, table_ref, cos_ref, sin_ref):
    flat = dot(table_ref[...], stack3(got_ref[...]))
    real = jnp.concatenate([flat[0:M], flat[2 * M : 3 * M]], 1)
    imag = jnp.concatenate([flat[M : 2 * M], flat[3 * M :]], 1)
    cosine, sine = cos_ref[...], sin_ref[...]
    return real * cosine + imag * sine, imag * cosine - real * sine


def weight_rows(mine_ref, other_ref):
    even = lax.axis_index("space") % 2 == 0
    mine, other = mine_ref[...], other_ref[...]
    first = jnp.where(even, mine, other)
    second = jnp.where(even, other, mine)
    whole = jnp.concatenate([first, second], 1)
    return whole[0], whole[1]


def row_synth(real, imag, table_ref, cos_ref, sin_ref):
    cosine, sine = cos_ref[...], sin_ref[...]
    turned = jnp.concatenate([real * cosine - imag * sine, imag * cosine + real * sine], 0)
    stacked = jnp.concatenate([stack3(turned[:, :N]), stack3(turned[:, N:])], 0)
    return dot(table_ref[...], stacked)


def mix_kernel(got_ref, mine_ref, other_ref, down_ref, up_ref, cos_ref, sin_ref, grow_ref, sum_ref, out_ref, coeff_ref):
    real, imag = row_spectrum(got_ref, down_ref, cos_ref, sin_ref)
    coeff = apply_exact(jnp.concatenate([real, imag], 0), grow_ref[...])
    coeff_ref[...] = coeff
    cr, ci = coeff[:M], coeff[M:]
    wr, wi = weight_rows(mine_ref, other_ref)
    mixed = apply_exact(jnp.concatenate([cr * wr - ci * wi, cr * wi + ci * wr], 0), sum_ref[...])
    out_ref[...] = row_synth(mixed[:M], mixed[M:], up_ref, cos_ref, sin_ref)


def back_kernel(got_ref, mine_ref, other_ref, coeff_ref, down_ref, up_ref, cos_ref, sin_ref, grow_ref, sum_ref, out_ref, keep_ref, send_ref):
    real, imag = row_spectrum(got_ref, down_ref, cos_ref, sin_ref)
    cot = apply_exact(jnp.concatenate([real, imag], 0), grow_ref[...])
    dr, di = cot[:M], cot[M:]
    wr, wi = weight_rows(mine_ref, other_ref)
    back = apply_exact(jnp.concatenate([dr * wr + di * wi, di * wr - dr * wi], 0), sum_ref[...])
    out = row_synth(back[:M], back[M:], up_ref, cos_ref, sin_ref)
    total = jnp.sum(got_ref[...].reshape(GROUPS, 8, N), 0)
    rows = row_ids((8, N))
    extra = jnp.where((rows == 4) | (rows == 5), total, 0.0)
    extra = extra + jnp.where(rows == 6, real[0:1, :N], 0.0) + jnp.where(rows == 7, real[0:1, N:], 0.0)
    out_ref[...] = (out.reshape(GROUPS, 8, N) + extra[None]).reshape(GROUPS * 8, N)
    cr, ci = coeff_ref[:M], coeff_ref[M:]
    scale = 1.0 / math.sqrt(S)
    outer_real = (cr * dr + ci * di) * scale
    outer_imag = (cr * di - ci * dr) * scale
    even = lax.axis_index("space") % 2 == 0
    for r, outer in enumerate((outer_real, outer_imag)):
        low, high = outer[: M // 2], outer[M // 2 :]
        keep_ref[r] = jnp.where(even, low, high)
        send_ref[r] = jnp.where(even, high, low)


def spread_kernel(with_sums, got_ref, table_a_ref, table_b_ref, out_ref):
    got = got_ref[...]
    stacked = stack3(got)
    out_a = dot(table_a_ref[...], stacked)
    out_b = dot(table_b_ref[...], stacked)
    if with_sums:
        lead = lax.axis_index("space") < S
        rows = row_ids((8, N))
        spare = (rows >= PLANES) & lead
        for h, out in enumerate((out_a, out_b)):
            slot = jnp.where(rows == 4, got[4 + h : 5 + h], 0.0)
            slot = slot + jnp.where(rows == 5, got[12 + h : 13 + h], 0.0)
            slot = slot + jnp.where(rows == 6, got[6 + h : 7 + h], 0.0)
            out = jnp.where(spare[None], slot[None], out.reshape(SPACES, 8, N))
            out_ref[:, h * N : (h + 1) * N] = out.reshape(SPACES * 8, N)
    else:
        out_ref[:, :N] = out_a
        out_ref[:, N:] = out_b


def gelu_kernel(got_ref, field_ref, cot_ref, forth_ref, bias_ref, up_ref, down_ref, block_ref, act_ref, grad_ref, out_ref):
    forth, bias, up = forth_ref[...], bias_ref[...], up_ref[...]
    moments = jnp.zeros((CY, CY), F32)
    for s in range(S):
        spectral = synth_depth(got_ref, s, up)
        for x in range(PLANES):
            at = s * PLANES + x
            field = field_ref[at]
            preact = spectral[:, x * N : (x + 1) * N] + dot(forth, field) + bias
            normal_cdf = 0.5 * (1.0 + lax.erf(preact * ROOT_HALF))
            act_ref[at] = (preact * normal_cdf).astype(BF16)
            slope = normal_cdf + preact * jnp.exp(-0.5 * preact * preact) * INV_ROOT_TAU
            grad = (cot_ref[at].astype(F32) * slope).astype(BF16)
            grad_ref[at] = grad
            moments = moments + dot_nt(field, grad)
    analyse_depth(lambda s, x: grad_ref[s * PLANES + x], down_ref[...], out_ref)
    same = row_ids((CY, CY)) % ROWS == lane_ids((CY, CY)) % ROWS
    moments = jnp.sum(jnp.where(same, moments, 0.0).reshape(C, ROWS, CY), 1)
    moments = apply_exact(moments, block_ref[...])
    same = row_ids((C, CY)) % ROWS == lane_ids((C, CY)) % ROWS
    moments = jnp.sum(jnp.where(same, moments, 0.0).reshape(C // 8, 8, CY), 1)
    for s in range(S):
        out_ref[0, s, PLANES : PLANES + 2, :] = moments[2 * s : 2 * s + 2]


def input_kernel(got_ref, grad_ref, back_ref, up_ref, own_ref, out_ref, mix_ref, bias_ref):
    back, up, own = back_ref[...], up_ref[...], own_ref[...]
    for s in range(S):
        spectral = synth_depth(got_ref, s, up)
        for x in range(PLANES):
            at = s * PLANES + x
            out_ref[at] = (spectral[:, x * N : (x + 1) * N] + dot(back, grad_ref[at])).astype(BF16)
    rows = []
    for s in range(S):
        for x in range(2):
            rows.append(jnp.broadcast_to(got_ref[0, s, PLANES + x : PLANES + x + 1, :], (8, CY)))
    wide = jnp.concatenate(rows, 0)
    same = row_ids((C, CY)) % ROWS == lane_ids((C, CY)) % ROWS
    mix_ref[...] = apply_exact(jnp.where(same, wide, 0.0), own) * SCALE_ALL
    lead = got_ref[0, 0, PLANES + 2 : PLANES + 3, :] + got_ref[0, 1, PLANES + 2 : PLANES + 3, :]
    lead = jnp.broadcast_to(lead, (16, CY))
    bias_ref[...] = apply_exact(lead, own)[0:8] * (SCALE_ALL / SCALE_CELLS)


def land_kernel(moved_ref, mine_ref):
    mine_ref[...] = moved_ref[...]


def return_kernel(outer_ref, weight_ref):
    for r in range(2):
        weight_ref[:, r, 0] = outer_ref[r]


def call(kernel, outs, *operands, flops=50_000_000):
    shapes = [jax.ShapeDtypeStruct(shape, kind) for shape, kind in outs]
    operands = [jnp.asarray(x) for x in operands]
    size = sum(math.prod(x.shape) * x.dtype.itemsize for x in operands + shapes)
    return pl.pallas_call(
        kernel,
        out_shape=shapes,
        compiler_params=pltpu.CompilerParams(vmem_limit_bytes=24 * 1024 * 1024),
        cost_estimate=pl.CostEstimate(flops=flops, bytes_accessed=size, transcendentals=0),
    )(*operands)


def swap(value, axis):
    return lax.all_to_all(value, axis, 0, 0, tiled=True)


def on_device(features, cotangent, spectral_weight, mix_weight, bias_term):
    planes = S * PLANES
    field = features.reshape(planes, CY, N)
    cot = cotangent.reshape(planes, CY, N)
    crossing = [
        ((2 * a + h) * GROUPS + b, (2 * b + h) * GROUPS + a)
        for a in range(M)
        for h in range(2)
        for b in range(M)
    ]
    pairing = [(i, i ^ 1) for i in range(SPACES)]
    cross = lambda v: lax.ppermute(v, ("space", "dp"), crossing)
    partner = lambda v: lax.ppermute(v, "space", pairing)

    depth_shape = ((M, S, 2 * PLANES, CY), F32)
    plane_shape = ((GROUPS * 8, N), F32)
    space_shape = ((SPACES * 2 * PLANES, CY), F32)
    flat = lambda v: v.reshape(SPACES * 2 * PLANES, CY)

    def over_space(v):
        return swap(v.reshape(SPACES, 2 * PLANES, CY), "space")

    def over_dp(v):
        return swap(v.reshape(GROUPS, 8, N), "dp").reshape(GROUPS * 8, N)

    (depth,) = call(depth_kernel, [depth_shape], field, Z_DOWN)
    weight = spectral_weight.reshape(M // 2, 2, CO).astype(F32).transpose(1, 0, 2)
    mine = cross(weight)
    forth, back, bias = call(
        prepare_kernel,
        [((CY, CY), BF16), ((CY, CY), BF16), ((CY, N), F32)],
        mix_weight, bias_term.reshape(1, C), OWN, OWN_T, depth[0, 0, :, :N],
    )
    got = flat(over_space(depth))
    (plane,) = call(lambda *r: plane_kernel(False, *r), [plane_shape], got, X_DOWN)
    (mine,) = call(land_kernel, [((2, M // 2, CO), F32)], mine, flops=5000000000)
    other = partner(mine)
    got = over_dp(plane)
    mixed, coeff = call(
        mix_kernel, [plane_shape, ((2 * M, CO), F32)],
        got, mine, other, Y_DOWN, Y_UP, ROW_COS, ROW_SIN, GROW_IN, SUM_OUT,
    )
    got = over_dp(mixed)
    (spread,) = call(lambda *r: spread_kernel(False, *r), [space_shape], got, X_UP_A, X_UP_B)
    got = over_space(spread).reshape(M, S, 2 * PLANES, CY)
    wide = ((planes, CY, N), BF16)
    activated, grad, depth = call(
        gelu_kernel, [wide, wide, depth_shape],
        got, field, cot, forth, bias, Z_UP, Z_DOWN, BLOCK,
    )
    got = flat(over_space(depth))
    (plane,) = call(lambda *r: plane_kernel(True, *r), [plane_shape], got, X_DOWN)
    got = over_dp(plane)
    half = ((2, M // 2, CO), F32)
    mixed, keep, send = call(
        back_kernel, [plane_shape, half, half],
        got, mine, other, coeff, Y_DOWN, Y_UP, ROW_COS, ROW_SIN, GROW_OUT, SUM_IN,
    )
    grad_spectral = cross(keep + partner(send))
    got = over_dp(mixed)
    (spread,) = call(lambda *r: spread_kernel(True, *r), [space_shape], got, X_UP_A, X_UP_B)
    got = over_space(spread).reshape(M, S, 2 * PLANES, CY)
    grad_input, grad_mix, grad_bias = call(
        input_kernel, [wide, ((C, C), F32), ((8, C), F32)],
        got, grad, back, Z_UP, OWN,
    )
    (grad_weight,) = call(return_kernel, [((M // 2, 2, 1, CO), F32)], grad_spectral, flops=20_000_000_000)
    return (
        activated.reshape(features.shape),
        grad_input.reshape(features.shape),
        grad_weight,
        grad_mix,
        grad_bias[0],
    )


def solution(mesh):
    field = P(None, "space", None, "dp", None)
    modes = P("space", None, "dp", None)
    return jax.shard_map(
        on_device,
        mesh=mesh,
        in_specs=(field, field, modes, P(), P()),
        out_specs=(field, field, modes, P(), P()),
        check_vma=False,
    )
```

```python
import math

import jax
import jax.numpy as jnp
import ml_dtypes
import numpy as np
from jax import lax
from jax.experimental import pallas as pl
from jax.experimental.pallas import tpu as pltpu
from jax.sharding import PartitionSpec as P

S, C, N, M = 2, 32, 128, 16
PLANES, ROWS = 4, 8
SPACES, GROUPS = 32, 16
CY = C * ROWS
CO = C * C
BF16, F32 = jnp.bfloat16, jnp.float32
ROOT_HALF = 0.7071067811865476
INV_ROOT_TAU = 0.3989422804014327
SCALE_CELLS = 1.0 / math.sqrt(N * N * N)
SCALE_MODES = 1.0 / math.sqrt(M * M * M)
SCALE_ALL = 1.0 / math.sqrt(N * N * N * S)


def rotation(modes, places):
    phases = modes[:, None] * places[None, :] % N
    angles = phases.astype(np.float32) * np.float32(2.0 * math.pi / N)
    return np.cos(angles.astype(np.float64)), np.sin(angles.astype(np.float64))


def narrow(table):
    return table.astype(np.float32).astype(ml_dtypes.bfloat16)


def halves(table):
    high = narrow(table)
    return high, narrow(table.astype(np.float32) - high.astype(np.float32))


def triple(table):
    high, low = halves(table)
    return np.concatenate([high, high, low], 1)


DEPTH = np.arange(M)
SIGNED = np.where(DEPTH < M // 2, DEPTH, DEPTH - M)
PLACES = np.arange(N)
EYE_XL = np.eye(PLANES)


def z_tables():
    cosine, sine = rotation(DEPTH, PLACES)
    both = np.stack([cosine, -sine], 1).astype(np.float32)
    spread = lambda t: np.einsum("krz,xw->krxwz", t, EYE_XL).reshape(M * 2 * PLANES, PLANES * N)
    forward = spread(narrow(both).astype(np.float32)).astype(ml_dtypes.bfloat16)
    high, low = halves(spread(both))
    return forward, np.concatenate([high, high, low], 0)


def turn(cosine, sine, sign):
    return np.stack([np.stack([cosine, -sign * sine]), np.stack([sign * sine, cosine])])


EYE_CH = np.eye(2)


def x_tables():
    cosine, sine = rotation(SIGNED, PLACES)
    down = turn(cosine, sine, -1).reshape(2, 2, M, SPACES, PLANES) * SCALE_CELLS
    analyse = np.zeros((2, M, 4, 2, SPACES, 2, PLANES))
    for h in range(2):
        for q in range(2):
            analyse[h, :, 2 * q + h, 0] = np.transpose(down[q], (1, 2, 0, 3))
    analyse = analyse[:, :, :, 0].reshape(2, M, 4, SPACES * 2 * PLANES)
    wide = np.zeros((2, M, 8, SPACES * 2 * PLANES))
    wide[:, :, :4] = analyse
    wide = wide.reshape(2, M * 8, -1)
    analyse = np.concatenate([triple(wide[0]), triple(wide[1])], 1)
    up = turn(cosine, sine, 1).reshape(2, 2, M, SPACES, PLANES) * SCALE_MODES
    synth = np.zeros((2, SPACES, 2, PLANES, M, 8))
    for h in range(2):
        for r in range(2):
            synth[h, :, :, :, :, 2 * r + h] = np.transpose(up[:, r], (2, 0, 3, 1))
    synth = synth.reshape(2, SPACES * 2 * PLANES, M * 8)
    return analyse, triple(synth[0]), triple(synth[1])


def y_tables():
    cosine, sine = rotation(SIGNED, np.arange(GROUPS) * ROWS)
    down = turn(cosine, sine, -1)
    analyse = np.zeros((2, 2, M, GROUPS, 8))
    for h in range(2):
        for r in range(2):
            analyse[h, :, :, :, 2 * r + h] = down[:, r]
    analyse = triple(analyse.reshape(2 * 2 * M, GROUPS * 8))
    up = turn(cosine, sine, 1)
    synth = np.zeros((2, GROUPS, 8, 2, M))
    for h in range(2):
        for q in range(2):
            synth[h, :, 2 * q + h] = np.transpose(up[q], (2, 0, 1))
    synth = synth.reshape(2, GROUPS * 8, 2 * M)
    synth = np.concatenate([triple(synth[0]), triple(synth[1])], 1)
    cosine, sine = rotation(SIGNED, np.arange(CY) % ROWS)
    return analyse, synth, cosine.astype(np.float32), sine.astype(np.float32)


def channel_tables():
    first = np.repeat(np.arange(C), ROWS)
    pair_in = np.repeat(np.arange(C), C)
    pair_out = np.tile(np.arange(C), C)
    grow_in = narrow((first[:, None] == pair_in[None, :]).astype(np.float32))
    grow_out = narrow((first[:, None] == pair_out[None, :]).astype(np.float32))
    own = narrow((first[:, None] == np.arange(C)[None, :]).astype(np.float32))
    block = narrow((first[:, None] == first[None, :]).astype(np.float32))
    return grow_in, grow_out, own, block


Z_DOWN, Z_UP = z_tables()
X_DOWN, X_UP_A, X_UP_B = x_tables()
Y_DOWN, Y_UP, ROW_COS, ROW_SIN = y_tables()
GROW_IN, GROW_OUT, OWN, BLOCK = channel_tables()
SUM_IN = np.ascontiguousarray(GROW_IN.T)
SUM_OUT = np.ascontiguousarray(GROW_OUT.T)
PACK = np.zeros((2, C, ROWS, 4 * N // 2), OWN.dtype)
for _c in range(C):
    for _s in range(S):
        for _i in range(2):
            PACK[_i, _c, :, _s * N + (2 * _s + _i) * C + _c] = 1
PACK = PACK.reshape(2 * CY, 2 * N)
PAIR_IN = np.ascontiguousarray(GROW_IN[::ROWS])
PAIR_OUT = np.ascontiguousarray(GROW_OUT[::ROWS])
OWN_T = np.ascontiguousarray(OWN.T)


def dot(a, b):
    return jnp.dot(a, b, preferred_element_type=F32)


def dot_nt(a, b):
    return lax.dot_general(a, b, (((1,), (1,)), ((), ())), preferred_element_type=F32)


def split(value):
    high = value.astype(BF16)
    return high, (value - high.astype(F32)).astype(BF16)


def stack3(value):
    high, low = split(value)
    return jnp.concatenate([high, low, high], 0)


def apply_exact(value, table):
    high, low = split(value)
    both = dot(jnp.concatenate([high, low], 0), table)
    rows = value.shape[0]
    return both[:rows] + both[rows:]


def row_ids(shape):
    return lax.broadcasted_iota(jnp.int32, shape, len(shape) - 2)


def lane_ids(shape):
    return lax.broadcasted_iota(jnp.int32, shape, len(shape) - 1)


def analyse_depth(planes, table, out_ref, copies=None):
    for s in range(S):
        if copies is not None:
            copies[s].wait()
        field = jnp.concatenate([planes(s, x) for x in range(PLANES)], 1)
        out_ref[:, s] = dot_nt(table, field).reshape(M, 2 * PLANES, CY)


def synth_depth(got_ref, s, table):
    rows = got_ref[:, s].reshape(M * 2 * PLANES, CY)
    high, low = split(rows.T)
    return dot(jnp.concatenate([high, low, high], 1), table)


def sample_copies(source, target, sems, base):
    out = []
    for s in range(S):
        part = pl.ds(s * PLANES, PLANES)
        out.append(pltpu.make_async_copy(source.at[part], target.at[part], sems.at[base + s]))
    return out


def depth_kernel(field_hbm, table_hbm, out_ref, field_ref, table_ref, sems):
    table_copy = pltpu.make_async_copy(table_hbm, table_ref, sems.at[S])
    copies = sample_copies(field_hbm, field_ref, sems, 0)
    for copy in [table_copy] + copies:
        copy.start()
    table_copy.wait()
    analyse_depth(lambda s, x: field_ref[s * PLANES + x], table_ref[...], out_ref, copies)


def same_row(rows):
    return row_ids((rows, CY)) % ROWS == lane_ids((rows, CY)) % ROWS


def grow_mix(mix_rows, own_t):
    return jnp.where(same_row(CY), dot(mix_rows.astype(BF16), own_t), 0.0).astype(BF16)


def bias_column(bias_ref):
    bias = jnp.broadcast_to(bias_ref[...], (CY, C))
    picked = jnp.where(lane_ids((CY, C)) == row_ids((CY, C)) // ROWS, bias, 0.0)
    return jnp.sum(picked, 1, keepdims=True)


def plane_kernel(with_sums, got_ref, table_ref, out_ref):
    got = got_ref[...]
    data = got
    if with_sums:
        lead = lax.axis_index("space") < S
        spare = (row_ids(got.shape) % (2 * PLANES) >= PLANES) & lead
        data = jnp.where(spare, 0.0, got)
    half = N
    stacked = jnp.concatenate([stack3(data[:, :half]), stack3(data[:, half:])], 0)
    out = dot(table_ref[...], stacked)
    if with_sums:
        total = jnp.sum(got.reshape(SPACES, 2 * PLANES, CY), 0)
        rows = row_ids((8, half))
        pair = []
        for x in range(2):
            own = total[PLANES + x : PLANES + x + 1]
            pair.append(
                jnp.where(rows == 4, own[:, :half], 0.0) + jnp.where(rows == 5, own[:, half:], 0.0)
            )
        pair = jnp.concatenate(pair, 0)
        out = (out.reshape(GROUPS // 2, 16, half) + pair[None]).reshape(GROUPS * 8, half)
    out_ref[...] = out


def row_spectrum(got_ref, table_ref, cos_ref, sin_ref):
    flat = dot(table_ref[...], stack3(got_ref[...]))
    real = jnp.concatenate([flat[0:M], flat[2 * M : 3 * M]], 1)
    imag = jnp.concatenate([flat[M : 2 * M], flat[3 * M :]], 1)
    cosine, sine = cos_ref[...], sin_ref[...]
    return real * cosine + imag * sine, imag * cosine - real * sine


def weight_rows(mine_ref, other_ref):
    even = lax.axis_index("space") % 2 == 0
    mine, other = mine_ref[...], other_ref[...]
    first = jnp.where(even, mine, other)
    second = jnp.where(even, other, mine)
    whole = jnp.concatenate([first, second], 1)
    return whole[0], whole[1]


def row_synth(real, imag, table_ref, cos_ref, sin_ref):
    cosine, sine = cos_ref[...], sin_ref[...]
    turned = jnp.concatenate([real * cosine - imag * sine, imag * cosine + real * sine], 0)
    stacked = jnp.concatenate([stack3(turned[:, :N]), stack3(turned[:, N:])], 0)
    return dot(table_ref[...], stacked)


def mix_kernel(got_ref, mine_ref, other_ref, down_ref, up_ref, cos_ref, sin_ref, grow_ref, sum_ref, out_ref, spectrum_ref):
    real, imag = row_spectrum(got_ref, down_ref, cos_ref, sin_ref)
    spectrum = jnp.concatenate([real, imag], 0)
    spectrum_ref[...] = spectrum
    coeff = apply_exact(spectrum, grow_ref[...])
    cr, ci = coeff[:M], coeff[M:]
    wr, wi = weight_rows(mine_ref, other_ref)
    mixed = apply_exact(jnp.concatenate([cr * wr - ci * wi, cr * wi + ci * wr], 0), sum_ref[...])
    out_ref[...] = row_synth(mixed[:M], mixed[M:], up_ref, cos_ref, sin_ref)


def back_kernel(got_ref, mine_ref, other_ref, down_ref, up_ref, cos_ref, sin_ref, grow_ref, sum_ref, out_ref, spectrum_ref):
    real, imag = row_spectrum(got_ref, down_ref, cos_ref, sin_ref)
    spectrum = jnp.concatenate([real, imag], 0)
    spectrum_ref[...] = spectrum
    cot = apply_exact(spectrum, grow_ref[...])
    dr, di = cot[:M], cot[M:]
    wr, wi = weight_rows(mine_ref, other_ref)
    back = apply_exact(jnp.concatenate([dr * wr + di * wi, di * wr - dr * wi], 0), sum_ref[...])
    out = row_synth(back[:M], back[M:], up_ref, cos_ref, sin_ref)
    total = jnp.sum(got_ref[...].reshape(GROUPS, 8, N), 0)
    rows = row_ids((8, N))
    extra = jnp.where((rows == 4) | (rows == 5), total, 0.0)
    extra = extra + jnp.where(rows == 6, real[0:1, :N], 0.0) + jnp.where(rows == 7, real[0:1, N:], 0.0)
    out_ref[...] = (out.reshape(GROUPS, 8, N) + extra[None]).reshape(GROUPS * 8, N)


def pack_kernel(coeff_ref, cot_ref, pack_ref, out_ref):
    even = lax.axis_index("space") % 2 == 0
    both = jnp.concatenate([coeff_ref[...], cot_ref[...]], 1)
    packed = apply_exact(both, pack_ref[...])
    packed = jnp.where(even, packed[:, :N], packed[:, N:])
    half = M // 2
    low = jnp.concatenate([packed[:half], packed[M : M + half]], 0)
    high = jnp.concatenate([packed[half:M], packed[M + half :]], 0)
    out_ref[0] = jnp.where(even, low, high)
    out_ref[1] = jnp.where(even, high, low)


def part_kernel(moved_ref, keep_ref, send_ref):
    keep_ref[...] = moved_ref[0]
    send_ref[...] = moved_ref[1]


def spread_kernel(with_sums, got_ref, table_a_ref, table_b_ref, out_ref):
    got = got_ref[...]
    stacked = stack3(got)
    out_a = dot(table_a_ref[...], stacked)
    out_b = dot(table_b_ref[...], stacked)
    if with_sums:
        lead = lax.axis_index("space") < S
        rows = row_ids((8, N))
        spare = (rows >= PLANES) & lead
        for h, out in enumerate((out_a, out_b)):
            slot = jnp.where(rows == 4, got[4 + h : 5 + h], 0.0)
            slot = slot + jnp.where(rows == 5, got[12 + h : 13 + h], 0.0)
            slot = slot + jnp.where(rows == 6, got[6 + h : 7 + h], 0.0)
            out = jnp.where(spare[None], slot[None], out.reshape(SPACES, 8, N))
            out_ref[:, h * N : (h + 1) * N] = out.reshape(SPACES * 8, N)
    else:
        out_ref[:, :N] = out_a
        out_ref[:, N:] = out_b


def gelu_kernel(got_ref, field_ref, cot_ref, mix_ref, bias_ref, own_ref, own_t_ref, up_ref, down_ref, block_ref, act_ref, grad_ref, out_ref):
    forth = grow_mix(dot_nt(own_ref[...], mix_ref[...]), own_t_ref[...])
    bias, up = bias_column(bias_ref), up_ref[...]
    moments = jnp.zeros((CY, CY), F32)
    for s in range(S):
        spectral = synth_depth(got_ref, s, up)
        for x in range(PLANES):
            at = s * PLANES + x
            field = field_ref[at]
            preact = spectral[:, x * N : (x + 1) * N] + dot(forth, field) + bias
            normal_cdf = 0.5 * (1.0 + lax.erf(preact * ROOT_HALF))
            act_ref[at] = (preact * normal_cdf).astype(BF16)
            slope = normal_cdf + preact * jnp.exp(-0.5 * preact * preact) * INV_ROOT_TAU
            grad = (cot_ref[at].astype(F32) * slope).astype(BF16)
            grad_ref[at] = grad
            moments = moments + dot_nt(field, grad)
    analyse_depth(lambda s, x: grad_ref[s * PLANES + x], down_ref[...], out_ref)
    same = same_row(CY)
    moments = jnp.sum(jnp.where(same, moments, 0.0).reshape(C, ROWS, CY), 1)
    moments = apply_exact(moments, block_ref[...])
    same = same_row(C)
    moments = jnp.sum(jnp.where(same, moments, 0.0).reshape(C // 8, 8, CY), 1)
    for s in range(S):
        out_ref[0, s, PLANES : PLANES + 2, :] = moments[2 * s : 2 * s + 2]


def input_kernel(got_ref, grad_ref, mix_in_ref, up_ref, own_ref, own_t_ref, out_ref, mix_ref, bias_ref):
    up, own = up_ref[...], own_ref[...]
    back = grow_mix(dot(own, mix_in_ref[...]), own_t_ref[...])
    for s in range(S):
        spectral = synth_depth(got_ref, s, up)
        for x in range(PLANES):
            at = s * PLANES + x
            out_ref[at] = (spectral[:, x * N : (x + 1) * N] + dot(back, grad_ref[at])).astype(BF16)
    rows = []
    for s in range(S):
        for x in range(2):
            rows.append(jnp.broadcast_to(got_ref[0, s, PLANES + x : PLANES + x + 1, :], (8, CY)))
    wide = jnp.concatenate(rows, 0)
    same = same_row(C)
    mix_ref[...] = apply_exact(jnp.where(same, wide, 0.0), own) * SCALE_ALL
    lead = got_ref[0, 0, PLANES + 2 : PLANES + 3, :] + got_ref[0, 1, PLANES + 2 : PLANES + 3, :]
    lead = jnp.broadcast_to(lead, (16, CY))
    bias_ref[...] = apply_exact(lead, own)[0:1] * (SCALE_ALL / SCALE_CELLS)


def land_kernel(moved_ref, mine_ref):
    mine_ref[...] = moved_ref[...]


def outer_kernel(keep_ref, other_ref, grow_in_ref, grow_out_ref, weight_ref):
    packed = keep_ref[...] + other_ref[...]
    part = lambda i: packed[:, i * C : (i + 1) * C]
    coeff = apply_exact(jnp.concatenate([part(0), part(2)], 0), grow_in_ref[...])
    cot = apply_exact(jnp.concatenate([part(1), part(3)], 0), grow_out_ref[...])
    half = M // 2
    real = imag = 0.0
    for s in range(S):
        cr, ci = coeff[s * M : s * M + half], coeff[s * M + half : (s + 1) * M]
        dr, di = cot[s * M : s * M + half], cot[s * M + half : (s + 1) * M]
        real = real + (cr * dr + ci * di)
        imag = imag + (cr * di - ci * dr)
    weight_ref[:, 0, 0] = real * (1.0 / math.sqrt(S))
    weight_ref[:, 1, 0] = imag * (1.0 / math.sqrt(S))


def call(kernel, outs, *operands, flops=50_000_000, far_in=(), far_out=(), scratch=(), room=24):
    shapes = [jax.ShapeDtypeStruct(shape, kind) for shape, kind in outs]
    operands = [jnp.asarray(x) for x in operands]
    size = sum(math.prod(x.shape) * x.dtype.itemsize for x in operands + shapes)
    near, far = pl.BlockSpec(memory_space=pltpu.VMEM), pl.BlockSpec(memory_space=pltpu.HBM)
    return pl.pallas_call(
        kernel,
        out_shape=shapes,
        in_specs=[far if i in far_in else near for i in range(len(operands))],
        out_specs=[far if i in far_out else near for i in range(len(shapes))],
        scratch_shapes=list(scratch),
        compiler_params=pltpu.CompilerParams(vmem_limit_bytes=room * 1024 * 1024),
        cost_estimate=pl.CostEstimate(flops=flops, bytes_accessed=size, transcendentals=0),
    )(*operands)


def swap(value, axis):
    return lax.all_to_all(value, axis, 0, 0, tiled=True)


def on_device(features, cotangent, spectral_weight, mix_weight, bias_term):
    planes = S * PLANES
    field = features.reshape(planes, CY, N)
    cot = cotangent.reshape(planes, CY, N)
    crossing = [
        ((2 * a + h) * GROUPS + b, (2 * b + h) * GROUPS + a)
        for a in range(M)
        for h in range(2)
        for b in range(M)
    ]
    pairing = [(i, i ^ 1) for i in range(SPACES)]
    cross = lambda v: lax.ppermute(v, ("space", "dp"), crossing)
    partner = lambda v: lax.ppermute(v, "space", pairing)

    depth_shape = ((M, S, 2 * PLANES, CY), F32)
    plane_shape = ((GROUPS * 8, N), F32)
    space_shape = ((SPACES * 2 * PLANES, CY), F32)
    flat = lambda v: v.reshape(SPACES * 2 * PLANES, CY)

    def over_space(v):
        return swap(v.reshape(SPACES, 2 * PLANES, CY), "space")

    def over_dp(v):
        return swap(v.reshape(GROUPS, 8, N), "dp").reshape(GROUPS * 8, N)

    planes_scratch = pltpu.VMEM((planes, CY, N), BF16)
    (depth,) = call(
        depth_kernel, [depth_shape], field, Z_DOWN, far_in=(0, 1), room=60,
        scratch=(planes_scratch, pltpu.VMEM(Z_DOWN.shape, BF16), pltpu.SemaphoreType.DMA((S + 1,))),
    )
    weight = spectral_weight.reshape(M // 2, 2, CO).astype(F32).transpose(1, 0, 2)
    mine = cross(weight)
    got = flat(over_space(depth))
    (plane,) = call(lambda *r: plane_kernel(False, *r), [plane_shape], got, X_DOWN)
    (mine,) = call(land_kernel, [((2, M // 2, CO), F32)], mine, flops=5000000000)
    other = partner(mine)
    got = over_dp(plane)
    mixed, coeff = call(
        mix_kernel, [plane_shape, ((2 * M, CY), F32)],
        got, mine, other, Y_DOWN, Y_UP, ROW_COS, ROW_SIN, GROW_IN, SUM_OUT,
    )
    got = over_dp(mixed)
    (spread,) = call(lambda *r: spread_kernel(False, *r), [space_shape], got, X_UP_A, X_UP_B)
    got = over_space(spread).reshape(M, S, 2 * PLANES, CY)
    wide = ((planes, CY, N), BF16)
    activated, grad, depth = call(
        gelu_kernel, [wide, wide, depth_shape],
        got, field, cot, mix_weight, bias_term.reshape(1, C), OWN, OWN_T, Z_UP, Z_DOWN, BLOCK,
    )
    got = flat(over_space(depth))
    (plane,) = call(lambda *r: plane_kernel(True, *r), [plane_shape], got, X_DOWN)
    got = over_dp(plane)
    mixed, cot_coeff = call(
        back_kernel, [plane_shape, ((2 * M, CY), F32)],
        got, mine, other, Y_DOWN, Y_UP, ROW_COS, ROW_SIN, GROW_OUT, SUM_IN,
    )
    half = ((M, N), F32)
    (packed,) = call(pack_kernel, [((2, M, N), F32)], coeff, cot_coeff, PACK)
    keep, send = call(part_kernel, [half, half], cross(packed), flops=5_000_000_000)
    other = partner(send)
    got = over_dp(mixed)
    (spread,) = call(lambda *r: spread_kernel(True, *r), [space_shape], got, X_UP_A, X_UP_B)
    got = over_space(spread).reshape(M, S, 2 * PLANES, CY)
    grad_input, grad_mix, grad_bias = call(
        input_kernel, [wide, ((C, C), F32), ((1, C), F32)],
        got, grad, mix_weight, Z_UP, OWN, OWN_T,
    )
    (grad_weight,) = call(outer_kernel, [((M // 2, 2, 1, CO), F32)], keep, other, PAIR_IN, PAIR_OUT)
    return (
        activated.reshape(features.shape),
        grad_input.reshape(features.shape),
        grad_weight,
        grad_mix,
        grad_bias.reshape(C),
    )


def solution(mesh):
    field = P(None, "space", None, "dp", None)
    modes = P("space", None, "dp", None)
    return jax.shard_map(
        on_device,
        mesh=mesh,
        in_specs=(field, field, modes, P(), P()),
        out_specs=(field, field, modes, P(), P()),
        check_vma=False,
    )
```

```python
import math

import jax
import jax.numpy as jnp
import ml_dtypes
import numpy as np
from jax import lax
from jax.experimental import pallas as pl
from jax.experimental.pallas import tpu as pltpu
from jax.sharding import PartitionSpec as P

S, C, N, M = 2, 32, 128, 16
PLANES, ROWS = 4, 8
SPACES, GROUPS = 32, 16
CY = C * ROWS
CO = C * C
BF16, F32 = jnp.bfloat16, jnp.float32
ROOT_HALF = 0.7071067811865476
INV_ROOT_TAU = 0.3989422804014327
SCALE_CELLS = 1.0 / math.sqrt(N * N * N)
SCALE_MODES = 1.0 / math.sqrt(M * M * M)
SCALE_ALL = 1.0 / math.sqrt(N * N * N * S)


def rotation(modes, places):
    phases = modes[:, None] * places[None, :] % N
    angles = phases.astype(np.float32) * np.float32(2.0 * math.pi / N)
    return np.cos(angles.astype(np.float64)), np.sin(angles.astype(np.float64))


def narrow(table):
    return table.astype(np.float32).astype(ml_dtypes.bfloat16)


def halves(table):
    high = narrow(table)
    return high, narrow(table.astype(np.float32) - high.astype(np.float32))


def triple(table):
    high, low = halves(table)
    return np.concatenate([high, high, low], 1)


DEPTH = np.arange(M)
SIGNED = np.where(DEPTH < M // 2, DEPTH, DEPTH - M)
PLACES = np.arange(N)
EYE_XL = np.eye(PLANES)


def z_tables():
    cosine, sine = rotation(DEPTH, PLACES)
    both = np.stack([cosine, -sine], 1).astype(np.float32)
    spread = lambda t: np.einsum("krz,xw->krxwz", t, EYE_XL).reshape(M * 2 * PLANES, PLANES * N)
    forward = spread(narrow(both).astype(np.float32)).astype(ml_dtypes.bfloat16)
    high, low = halves(spread(both))
    return forward, np.concatenate([high, high, low], 0)


def turn(cosine, sine, sign):
    return np.stack([np.stack([cosine, -sign * sine]), np.stack([sign * sine, cosine])])


EYE_CH = np.eye(2)


def x_tables():
    cosine, sine = rotation(SIGNED, PLACES)
    down = turn(cosine, sine, -1).reshape(2, 2, M, SPACES, PLANES) * SCALE_CELLS
    analyse = np.zeros((2, M, 4, 2, SPACES, 2, PLANES))
    for h in range(2):
        for q in range(2):
            analyse[h, :, 2 * q + h, 0] = np.transpose(down[q], (1, 2, 0, 3))
    analyse = analyse[:, :, :, 0].reshape(2, M, 4, SPACES * 2 * PLANES)
    wide = np.zeros((2, M, 8, SPACES * 2 * PLANES))
    wide[:, :, :4] = analyse
    wide = wide.reshape(2, M * 8, -1)
    analyse = np.concatenate([triple(wide[0]), triple(wide[1])], 1)
    up = turn(cosine, sine, 1).reshape(2, 2, M, SPACES, PLANES) * SCALE_MODES
    synth = np.zeros((2, SPACES, 2, PLANES, M, 8))
    for h in range(2):
        for r in range(2):
            synth[h, :, :, :, :, 2 * r + h] = np.transpose(up[:, r], (2, 0, 3, 1))
    synth = synth.reshape(2, SPACES * 2 * PLANES, M * 8)
    return analyse, triple(synth[0]), triple(synth[1])


def y_tables():
    cosine, sine = rotation(SIGNED, np.arange(GROUPS) * ROWS)
    down = turn(cosine, sine, -1)
    analyse = np.zeros((2, 2, M, GROUPS, 8))
    for h in range(2):
        for r in range(2):
            analyse[h, :, :, :, 2 * r + h] = down[:, r]
    analyse = triple(analyse.reshape(2 * 2 * M, GROUPS * 8))
    up = turn(cosine, sine, 1)
    synth = np.zeros((2, GROUPS, 8, 2, M))
    for h in range(2):
        for q in range(2):
            synth[h, :, 2 * q + h] = np.transpose(up[q], (2, 0, 1))
    synth = synth.reshape(2, GROUPS * 8, 2 * M)
    synth = np.concatenate([triple(synth[0]), triple(synth[1])], 1)
    cosine, sine = rotation(SIGNED, np.arange(CY) % ROWS)
    return analyse, synth, cosine.astype(np.float32), sine.astype(np.float32)


def channel_tables():
    first = np.repeat(np.arange(C), ROWS)
    pair_in = np.repeat(np.arange(C), C)
    pair_out = np.tile(np.arange(C), C)
    grow_in = narrow((first[:, None] == pair_in[None, :]).astype(np.float32))
    grow_out = narrow((first[:, None] == pair_out[None, :]).astype(np.float32))
    own = narrow((first[:, None] == np.arange(C)[None, :]).astype(np.float32))
    block = narrow((first[:, None] == first[None, :]).astype(np.float32))
    return grow_in, grow_out, own, block


Z_DOWN, Z_UP = z_tables()
X_DOWN, X_UP_A, X_UP_B = x_tables()
Y_DOWN, Y_UP, ROW_COS, ROW_SIN = y_tables()
GROW_IN, GROW_OUT, OWN, BLOCK = channel_tables()
SUM_IN = np.ascontiguousarray(GROW_IN.T)
SUM_OUT = np.ascontiguousarray(GROW_OUT.T)
PACK = np.zeros((2, C, ROWS, 4 * N // 2), OWN.dtype)
for _c in range(C):
    for _s in range(S):
        for _i in range(2):
            PACK[_i, _c, :, _s * N + (2 * _s + _i) * C + _c] = 1
PACK = PACK.reshape(2 * CY, 2 * N)
PAIR_IN = np.ascontiguousarray(GROW_IN[::ROWS])
PAIR_OUT = np.ascontiguousarray(GROW_OUT[::ROWS])
OWN_T = np.ascontiguousarray(OWN.T)


SIDE = 4


def plane_steps():
    hops = lambda d, n: min(d, n - d)
    steps = [(y, x) for y in range(SIDE) for x in range(SIDE)]
    steps.sort(key=lambda s: -(hops(s[0], SIDE) + hops(s[1], SIDE)))
    places = sorted(range(GROUPS), key=lambda e: hops(e, GROUPS))
    out = [None] * GROUPS
    for place, step in zip(places, steps):
        out[place] = step
    return out


PLANE_STEPS = plane_steps()


def placed(kz, e):
    dy, dx = PLANE_STEPS[e]
    kx = (kz // SIDE + dy) % SIDE * SIDE + (kz % SIDE + dx) % SIDE
    return kx, (kz + e) % GROUPS


def dot(a, b):
    return jnp.dot(a, b, preferred_element_type=F32)


def dot_nt(a, b):
    return lax.dot_general(a, b, (((1,), (1,)), ((), ())), preferred_element_type=F32)


def split(value):
    high = value.astype(BF16)
    return high, (value - high.astype(F32)).astype(BF16)


def stack3(value):
    high, low = split(value)
    return jnp.concatenate([high, low, high], 0)


def apply_exact(value, table):
    high, low = split(value)
    both = dot(jnp.concatenate([high, low], 0), table)
    rows = value.shape[0]
    return both[:rows] + both[rows:]


def row_ids(shape):
    return lax.broadcasted_iota(jnp.int32, shape, len(shape) - 2)


def lane_ids(shape):
    return lax.broadcasted_iota(jnp.int32, shape, len(shape) - 1)


def analyse_depth(planes, table, out_ref, copies=None):
    for s in range(S):
        if copies is not None:
            copies[s].wait()
        field = jnp.concatenate([planes(s, x) for x in range(PLANES)], 1)
        out_ref[:, s] = dot_nt(table, field).reshape(M, 2 * PLANES, CY)


def synth_depth(got_ref, s, table):
    rows = got_ref[:, s].reshape(M * 2 * PLANES, CY)
    high, low = split(rows.T)
    return dot(jnp.concatenate([high, low, high], 1), table)


def sample_copies(source, target, sems, base):
    out = []
    for s in range(S):
        part = pl.ds(s * PLANES, PLANES)
        out.append(pltpu.make_async_copy(source.at[part], target.at[part], sems.at[base + s]))
    return out


def depth_kernel(field_ref, table_ref, out_ref):
    analyse_depth(lambda s, x: field_ref[s * PLANES + x], table_ref[...], out_ref)


def same_row(rows):
    return row_ids((rows, CY)) % ROWS == lane_ids((rows, CY)) % ROWS


def grow_mix(mix_rows, own_t):
    return jnp.where(same_row(CY), dot(mix_rows.astype(BF16), own_t), 0.0).astype(BF16)


def bias_column(bias_ref):
    bias = jnp.broadcast_to(bias_ref[0:1], (CY, C))
    picked = jnp.where(lane_ids((CY, C)) == row_ids((CY, C)) // ROWS, bias, 0.0)
    return jnp.sum(picked, 1, keepdims=True)


def block_at(i):
    return pl.ds(pl.multiple_of(i * 8, 8), 8)


def plane_kernel(with_sums, got_ref, table_ref, out_ref, held_ref):
    got = got_ref[...]
    data = got
    if with_sums:
        lead = lax.axis_index("space") < S
        spare = (row_ids(got.shape) % (2 * PLANES) >= PLANES) & lead
        data = jnp.where(spare, 0.0, got)
    half = N
    stacked = jnp.concatenate([stack3(data[:, :half]), stack3(data[:, half:])], 0)
    out = dot(table_ref[...], stacked)
    if with_sums:
        total = jnp.sum(got.reshape(SPACES, 2 * PLANES, CY), 0)
        rows = row_ids((8, half))
        pair = []
        for x in range(2):
            own = total[PLANES + x : PLANES + x + 1]
            pair.append(
                jnp.where(rows == 4, own[:, :half], 0.0) + jnp.where(rows == 5, own[:, half:], 0.0)
            )
        pair = jnp.concatenate(pair, 0)
        out = (out.reshape(GROUPS // 2, 16, half) + pair[None]).reshape(GROUPS * 8, half)
    held_ref[...] = out
    kz = lax.axis_index("space") // 2
    for e in range(GROUPS):
        kx, place = placed(kz, e)
        out_ref[block_at(place), :] = held_ref[block_at(kx), :]


def row_spectrum(got_ref, table_ref, cos_ref, sin_ref):
    flat = dot(table_ref[...], stack3(got_ref[...]))
    real = jnp.concatenate([flat[0:M], flat[2 * M : 3 * M]], 1)
    imag = jnp.concatenate([flat[M : 2 * M], flat[3 * M :]], 1)
    cosine, sine = cos_ref[...], sin_ref[...]
    return real * cosine + imag * sine, imag * cosine - real * sine


def weight_rows(mine_ref, other_ref):
    even = lax.axis_index("space") % 2 == 0
    mine, other = mine_ref[...], other_ref[...]
    first = jnp.where(even, mine, other)
    second = jnp.where(even, other, mine)
    whole = jnp.concatenate([first, second], 1)
    return whole[0], whole[1]


def row_synth(real, imag, table_ref, cos_ref, sin_ref):
    cosine, sine = cos_ref[...], sin_ref[...]
    turned = jnp.concatenate([real * cosine - imag * sine, imag * cosine + real * sine], 0)
    stacked = jnp.concatenate([stack3(turned[:, :N]), stack3(turned[:, N:])], 0)
    return dot(table_ref[...], stacked)


def mix_kernel(got_ref, mine_ref, other_ref, down_ref, up_ref, cos_ref, sin_ref, grow_ref, sum_ref, out_ref, spectrum_ref):
    real, imag = row_spectrum(got_ref, down_ref, cos_ref, sin_ref)
    spectrum = jnp.concatenate([real, imag], 0)
    spectrum_ref[...] = spectrum
    coeff = apply_exact(spectrum, grow_ref[...])
    cr, ci = coeff[:M], coeff[M:]
    wr, wi = weight_rows(mine_ref, other_ref)
    mixed = apply_exact(jnp.concatenate([cr * wr - ci * wi, cr * wi + ci * wr], 0), sum_ref[...])
    out_ref[...] = row_synth(mixed[:M], mixed[M:], up_ref, cos_ref, sin_ref)


def back_kernel(got_ref, mine_ref, other_ref, down_ref, up_ref, cos_ref, sin_ref, grow_ref, sum_ref, out_ref, spectrum_ref):
    real, imag = row_spectrum(got_ref, down_ref, cos_ref, sin_ref)
    spectrum = jnp.concatenate([real, imag], 0)
    spectrum_ref[...] = spectrum
    cot = apply_exact(spectrum, grow_ref[...])
    dr, di = cot[:M], cot[M:]
    wr, wi = weight_rows(mine_ref, other_ref)
    back = apply_exact(jnp.concatenate([dr * wr + di * wi, di * wr - dr * wi], 0), sum_ref[...])
    out = row_synth(back[:M], back[M:], up_ref, cos_ref, sin_ref)
    total = jnp.sum(got_ref[...].reshape(GROUPS, 8, N), 0)
    rows = row_ids((8, N))
    extra = jnp.where((rows == 4) | (rows == 5), total, 0.0)
    extra = extra + jnp.where(rows == 6, real[0:1, :N], 0.0) + jnp.where(rows == 7, real[0:1, N:], 0.0)
    out_ref[...] = (out.reshape(GROUPS, 8, N) + extra[None]).reshape(GROUPS * 8, N)


def pack_kernel(coeff_ref, cot_ref, pack_ref, out_ref):
    even = lax.axis_index("space") % 2 == 0
    both = jnp.concatenate([coeff_ref[...], cot_ref[...]], 1)
    packed = apply_exact(both, pack_ref[...])
    packed = jnp.where(even, packed[:, :N], packed[:, N:])
    half = M // 2
    low = jnp.concatenate([packed[:half], packed[M : M + half]], 0)
    high = jnp.concatenate([packed[half:M], packed[M + half :]], 0)
    out_ref[0] = jnp.where(even, low, high)
    out_ref[1] = jnp.where(even, high, low)


def part_kernel(moved_ref, keep_ref, send_ref):
    keep_ref[...] = moved_ref[0]
    send_ref[...] = moved_ref[1]


def spread_kernel(with_sums, got_ref, table_a_ref, table_b_ref, out_ref, held_ref):
    kz = lax.axis_index("space") // 2
    for e in range(GROUPS):
        kx, place = placed(kz, e)
        held_ref[block_at(kx), :] = got_ref[block_at(place), :]
    got = held_ref[...]
    stacked = stack3(got)
    out_a = dot(table_a_ref[...], stacked)
    out_b = dot(table_b_ref[...], stacked)
    if with_sums:
        lead = lax.axis_index("space") < S
        rows = row_ids((8, N))
        spare = (rows >= PLANES) & lead
        for h, out in enumerate((out_a, out_b)):
            slot = jnp.where(rows == 4, got[4 + h : 5 + h], 0.0)
            slot = slot + jnp.where(rows == 5, got[12 + h : 13 + h], 0.0)
            slot = slot + jnp.where(rows == 6, got[6 + h : 7 + h], 0.0)
            out = jnp.where(spare[None], slot[None], out.reshape(SPACES, 8, N))
            out_ref[:, h * N : (h + 1) * N] = out.reshape(SPACES * 8, N)
    else:
        out_ref[:, :N] = out_a
        out_ref[:, N:] = out_b


def gelu_kernel(got_ref, field_ref, cot_ref, mix_ref, bias_ref, own_ref, own_t_ref, up_ref, down_ref, block_ref, act_ref, grad_ref, out_ref):
    forth = grow_mix(dot_nt(own_ref[...], mix_ref[...]), own_t_ref[...])
    bias, up = bias_column(bias_ref), up_ref[...]
    moments = jnp.zeros((CY, CY), F32)
    for s in range(S):
        spectral = synth_depth(got_ref, s, up)
        for x in range(PLANES):
            at = s * PLANES + x
            field = field_ref[at]
            preact = spectral[:, x * N : (x + 1) * N] + dot(forth, field) + bias
            normal_cdf = 0.5 * (1.0 + lax.erf(preact * ROOT_HALF))
            act_ref[at] = (preact * normal_cdf).astype(BF16)
            slope = normal_cdf + preact * jnp.exp(-0.5 * preact * preact) * INV_ROOT_TAU
            grad = (cot_ref[at].astype(F32) * slope).astype(BF16)
            grad_ref[at] = grad
            moments = moments + dot_nt(field, grad)
    analyse_depth(lambda s, x: grad_ref[s * PLANES + x], down_ref[...], out_ref)
    same = same_row(CY)
    moments = jnp.sum(jnp.where(same, moments, 0.0).reshape(C, ROWS, CY), 1)
    moments = apply_exact(moments, block_ref[...])
    same = same_row(C)
    moments = jnp.sum(jnp.where(same, moments, 0.0).reshape(C // 8, 8, CY), 1)
    for s in range(S):
        out_ref[0, s, PLANES : PLANES + 2, :] = moments[2 * s : 2 * s + 2]


def input_kernel(got_ref, grad_ref, mix_in_ref, up_ref, own_ref, own_t_ref, out_ref, mix_ref, bias_ref):
    up, own = up_ref[...], own_ref[...]
    back = grow_mix(dot(own, mix_in_ref[...]), own_t_ref[...])
    for s in range(S):
        spectral = synth_depth(got_ref, s, up)
        for x in range(PLANES):
            at = s * PLANES + x
            out_ref[at] = (spectral[:, x * N : (x + 1) * N] + dot(back, grad_ref[at])).astype(BF16)
    rows = []
    for s in range(S):
        for x in range(2):
            rows.append(jnp.broadcast_to(got_ref[0, s, PLANES + x : PLANES + x + 1, :], (8, CY)))
    wide = jnp.concatenate(rows, 0)
    same = same_row(C)
    mix_ref[...] = apply_exact(jnp.where(same, wide, 0.0), own) * SCALE_ALL
    lead = got_ref[0, 0, PLANES + 2 : PLANES + 3, :] + got_ref[0, 1, PLANES + 2 : PLANES + 3, :]
    lead = jnp.broadcast_to(lead, (16, CY))
    bias_ref[...] = apply_exact(lead, own)[0:1] * (SCALE_ALL / SCALE_CELLS)


def land_kernel(moved_ref, bias_in_ref, mine_ref, bias_ref):
    mine_ref[...] = moved_ref[...]
    bias_ref[...] = jnp.broadcast_to(bias_in_ref[...], (8, C))


def outer_kernel(keep_ref, other_ref, grow_in_ref, grow_out_ref, weight_ref):
    packed = keep_ref[...] + other_ref[...]
    part = lambda i: packed[:, i * C : (i + 1) * C]
    coeff = apply_exact(jnp.concatenate([part(0), part(2)], 0), grow_in_ref[...])
    cot = apply_exact(jnp.concatenate([part(1), part(3)], 0), grow_out_ref[...])
    half = M // 2
    real = imag = 0.0
    for s in range(S):
        cr, ci = coeff[s * M : s * M + half], coeff[s * M + half : (s + 1) * M]
        dr, di = cot[s * M : s * M + half], cot[s * M + half : (s + 1) * M]
        real = real + (cr * dr + ci * di)
        imag = imag + (cr * di - ci * dr)
    weight_ref[:, 0, 0] = real * (1.0 / math.sqrt(S))
    weight_ref[:, 1, 0] = imag * (1.0 / math.sqrt(S))


def call(kernel, outs, *operands, flops=50_000_000, far_in=(), far_out=(), scratch=(), room=24):
    shapes = [jax.ShapeDtypeStruct(shape, kind) for shape, kind in outs]
    operands = [jnp.asarray(x) for x in operands]
    size = sum(math.prod(x.shape) * x.dtype.itemsize for x in operands + shapes)
    near, far = pl.BlockSpec(memory_space=pltpu.VMEM), pl.BlockSpec(memory_space=pltpu.HBM)
    return pl.pallas_call(
        kernel,
        out_shape=shapes,
        in_specs=[far if i in far_in else near for i in range(len(operands))],
        out_specs=[far if i in far_out else near for i in range(len(shapes))],
        scratch_shapes=list(scratch),
        compiler_params=pltpu.CompilerParams(vmem_limit_bytes=room * 1024 * 1024),
        cost_estimate=pl.CostEstimate(flops=flops, bytes_accessed=size, transcendentals=0),
    )(*operands)


def swap(value, axis):
    return lax.all_to_all(value, axis, 0, 0, tiled=True)


def on_device(features, cotangent, spectral_weight, mix_weight, bias_term):
    planes = S * PLANES
    field = features.reshape(planes, CY, N)
    cot = cotangent.reshape(planes, CY, N)
    held = (pltpu.VMEM((GROUPS * 8, N), F32),)
    crossing = []
    for kz in range(M):
        for e in range(GROUPS):
            kx, place = placed(kz, e)
            for h in range(2):
                crossing.append(((2 * kx + h) * GROUPS + kz, (2 * kz + h) * GROUPS + place))
    pairing = [(i, i ^ 1) for i in range(SPACES)]
    cross = lambda v: lax.ppermute(v, ("space", "dp"), crossing)
    cross_home = lambda v: lax.ppermute(v, ("space", "dp"), [(b, a) for a, b in crossing])
    partner = lambda v: lax.ppermute(v, "space", pairing)

    depth_shape = ((M, S, 2 * PLANES, CY), F32)
    plane_shape = ((GROUPS * 8, N), F32)
    space_shape = ((SPACES * 2 * PLANES, CY), F32)
    flat = lambda v: v.reshape(SPACES * 2 * PLANES, CY)

    def over_space(v):
        return swap(v.reshape(SPACES, 2 * PLANES, CY), "space")

    def over_dp(v):
        return swap(v.reshape(GROUPS, 8, N), "dp").reshape(GROUPS * 8, N)

    planes_scratch = pltpu.VMEM((planes, CY, N), BF16)
    (depth,) = call(
        depth_kernel, [depth_shape], field, Z_DOWN, room=60,
    )
    weight = spectral_weight.reshape(M // 2, 2, CO).astype(F32).transpose(1, 0, 2)
    mine = cross(weight)
    got = flat(over_space(depth))
    (plane,) = call(lambda *r: plane_kernel(False, *r), [plane_shape], got, X_DOWN, scratch=held)
    mine, bias = call(land_kernel, [((2, M // 2, CO), F32), ((8, C), F32)], mine, bias_term.reshape(1, C), flops=5000000000)
    other = partner(mine)
    got = over_dp(plane)
    mixed, coeff = call(
        mix_kernel, [plane_shape, ((2 * M, CY), F32)],
        got, mine, other, Y_DOWN, Y_UP, ROW_COS, ROW_SIN, GROW_IN, SUM_OUT,
    )
    got = over_dp(mixed)
    (spread,) = call(lambda *r: spread_kernel(False, *r), [space_shape], got, X_UP_A, X_UP_B, scratch=held)
    got = over_space(spread).reshape(M, S, 2 * PLANES, CY)
    wide = ((planes, CY, N), BF16)
    activated, grad, depth = call(
        gelu_kernel, [wide, wide, depth_shape],
        got, field, cot, mix_weight, bias, OWN, OWN_T, Z_UP, Z_DOWN, BLOCK,
    )
    got = flat(over_space(depth))
    (plane,) = call(lambda *r: plane_kernel(True, *r), [plane_shape], got, X_DOWN, scratch=held)
    got = over_dp(plane)
    mixed, cot_coeff = call(
        back_kernel, [plane_shape, ((2 * M, CY), F32)],
        got, mine, other, Y_DOWN, Y_UP, ROW_COS, ROW_SIN, GROW_OUT, SUM_IN,
    )
    half = ((M, N), F32)
    (packed,) = call(pack_kernel, [((2, M, N), F32)], coeff, cot_coeff, PACK)
    keep, send = call(part_kernel, [half, half], cross_home(packed), flops=5_000_000_000)
    other = partner(send)
    got = over_dp(mixed)
    (spread,) = call(lambda *r: spread_kernel(True, *r), [space_shape], got, X_UP_A, X_UP_B, scratch=held)
    got = over_space(spread).reshape(M, S, 2 * PLANES, CY)
    grad_input, grad_mix, grad_bias = call(
        input_kernel, [wide, ((C, C), F32), ((1, C), F32)],
        got, grad, mix_weight, Z_UP, OWN, OWN_T,
    )
    (grad_weight,) = call(outer_kernel, [((M // 2, 2, 1, CO), F32)], keep, other, PAIR_IN, PAIR_OUT)
    return (
        activated.reshape(features.shape),
        grad_input.reshape(features.shape),
        grad_weight,
        grad_mix,
        grad_bias.reshape(C),
    )


def solution(mesh):
    field = P(None, "space", None, "dp", None)
    modes = P("space", None, "dp", None)
    return jax.shard_map(
        on_device,
        mesh=mesh,
        in_specs=(field, field, modes, P(), P()),
        out_specs=(field, field, modes, P(), P()),
        check_vma=False,
    )
```

```python
import math

import jax
import jax.numpy as jnp
import ml_dtypes
import numpy as np
from jax import lax
from jax.experimental import pallas as pl
from jax.experimental.pallas import tpu as pltpu
from jax.sharding import PartitionSpec as P

S, C, N, M = 2, 32, 128, 16
PLANES, ROWS = 4, 8
SPACES, GROUPS = 32, 16
CY = C * ROWS
CO = C * C
BF16, F32 = jnp.bfloat16, jnp.float32
ROOT_HALF = 0.7071067811865476
INV_ROOT_TAU = 0.3989422804014327
SCALE_CELLS = 1.0 / math.sqrt(N * N * N)
SCALE_MODES = 1.0 / math.sqrt(M * M * M)
SCALE_ALL = 1.0 / math.sqrt(N * N * N * S)


def rotation(modes, places):
    phases = modes[:, None] * places[None, :] % N
    angles = phases.astype(np.float32) * np.float32(2.0 * math.pi / N)
    return np.cos(angles.astype(np.float64)), np.sin(angles.astype(np.float64))


def narrow(table):
    return table.astype(np.float32).astype(ml_dtypes.bfloat16)


def halves(table):
    high = narrow(table)
    return high, narrow(table.astype(np.float32) - high.astype(np.float32))


def triple(table):
    high, low = halves(table)
    return np.concatenate([high, high, low], 1)


DEPTH = np.arange(M)
SIGNED = np.where(DEPTH < M // 2, DEPTH, DEPTH - M)
PLACES = np.arange(N)
EYE_XL = np.eye(PLANES)


def z_tables():
    cosine, sine = rotation(DEPTH, PLACES)
    both = np.stack([cosine, -sine], 1).astype(np.float32)
    spread = lambda t: np.einsum("krz,xw->krxwz", t, EYE_XL).reshape(M * 2 * PLANES, PLANES * N)
    forward = spread(narrow(both).astype(np.float32)).astype(ml_dtypes.bfloat16)
    high, low = halves(spread(both))
    return forward, np.concatenate([high, high, low], 0)


def turn(cosine, sine, sign):
    return np.stack([np.stack([cosine, -sign * sine]), np.stack([sign * sine, cosine])])


EYE_CH = np.eye(2)


def x_tables():
    cosine, sine = rotation(SIGNED, PLACES)
    down = turn(cosine, sine, -1).reshape(2, 2, M, SPACES, PLANES) * SCALE_CELLS
    analyse = np.zeros((2, M, 4, 2, SPACES, 2, PLANES))
    for h in range(2):
        for q in range(2):
            analyse[h, :, 2 * q + h, 0] = np.transpose(down[q], (1, 2, 0, 3))
    analyse = analyse[:, :, :, 0].reshape(2, M, 4, SPACES * 2 * PLANES)
    wide = np.zeros((2, M, 8, SPACES * 2 * PLANES))
    wide[:, :, :4] = analyse
    wide = wide.reshape(2, M * 8, -1)
    analyse = np.concatenate([triple(wide[0]), triple(wide[1])], 1)
    up = turn(cosine, sine, 1).reshape(2, 2, M, SPACES, PLANES) * SCALE_MODES
    synth = np.zeros((2, SPACES, 2, PLANES, M, 8))
    for h in range(2):
        for r in range(2):
            synth[h, :, :, :, :, 2 * r + h] = np.transpose(up[:, r], (2, 0, 3, 1))
    synth = synth.reshape(2, SPACES * 2 * PLANES, M * 8)
    return analyse, triple(synth[0]), triple(synth[1])


def y_tables():
    cosine, sine = rotation(SIGNED, np.arange(GROUPS) * ROWS)
    down = turn(cosine, sine, -1)
    analyse = np.zeros((2, 2, M, GROUPS, 8))
    for h in range(2):
        for r in range(2):
            analyse[h, :, :, :, 2 * r + h] = down[:, r]
    analyse = triple(analyse.reshape(2 * 2 * M, GROUPS * 8))
    up = turn(cosine, sine, 1)
    synth = np.zeros((2, GROUPS, 8, 2, M))
    for h in range(2):
        for q in range(2):
            synth[h, :, 2 * q + h] = np.transpose(up[q], (2, 0, 1))
    synth = synth.reshape(2, GROUPS * 8, 2 * M)
    synth = np.concatenate([triple(synth[0]), triple(synth[1])], 1)
    cosine, sine = rotation(SIGNED, np.arange(CY) % ROWS)
    return analyse, synth, cosine.astype(np.float32), sine.astype(np.float32)


def channel_tables():
    first = np.repeat(np.arange(C), ROWS)
    pair_in = np.repeat(np.arange(C), C)
    pair_out = np.tile(np.arange(C), C)
    grow_in = narrow((first[:, None] == pair_in[None, :]).astype(np.float32))
    grow_out = narrow((first[:, None] == pair_out[None, :]).astype(np.float32))
    own = narrow((first[:, None] == np.arange(C)[None, :]).astype(np.float32))
    block = narrow((first[:, None] == first[None, :]).astype(np.float32))
    return grow_in, grow_out, own, block


Z_DOWN, Z_UP = z_tables()
X_DOWN, X_UP_A, X_UP_B = x_tables()
Y_DOWN, Y_UP, ROW_COS, ROW_SIN = y_tables()
GROW_IN, GROW_OUT, OWN, BLOCK = channel_tables()
SUM_IN = np.ascontiguousarray(GROW_IN.T)
SUM_OUT = np.ascontiguousarray(GROW_OUT.T)
PACK = np.zeros((2, C, ROWS, 4 * N // 2), OWN.dtype)
for _c in range(C):
    for _s in range(S):
        for _i in range(2):
            PACK[_i, _c, :, _s * N + (2 * _s + _i) * C + _c] = 1
PACK = PACK.reshape(2 * CY, 2 * N)
PAIR_IN = np.ascontiguousarray(GROW_IN[::ROWS])
PAIR_OUT = np.ascontiguousarray(GROW_OUT[::ROWS])
OWN_T = np.ascontiguousarray(OWN.T)
X_DOWN_4 = X_DOWN.reshape(M, 8, -1)[:, :4].reshape(M * 4, -1)
Y_DOWN_4 = Y_DOWN.reshape(-1, 3, GROUPS, 8)[..., :4].reshape(4 * M, -1)
Y_UP_4 = Y_UP.reshape(GROUPS, 8, -1)[:, :4].reshape(GROUPS * 4, -1)
X_UP_A_4 = X_UP_A.reshape(-1, 3, M, 8)[..., :4].reshape(SPACES * 8, -1)
X_UP_B_4 = X_UP_B.reshape(-1, 3, M, 8)[..., :4].reshape(SPACES * 8, -1)


SIDE = 4


def plane_steps():
    hops = lambda d, n: min(d, n - d)
    steps = [(y, x) for y in range(SIDE) for x in range(SIDE)]
    steps.sort(key=lambda s: -(hops(s[0], SIDE) + hops(s[1], SIDE)))
    places = sorted(range(GROUPS), key=lambda e: hops(e, GROUPS))
    out = [None] * GROUPS
    for place, step in zip(places, steps):
        out[place] = step
    return out


PLANE_STEPS = plane_steps()


def placed(kz, e):
    dy, dx = PLANE_STEPS[e]
    kx = (kz // SIDE + dy) % SIDE * SIDE + (kz % SIDE + dx) % SIDE
    return kx, (kz + e) % GROUPS


def dot(a, b):
    return jnp.dot(a, b, preferred_element_type=F32)


def dot_nt(a, b):
    return lax.dot_general(a, b, (((1,), (1,)), ((), ())), preferred_element_type=F32)


def split(value):
    high = value.astype(BF16)
    return high, (value - high.astype(F32)).astype(BF16)


def stack3(value):
    high, low = split(value)
    return jnp.concatenate([high, low, high], 0)


def apply_exact(value, table):
    high, low = split(value)
    both = dot(jnp.concatenate([high, low], 0), table)
    rows = value.shape[0]
    return both[:rows] + both[rows:]


def row_ids(shape):
    return lax.broadcasted_iota(jnp.int32, shape, len(shape) - 2)


def lane_ids(shape):
    return lax.broadcasted_iota(jnp.int32, shape, len(shape) - 1)


def analyse_depth(planes, table, out_ref, copies=None):
    for s in range(S):
        if copies is not None:
            copies[s].wait()
        field = jnp.concatenate([planes(s, x) for x in range(PLANES)], 1)
        out_ref[:, s] = dot_nt(table, field).reshape(M, 2 * PLANES, CY)


def synth_depth(got_ref, s, table):
    rows = got_ref[:, s].reshape(M * 2 * PLANES, CY)
    high, low = split(rows.T)
    return dot(jnp.concatenate([high, low, high], 1), table)


def sample_copies(source, target, sems, base):
    out = []
    for s in range(S):
        part = pl.ds(s * PLANES, PLANES)
        out.append(pltpu.make_async_copy(source.at[part], target.at[part], sems.at[base + s]))
    return out


def depth_kernel(field_ref, table_ref, out_ref):
    analyse_depth(lambda s, x: field_ref[s * PLANES + x], table_ref[...], out_ref)


def same_row(rows):
    return row_ids((rows, CY)) % ROWS == lane_ids((rows, CY)) % ROWS


def grow_mix(mix_rows, own_t):
    return jnp.where(same_row(CY), dot(mix_rows.astype(BF16), own_t), 0.0).astype(BF16)


def bias_column(bias_ref):
    bias = jnp.broadcast_to(bias_ref[0:1], (CY, C))
    picked = jnp.where(lane_ids((CY, C)) == row_ids((CY, C)) // ROWS, bias, 0.0)
    return jnp.sum(picked, 1, keepdims=True)


def put_blocks(value, blocks_ref):
    rows = blocks_ref.shape[1]
    for i in range(GROUPS):
        blocks_ref[i] = value[i * rows : (i + 1) * rows]


def take_blocks(blocks_ref, flat_ref):
    rows = blocks_ref.shape[1]
    for i in range(GROUPS):
        flat_ref[i * rows : (i + 1) * rows, :] = blocks_ref[i]
    return flat_ref[...]


def plane_kernel(with_sums, got_ref, table_ref, out_ref, held_ref):
    got = got_ref[...]
    data = got
    if with_sums:
        lead = lax.axis_index("space") < S
        spare = (row_ids(got.shape) % (2 * PLANES) >= PLANES) & lead
        data = jnp.where(spare, 0.0, got)
    half = N
    stacked = jnp.concatenate([stack3(data[:, :half]), stack3(data[:, half:])], 0)
    out = dot(table_ref[...], stacked)
    if with_sums:
        total = jnp.sum(got.reshape(SPACES, 2 * PLANES, CY), 0)
        rows = row_ids((8, half))
        pair = []
        for x in range(2):
            own = total[PLANES + x : PLANES + x + 1]
            pair.append(
                jnp.where(rows == 4, own[:, :half], 0.0) + jnp.where(rows == 5, own[:, half:], 0.0)
            )
        pair = jnp.concatenate(pair, 0)
        out = (out.reshape(GROUPS // 2, 16, half) + pair[None]).reshape(GROUPS * 8, half)
    kz = lax.axis_index("space") // 2
    put_blocks(out, held_ref)
    for e in range(GROUPS):
        kx, place = placed(kz, e)
        out_ref[place] = held_ref[kx]


def row_spectrum(got, table_ref, cos_ref, sin_ref):
    flat = dot(table_ref[...], stack3(got))
    real = jnp.concatenate([flat[0:M], flat[2 * M : 3 * M]], 1)
    imag = jnp.concatenate([flat[M : 2 * M], flat[3 * M :]], 1)
    cosine, sine = cos_ref[...], sin_ref[...]
    return real * cosine + imag * sine, imag * cosine - real * sine


def weight_rows(mine_ref, other_ref):
    even = lax.axis_index("space") % 2 == 0
    mine, other = mine_ref[...], other_ref[...]
    first = jnp.where(even, mine, other)
    second = jnp.where(even, other, mine)
    whole = jnp.concatenate([first, second], 1)
    return whole[0], whole[1]


def row_synth(real, imag, table_ref, cos_ref, sin_ref):
    cosine, sine = cos_ref[...], sin_ref[...]
    turned = jnp.concatenate([real * cosine - imag * sine, imag * cosine + real * sine], 0)
    stacked = jnp.concatenate([stack3(turned[:, :N]), stack3(turned[:, N:])], 0)
    return dot(table_ref[...], stacked)


def mix_kernel(got_ref, mine_ref, other_ref, down_ref, up_ref, cos_ref, sin_ref, grow_ref, sum_ref, out_ref, spectrum_ref, flat_ref):
    real, imag = row_spectrum(take_blocks(got_ref, flat_ref), down_ref, cos_ref, sin_ref)
    spectrum = jnp.concatenate([real, imag], 0)
    spectrum_ref[...] = spectrum
    coeff = apply_exact(spectrum, grow_ref[...])
    cr, ci = coeff[:M], coeff[M:]
    wr, wi = weight_rows(mine_ref, other_ref)
    mixed = apply_exact(jnp.concatenate([cr * wr - ci * wi, cr * wi + ci * wr], 0), sum_ref[...])
    put_blocks(row_synth(mixed[:M], mixed[M:], up_ref, cos_ref, sin_ref), out_ref)


def back_kernel(got_ref, mine_ref, other_ref, down_ref, up_ref, cos_ref, sin_ref, grow_ref, sum_ref, pack_ref, coeff_ref, out_ref, packed_ref):
    real, imag = row_spectrum(got_ref[...].reshape(GROUPS * 8, N), down_ref, cos_ref, sin_ref)
    spectrum = jnp.concatenate([real, imag], 0)
    pack(coeff_ref[...], spectrum, pack_ref[...], packed_ref)
    cot = apply_exact(spectrum, grow_ref[...])
    dr, di = cot[:M], cot[M:]
    wr, wi = weight_rows(mine_ref, other_ref)
    back = apply_exact(jnp.concatenate([dr * wr + di * wi, di * wr - dr * wi], 0), sum_ref[...])
    out = row_synth(back[:M], back[M:], up_ref, cos_ref, sin_ref)
    total = jnp.sum(got_ref[...], 0)
    rows = row_ids((8, N))
    extra = jnp.where((rows == 4) | (rows == 5), total, 0.0)
    extra = extra + jnp.where(rows == 6, real[0:1, :N], 0.0) + jnp.where(rows == 7, real[0:1, N:], 0.0)
    out_ref[...] = out.reshape(GROUPS, 8, N) + extra[None]


def pack(coeff, cot, table, out_ref):
    even = lax.axis_index("space") % 2 == 0
    packed = apply_exact(jnp.concatenate([coeff, cot], 1), table)
    packed = jnp.where(even, packed[:, :N], packed[:, N:])
    half = M // 2
    low = jnp.concatenate([packed[:half], packed[M : M + half]], 0)
    high = jnp.concatenate([packed[half:M], packed[M + half :]], 0)
    out_ref[0] = jnp.where(even, low, high)
    out_ref[1] = jnp.where(even, high, low)


def part_kernel(moved_ref, keep_ref, send_ref):
    keep_ref[...] = moved_ref[0]
    send_ref[...] = moved_ref[1]


def spread_kernel(with_sums, got_ref, table_a_ref, table_b_ref, out_ref, held_ref, flat_ref):
    kz = lax.axis_index("space") // 2
    for e in range(GROUPS):
        kx, place = placed(kz, e)
        held_ref[kx] = got_ref[place]
    got = take_blocks(held_ref, flat_ref)
    stacked = stack3(got)
    out_a = dot(table_a_ref[...], stacked)
    out_b = dot(table_b_ref[...], stacked)
    if with_sums:
        lead = lax.axis_index("space") < S
        rows = row_ids((8, N))
        spare = (rows >= PLANES) & lead
        for h, out in enumerate((out_a, out_b)):
            slot = jnp.where(rows == 4, got[4 + h : 5 + h], 0.0)
            slot = slot + jnp.where(rows == 5, got[12 + h : 13 + h], 0.0)
            slot = slot + jnp.where(rows == 6, got[6 + h : 7 + h], 0.0)
            out = jnp.where(spare[None], slot[None], out.reshape(SPACES, 8, N))
            out_ref[:, h * N : (h + 1) * N] = out.reshape(SPACES * 8, N)
    else:
        out_ref[:, :N] = out_a
        out_ref[:, N:] = out_b


def gelu_kernel(got_ref, field_ref, cot_ref, mix_ref, bias_ref, own_ref, own_t_ref, up_ref, down_ref, block_ref, act_ref, grad_ref, out_ref):
    forth = grow_mix(dot_nt(own_ref[...], mix_ref[...]), own_t_ref[...])
    bias, up = bias_column(bias_ref), up_ref[...]
    moments = jnp.zeros((CY, CY), F32)
    for s in range(S):
        spectral = synth_depth(got_ref, s, up)
        field = jnp.concatenate([field_ref[s * PLANES + x] for x in range(PLANES)], 1)
        linear = dot(forth, field)
        grads = []
        for x in range(PLANES):
            at = s * PLANES + x
            lanes = slice(x * N, (x + 1) * N)
            preact = spectral[:, lanes] + linear[:, lanes] + bias
            normal_cdf = 0.5 * (1.0 + lax.erf(preact * ROOT_HALF))
            act_ref[at] = (preact * normal_cdf).astype(BF16)
            slope = normal_cdf + preact * jnp.exp(-0.5 * preact * preact) * INV_ROOT_TAU
            grad = (cot_ref[at].astype(F32) * slope).astype(BF16)
            grad_ref[at] = grad
            grads.append(grad)
        moments = moments + dot_nt(field, jnp.concatenate(grads, 1))
    analyse_depth(lambda s, x: grad_ref[s * PLANES + x], down_ref[...], out_ref)
    same = same_row(CY)
    moments = jnp.sum(jnp.where(same, moments, 0.0).reshape(C, ROWS, CY), 1)
    moments = apply_exact(moments, block_ref[...])
    same = same_row(C)
    moments = jnp.sum(jnp.where(same, moments, 0.0).reshape(C // 8, 8, CY), 1)
    for s in range(S):
        out_ref[0, s, PLANES : PLANES + 2, :] = moments[2 * s : 2 * s + 2]


def input_kernel(got_ref, grad_ref, mix_in_ref, up_ref, own_ref, own_t_ref, out_ref, mix_ref, bias_ref):
    up, own = up_ref[...], own_ref[...]
    back = grow_mix(dot(own, mix_in_ref[...]), own_t_ref[...])
    for s in range(S):
        spectral = synth_depth(got_ref, s, up)
        linear = dot(back, jnp.concatenate([grad_ref[s * PLANES + x] for x in range(PLANES)], 1))
        total = (spectral + linear).astype(BF16)
        for x in range(PLANES):
            out_ref[s * PLANES + x] = total[:, x * N : (x + 1) * N]
    rows = []
    for s in range(S):
        for x in range(2):
            rows.append(jnp.broadcast_to(got_ref[0, s, PLANES + x : PLANES + x + 1, :], (8, CY)))
    wide = jnp.concatenate(rows, 0)
    same = same_row(C)
    mix_ref[...] = apply_exact(jnp.where(same, wide, 0.0), own) * SCALE_ALL
    lead = got_ref[0, 0, PLANES + 2 : PLANES + 3, :] + got_ref[0, 1, PLANES + 2 : PLANES + 3, :]
    lead = jnp.broadcast_to(lead, (16, CY))
    bias_ref[...] = apply_exact(lead, own)[0:1] * (SCALE_ALL / SCALE_CELLS)


def land_kernel(moved_ref, bias_in_ref, mine_ref, bias_ref):
    mine_ref[...] = moved_ref[...]
    bias_ref[...] = jnp.broadcast_to(bias_in_ref[...], (8, C))


def outer_kernel(keep_ref, other_ref, grow_in_ref, grow_out_ref, weight_ref):
    packed = keep_ref[...] + other_ref[...]
    part = lambda i: packed[:, i * C : (i + 1) * C]
    coeff = apply_exact(jnp.concatenate([part(0), part(2)], 0), grow_in_ref[...])
    cot = apply_exact(jnp.concatenate([part(1), part(3)], 0), grow_out_ref[...])
    half = M // 2
    real = imag = 0.0
    for s in range(S):
        cr, ci = coeff[s * M : s * M + half], coeff[s * M + half : (s + 1) * M]
        dr, di = cot[s * M : s * M + half], cot[s * M + half : (s + 1) * M]
        real = real + (cr * dr + ci * di)
        imag = imag + (cr * di - ci * dr)
    weight_ref[:, 0, 0] = real * (1.0 / math.sqrt(S))
    weight_ref[:, 1, 0] = imag * (1.0 / math.sqrt(S))


def call(kernel, outs, *operands, flops=50_000_000, far_in=(), far_out=(), scratch=(), room=24):
    shapes = [jax.ShapeDtypeStruct(shape, kind) for shape, kind in outs]
    operands = [jnp.asarray(x) for x in operands]
    size = sum(math.prod(x.shape) * x.dtype.itemsize for x in operands + shapes)
    near, far = pl.BlockSpec(memory_space=pltpu.VMEM), pl.BlockSpec(memory_space=pltpu.HBM)
    return pl.pallas_call(
        kernel,
        out_shape=shapes,
        in_specs=[far if i in far_in else near for i in range(len(operands))],
        out_specs=[far if i in far_out else near for i in range(len(shapes))],
        scratch_shapes=list(scratch),
        compiler_params=pltpu.CompilerParams(vmem_limit_bytes=room * 1024 * 1024),
        cost_estimate=pl.CostEstimate(flops=flops, bytes_accessed=size, transcendentals=0),
    )(*operands)


def swap(value, axis):
    return lax.all_to_all(value, axis, 0, 0, tiled=True)


def on_device(features, cotangent, spectral_weight, mix_weight, bias_term):
    planes = S * PLANES
    field = features.reshape(planes, CY, N)
    cot = cotangent.reshape(planes, CY, N)
    held = lambda rows: (pltpu.VMEM((GROUPS, rows, N), F32),)
    line = lambda rows: (pltpu.VMEM((GROUPS * rows, N), F32),)
    crossing = []
    for kz in range(M):
        for e in range(GROUPS):
            kx, place = placed(kz, e)
            for h in range(2):
                crossing.append(((2 * kx + h) * GROUPS + kz, (2 * kz + h) * GROUPS + place))
    pairing = [(i, i ^ 1) for i in range(SPACES)]
    cross = lambda v: lax.ppermute(v, ("space", "dp"), crossing)
    cross_home = lambda v: lax.ppermute(v, ("space", "dp"), [(b, a) for a, b in crossing])
    partner = lambda v: lax.ppermute(v, "space", pairing)

    depth_shape = ((M, S, 2 * PLANES, CY), F32)
    short_shape, plane_shape = ((GROUPS, 4, N), F32), ((GROUPS, 8, N), F32)
    space_shape = ((SPACES * 2 * PLANES, CY), F32)
    flat = lambda v: v.reshape(SPACES * 2 * PLANES, CY)

    def over_space(v):
        return swap(v.reshape(SPACES, 2 * PLANES, CY), "space")

    def over_dp(v):
        return swap(v, "dp")

    planes_scratch = pltpu.VMEM((planes, CY, N), BF16)
    (depth,) = call(
        depth_kernel, [depth_shape], field, Z_DOWN, room=60,
    )
    weight = spectral_weight.reshape(M // 2, 2, CO).astype(F32).transpose(1, 0, 2)
    mine = cross(weight)
    got = flat(over_space(depth))
    (plane,) = call(lambda *r: plane_kernel(False, *r), [short_shape], got, X_DOWN_4, scratch=held(4))
    mine, bias = call(land_kernel, [((2, M // 2, CO), F32), ((8, C), F32)], mine, bias_term.reshape(1, C), flops=5000000000)
    other = partner(mine)
    got = over_dp(plane)
    mixed, coeff = call(
        mix_kernel, [short_shape, ((2 * M, CY), F32)],
        got, mine, other, Y_DOWN_4, Y_UP_4, ROW_COS, ROW_SIN, GROW_IN, SUM_OUT, scratch=line(4),
    )
    got = over_dp(mixed)
    (spread,) = call(lambda *r: spread_kernel(False, *r), [space_shape], got, X_UP_A_4, X_UP_B_4, scratch=held(4) + line(4))
    got = over_space(spread).reshape(M, S, 2 * PLANES, CY)
    wide = ((planes, CY, N), BF16)
    activated, grad, depth = call(
        gelu_kernel, [wide, wide, depth_shape],
        got, field, cot, mix_weight, bias, OWN, OWN_T, Z_UP, Z_DOWN, BLOCK,
    )
    got = flat(over_space(depth))
    (plane,) = call(lambda *r: plane_kernel(True, *r), [plane_shape], got, X_DOWN, scratch=held(8))
    got = over_dp(plane)
    mixed, packed = call(
        back_kernel, [plane_shape, ((2, M, N), F32)],
        got, mine, other, Y_DOWN, Y_UP, ROW_COS, ROW_SIN, GROW_OUT, SUM_IN, PACK, coeff,
    )
    half = ((M, N), F32)
    keep, send = call(part_kernel, [half, half], cross_home(packed), flops=5_000_000_000)
    other = partner(send)
    got = over_dp(mixed)
    (spread,) = call(lambda *r: spread_kernel(True, *r), [space_shape], got, X_UP_A, X_UP_B, scratch=held(8) + line(8))
    got = over_space(spread).reshape(M, S, 2 * PLANES, CY)
    grad_input, grad_mix, grad_bias = call(
        input_kernel, [wide, ((C, C), F32), ((1, C), F32)],
        got, grad, mix_weight, Z_UP, OWN, OWN_T,
    )
    (grad_weight,) = call(outer_kernel, [((M // 2, 2, 1, CO), F32)], keep, other, PAIR_IN, PAIR_OUT)
    return (
        activated.reshape(features.shape),
        grad_input.reshape(features.shape),
        grad_weight,
        grad_mix,
        grad_bias.reshape(C),
    )


def solution(mesh):
    field = P(None, "space", None, "dp", None)
    modes = P("space", None, "dp", None)
    return jax.shard_map(
        on_device,
        mesh=mesh,
        in_specs=(field, field, modes, P(), P()),
        out_specs=(field, field, modes, P(), P()),
        check_vma=False,
    )
```

```python
import math

import jax
import jax.numpy as jnp
import ml_dtypes
import numpy as np
from jax import lax
from jax.experimental import pallas as pl
from jax.experimental.pallas import tpu as pltpu
from jax.sharding import PartitionSpec as P

S, C, N, M = 2, 32, 128, 16
PLANES, ROWS = 4, 8
SPACES, GROUPS = 32, 16
CY = C * ROWS
CO = C * C
BF16, F32 = jnp.bfloat16, jnp.float32
ROOT_HALF = 0.7071067811865476
INV_ROOT_TAU = 0.3989422804014327
SCALE_CELLS = 1.0 / math.sqrt(N * N * N)
SCALE_MODES = 1.0 / math.sqrt(M * M * M)
SCALE_ALL = 1.0 / math.sqrt(N * N * N * S)


def rotation(modes, places):
    phases = modes[:, None] * places[None, :] % N
    angles = phases.astype(np.float32) * np.float32(2.0 * math.pi / N)
    return np.cos(angles.astype(np.float64)), np.sin(angles.astype(np.float64))


def narrow(table):
    return table.astype(np.float32).astype(ml_dtypes.bfloat16)


def halves(table):
    high = narrow(table)
    return high, narrow(table.astype(np.float32) - high.astype(np.float32))


def triple(table):
    high, low = halves(table)
    return np.concatenate([high, high, low], 1)


DEPTH = np.arange(M)
SIGNED = np.where(DEPTH < M // 2, DEPTH, DEPTH - M)
PLACES = np.arange(N)
EYE_XL = np.eye(PLANES)


def z_tables():
    cosine, sine = rotation(DEPTH, PLACES)
    both = np.stack([cosine, -sine], 1).astype(np.float32)
    spread = lambda t: np.einsum("krz,xw->krxwz", t, EYE_XL).reshape(M * 2 * PLANES, PLANES * N)
    forward = spread(narrow(both).astype(np.float32)).astype(ml_dtypes.bfloat16)
    high, low = halves(spread(both))
    return forward, np.concatenate([high, high, low], 0)


def turn(cosine, sine, sign):
    return np.stack([np.stack([cosine, -sign * sine]), np.stack([sign * sine, cosine])])


EYE_CH = np.eye(2)


def x_tables():
    cosine, sine = rotation(SIGNED, PLACES)
    down = turn(cosine, sine, -1).reshape(2, 2, M, SPACES, PLANES) * SCALE_CELLS
    analyse = np.zeros((2, M, 4, 2, SPACES, 2, PLANES))
    for h in range(2):
        for q in range(2):
            analyse[h, :, 2 * q + h, 0] = np.transpose(down[q], (1, 2, 0, 3))
    analyse = analyse[:, :, :, 0].reshape(2, M, 4, SPACES * 2 * PLANES)
    wide = np.zeros((2, M, 8, SPACES * 2 * PLANES))
    wide[:, :, :4] = analyse
    wide = wide.reshape(2, M * 8, -1)
    analyse = np.concatenate([triple(wide[0]), triple(wide[1])], 1)
    up = turn(cosine, sine, 1).reshape(2, 2, M, SPACES, PLANES) * SCALE_MODES
    synth = np.zeros((2, SPACES, 2, PLANES, M, 8))
    for h in range(2):
        for r in range(2):
            synth[h, :, :, :, :, 2 * r + h] = np.transpose(up[:, r], (2, 0, 3, 1))
    synth = synth.reshape(2, SPACES * 2 * PLANES, M * 8)
    return analyse, triple(synth[0]), triple(synth[1])


def y_tables():
    cosine, sine = rotation(SIGNED, np.arange(GROUPS) * ROWS)
    down = turn(cosine, sine, -1)
    analyse = np.zeros((2, 2, M, GROUPS, 8))
    for h in range(2):
        for r in range(2):
            analyse[h, :, :, :, 2 * r + h] = down[:, r]
    analyse = triple(analyse.reshape(2 * 2 * M, GROUPS * 8))
    up = turn(cosine, sine, 1)
    synth = np.zeros((2, GROUPS, 8, 2, M))
    for h in range(2):
        for q in range(2):
            synth[h, :, 2 * q + h] = np.transpose(up[q], (2, 0, 1))
    synth = synth.reshape(2, GROUPS * 8, 2 * M)
    synth = np.concatenate([triple(synth[0]), triple(synth[1])], 1)
    cosine, sine = rotation(SIGNED, np.arange(CY) % ROWS)
    return analyse, synth, cosine.astype(np.float32), sine.astype(np.float32)


def channel_tables():
    first = np.repeat(np.arange(C), ROWS)
    pair_in = np.repeat(np.arange(C), C)
    pair_out = np.tile(np.arange(C), C)
    grow_in = narrow((first[:, None] == pair_in[None, :]).astype(np.float32))
    grow_out = narrow((first[:, None] == pair_out[None, :]).astype(np.float32))
    own = narrow((first[:, None] == np.arange(C)[None, :]).astype(np.float32))
    block = narrow((first[:, None] == first[None, :]).astype(np.float32))
    return grow_in, grow_out, own, block


Z_DOWN, Z_UP = z_tables()
X_DOWN, X_UP_A, X_UP_B = x_tables()
Y_DOWN, Y_UP, ROW_COS, ROW_SIN = y_tables()
GROW_IN, GROW_OUT, OWN, BLOCK = channel_tables()
SUM_IN = np.ascontiguousarray(GROW_IN.T)
SUM_OUT = np.ascontiguousarray(GROW_OUT.T)
PACK = np.zeros((2, C, ROWS, 4 * N // 2), OWN.dtype)
for _c in range(C):
    for _s in range(S):
        for _i in range(2):
            PACK[_i, _c, :, _s * N + (2 * _s + _i) * C + _c] = 1
PACK = PACK.reshape(2 * CY, 2 * N)
PAIR_IN = np.ascontiguousarray(GROW_IN[::ROWS])
PAIR_OUT = np.ascontiguousarray(GROW_OUT[::ROWS])
OWN_T = np.ascontiguousarray(OWN.T)
X_DOWN_4 = X_DOWN.reshape(M, 8, -1)[:, :4].reshape(M * 4, -1)
Y_DOWN_4 = Y_DOWN.reshape(-1, 3, GROUPS, 8)[..., :4].reshape(4 * M, -1)
Y_UP_4 = Y_UP.reshape(GROUPS, 8, -1)[:, :4].reshape(GROUPS * 4, -1)
X_UP_A_4 = X_UP_A.reshape(-1, 3, M, 8)[..., :4].reshape(SPACES * 8, -1)
X_UP_B_4 = X_UP_B.reshape(-1, 3, M, 8)[..., :4].reshape(SPACES * 8, -1)


SIDE = 4


def plane_steps():
    hops = lambda d, n: min(d, n - d)
    steps = [(y, x) for y in range(SIDE) for x in range(SIDE)]
    steps.sort(key=lambda s: -(hops(s[0], SIDE) + hops(s[1], SIDE)))
    places = sorted(range(GROUPS), key=lambda e: hops(e, GROUPS))
    out = [None] * GROUPS
    for place, step in zip(places, steps):
        out[place] = step
    return out


PLANE_STEPS = plane_steps()


def placed(kz, e):
    dy, dx = PLANE_STEPS[e]
    kx = (kz // SIDE + dy) % SIDE * SIDE + (kz % SIDE + dx) % SIDE
    return kx, (kz + e) % GROUPS


def dot(a, b):
    return jnp.dot(a, b, preferred_element_type=F32)


def dot_nt(a, b):
    return lax.dot_general(a, b, (((1,), (1,)), ((), ())), preferred_element_type=F32)


def split(value):
    high = value.astype(BF16)
    return high, (value - high.astype(F32)).astype(BF16)


def stack3(value):
    high, low = split(value)
    return jnp.concatenate([high, low, high], 0)


def apply_exact(value, table):
    high, low = split(value)
    both = dot(jnp.concatenate([high, low], 0), table)
    rows = value.shape[0]
    return both[:rows] + both[rows:]


def row_ids(shape):
    return lax.broadcasted_iota(jnp.int32, shape, len(shape) - 2)


def lane_ids(shape):
    return lax.broadcasted_iota(jnp.int32, shape, len(shape) - 1)


def analyse_depth(planes, table, out_ref, copies=None):
    for s in range(S):
        if copies is not None:
            copies[s].wait()
        field = jnp.concatenate([planes(s, x) for x in range(PLANES)], 1)
        out_ref[:, s] = dot_nt(table, field).reshape(M, 2 * PLANES, CY)


def synth_depth(got_ref, s, table):
    rows = got_ref[:, s].reshape(M * 2 * PLANES, CY)
    high, low = split(rows.T)
    return dot(jnp.concatenate([high, low, high], 1), table)


def sample_copies(source, target, sems, base):
    out = []
    for s in range(S):
        part = pl.ds(s * PLANES, PLANES)
        out.append(pltpu.make_async_copy(source.at[part], target.at[part], sems.at[base + s]))
    return out


def depth_kernel(field_ref, table_ref, out_ref):
    analyse_depth(lambda s, x: field_ref[s * PLANES + x], table_ref[...], out_ref)


def same_row(rows):
    return row_ids((rows, CY)) % ROWS == lane_ids((rows, CY)) % ROWS


def grow_mix(mix_rows, own_t):
    return jnp.where(same_row(CY), dot(mix_rows.astype(BF16), own_t), 0.0).astype(BF16)


def bias_column(bias_ref):
    bias = jnp.broadcast_to(bias_ref[0:1], (CY, C))
    picked = jnp.where(lane_ids((CY, C)) == row_ids((CY, C)) // ROWS, bias, 0.0)
    return jnp.sum(picked, 1, keepdims=True)


def put_blocks(value, blocks_ref):
    rows = blocks_ref.shape[1]
    for i in range(GROUPS):
        blocks_ref[i] = value[i * rows : (i + 1) * rows]


def take_blocks(blocks_ref, flat_ref):
    rows = blocks_ref.shape[1]
    for i in range(GROUPS):
        flat_ref[i * rows : (i + 1) * rows, :] = blocks_ref[i]
    return flat_ref[...]


def plane_kernel(with_sums, got_ref, table_ref, out_ref, held_ref):
    got = got_ref[...]
    data = got
    if with_sums:
        lead = lax.axis_index("space") < S
        spare = (row_ids(got.shape) % (2 * PLANES) >= PLANES) & lead
        data = jnp.where(spare, 0.0, got)
    half = N
    stacked = jnp.concatenate([stack3(data[:, :half]), stack3(data[:, half:])], 0)
    out = dot(table_ref[...], stacked)
    if with_sums:
        total = jnp.sum(got.reshape(SPACES, 2 * PLANES, CY), 0)
        rows = row_ids((8, half))
        pair = []
        for x in range(2):
            own = total[PLANES + x : PLANES + x + 1]
            pair.append(
                jnp.where(rows == 4, own[:, :half], 0.0) + jnp.where(rows == 5, own[:, half:], 0.0)
            )
        pair = jnp.concatenate(pair, 0)
        out = (out.reshape(GROUPS // 2, 16, half) + pair[None]).reshape(GROUPS * 8, half)
    kz = lax.axis_index("space") // 2
    put_blocks(out, held_ref)
    for e in range(GROUPS):
        kx, place = placed(kz, e)
        out_ref[place] = held_ref[kx]


def row_spectrum(got, table_ref, cos_ref, sin_ref):
    flat = dot(table_ref[...], stack3(got))
    real = jnp.concatenate([flat[0:M], flat[2 * M : 3 * M]], 1)
    imag = jnp.concatenate([flat[M : 2 * M], flat[3 * M :]], 1)
    cosine, sine = cos_ref[...], sin_ref[...]
    return real * cosine + imag * sine, imag * cosine - real * sine


def weight_rows(mine_ref, other_ref):
    even = lax.axis_index("space") % 2 == 0
    mine, other = mine_ref[...], other_ref[...]
    first = jnp.where(even, mine, other)
    second = jnp.where(even, other, mine)
    whole = jnp.concatenate([first, second], 1)
    return whole[0], whole[1]


def row_synth(real, imag, table_ref, cos_ref, sin_ref):
    cosine, sine = cos_ref[...], sin_ref[...]
    turned = jnp.concatenate([real * cosine - imag * sine, imag * cosine + real * sine], 0)
    stacked = jnp.concatenate([stack3(turned[:, :N]), stack3(turned[:, N:])], 0)
    return dot(table_ref[...], stacked)


def mix_kernel(got_ref, mine_ref, other_ref, down_ref, up_ref, cos_ref, sin_ref, grow_ref, sum_ref, out_ref, spectrum_ref, flat_ref):
    real, imag = row_spectrum(take_blocks(got_ref, flat_ref), down_ref, cos_ref, sin_ref)
    spectrum = jnp.concatenate([real, imag], 0)
    spectrum_ref[...] = spectrum
    coeff = apply_exact(spectrum, grow_ref[...])
    cr, ci = coeff[:M], coeff[M:]
    wr, wi = weight_rows(mine_ref, other_ref)
    mixed = apply_exact(jnp.concatenate([cr * wr - ci * wi, cr * wi + ci * wr], 0), sum_ref[...])
    put_blocks(row_synth(mixed[:M], mixed[M:], up_ref, cos_ref, sin_ref), out_ref)


def back_kernel(got_ref, mine_ref, other_ref, down_ref, up_ref, cos_ref, sin_ref, grow_ref, sum_ref, pack_ref, coeff_ref, out_ref, packed_ref):
    real, imag = row_spectrum(got_ref[...].reshape(GROUPS * 8, N), down_ref, cos_ref, sin_ref)
    spectrum = jnp.concatenate([real, imag], 0)
    pack(coeff_ref[...], spectrum, pack_ref[...], packed_ref)
    cot = apply_exact(spectrum, grow_ref[...])
    dr, di = cot[:M], cot[M:]
    wr, wi = weight_rows(mine_ref, other_ref)
    back = apply_exact(jnp.concatenate([dr * wr + di * wi, di * wr - dr * wi], 0), sum_ref[...])
    out = row_synth(back[:M], back[M:], up_ref, cos_ref, sin_ref)
    total = jnp.sum(got_ref[...], 0)
    rows = row_ids((8, N))
    extra = jnp.where((rows == 4) | (rows == 5), total, 0.0)
    extra = extra + jnp.where(rows == 6, real[0:1, :N], 0.0) + jnp.where(rows == 7, real[0:1, N:], 0.0)
    out_ref[...] = out.reshape(GROUPS, 8, N) + extra[None]


def pack(coeff, cot, table, out_ref):
    even = lax.axis_index("space") % 2 == 0
    packed = apply_exact(jnp.concatenate([coeff, cot], 1), table)
    packed = jnp.where(even, packed[:, :N], packed[:, N:])
    half = M // 2
    low = jnp.concatenate([packed[:half], packed[M : M + half]], 0)
    high = jnp.concatenate([packed[half:M], packed[M + half :]], 0)
    out_ref[0] = jnp.where(even, low, high)
    out_ref[1] = jnp.where(even, high, low)


def part_kernel(moved_ref, keep_ref, send_ref):
    keep_ref[...] = moved_ref[0]
    send_ref[...] = moved_ref[1]


def spread_kernel(with_sums, got_ref, table_a_ref, table_b_ref, out_ref, held_ref, flat_ref):
    kz = lax.axis_index("space") // 2
    for e in range(GROUPS):
        kx, place = placed(kz, e)
        held_ref[kx] = got_ref[place]
    got = take_blocks(held_ref, flat_ref)
    stacked = stack3(got)
    out_a = dot(table_a_ref[...], stacked)
    out_b = dot(table_b_ref[...], stacked)
    if with_sums:
        lead = lax.axis_index("space") < S
        rows = row_ids((8, N))
        spare = (rows >= PLANES) & lead
        for h, out in enumerate((out_a, out_b)):
            slot = jnp.where(rows == 4, got[4 + h : 5 + h], 0.0)
            slot = slot + jnp.where(rows == 5, got[12 + h : 13 + h], 0.0)
            slot = slot + jnp.where(rows == 6, got[6 + h : 7 + h], 0.0)
            out = jnp.where(spare[None], slot[None], out.reshape(SPACES, 8, N))
            out_ref[:, h * N : (h + 1) * N] = out.reshape(SPACES * 8, N)
    else:
        out_ref[:, :N] = out_a
        out_ref[:, N:] = out_b


def gelu_kernel(got_ref, field_ref, cot_ref, mix_ref, bias_ref, own_ref, own_t_ref, up_ref, down_ref, block_ref, act_ref, grad_ref, out_ref):
    forth = grow_mix(dot_nt(own_ref[...], mix_ref[...]), own_t_ref[...])
    bias, up = bias_column(bias_ref), up_ref[...]
    moments = jnp.zeros((CY, CY), F32)
    for s in range(S):
        spectral = synth_depth(got_ref, s, up)
        field = jnp.concatenate([field_ref[s * PLANES + x] for x in range(PLANES)], 1)
        linear = dot(forth, field)
        grads = []
        for x in range(PLANES):
            at = s * PLANES + x
            lanes = slice(x * N, (x + 1) * N)
            preact = spectral[:, lanes] + linear[:, lanes] + bias
            normal_cdf = 0.5 * (1.0 + lax.erf(preact * ROOT_HALF))
            act_ref[at] = (preact * normal_cdf).astype(BF16)
            slope = normal_cdf + preact * jnp.exp(-0.5 * preact * preact) * INV_ROOT_TAU
            grad = (cot_ref[at].astype(F32) * slope).astype(BF16)
            grad_ref[at] = grad
            grads.append(grad)
        moments = moments + dot_nt(field, jnp.concatenate(grads, 1))
    analyse_depth(lambda s, x: grad_ref[s * PLANES + x], down_ref[...], out_ref)
    same = same_row(CY)
    moments = jnp.sum(jnp.where(same, moments, 0.0).reshape(C, ROWS, CY), 1)
    moments = apply_exact(moments, block_ref[...])
    same = same_row(C)
    moments = jnp.sum(jnp.where(same, moments, 0.0).reshape(C // 8, 8, CY), 1)
    for s in range(S):
        out_ref[0, s, PLANES : PLANES + 2, :] = moments[2 * s : 2 * s + 2]


def store_kernel(held_ref, after_ref, out_ref):
    del after_ref
    out_ref[...] = held_ref[...]


def linear_kernel(grad_ref, back_ref, after_ref, out_ref):
    del after_ref
    for s in range(S):
        grad = jnp.concatenate([grad_ref[s * PLANES + x] for x in range(PLANES)], 1)
        out_ref[s] = dot(back_ref[...], grad)


def input_kernel(got_ref, linear_ref, up_ref, own_ref, out_ref, mix_ref, bias_ref):
    up, own = up_ref[...], own_ref[...]
    for s in range(S):
        spectral = synth_depth(got_ref, s, up)
        total = (spectral + linear_ref[s]).astype(BF16)
        for x in range(PLANES):
            out_ref[s * PLANES + x] = total[:, x * N : (x + 1) * N]
    rows = []
    for s in range(S):
        for x in range(2):
            rows.append(jnp.broadcast_to(got_ref[0, s, PLANES + x : PLANES + x + 1, :], (8, CY)))
    wide = jnp.concatenate(rows, 0)
    same = same_row(C)
    mix_ref[...] = apply_exact(jnp.where(same, wide, 0.0), own) * SCALE_ALL
    lead = got_ref[0, 0, PLANES + 2 : PLANES + 3, :] + got_ref[0, 1, PLANES + 2 : PLANES + 3, :]
    lead = jnp.broadcast_to(lead, (16, CY))
    bias_ref[...] = apply_exact(lead, own)[0:1] * (SCALE_ALL / SCALE_CELLS)


def land_kernel(moved_ref, bias_in_ref, mix_ref, own_ref, own_t_ref, mine_ref, bias_ref, back_ref):
    back_ref[...] = grow_mix(dot(own_ref[...], mix_ref[...]), own_t_ref[...])
    mine_ref[...] = moved_ref[...]
    bias_ref[...] = jnp.broadcast_to(bias_in_ref[...], (8, C))


def outer_kernel(keep_ref, other_ref, grow_in_ref, grow_out_ref, weight_ref):
    packed = keep_ref[...] + other_ref[...]
    part = lambda i: packed[:, i * C : (i + 1) * C]
    coeff = apply_exact(jnp.concatenate([part(0), part(2)], 0), grow_in_ref[...])
    cot = apply_exact(jnp.concatenate([part(1), part(3)], 0), grow_out_ref[...])
    half = M // 2
    real = imag = 0.0
    for s in range(S):
        cr, ci = coeff[s * M : s * M + half], coeff[s * M + half : (s + 1) * M]
        dr, di = cot[s * M : s * M + half], cot[s * M + half : (s + 1) * M]
        real = real + (cr * dr + ci * di)
        imag = imag + (cr * di - ci * dr)
    weight_ref[:, 0, 0] = real * (1.0 / math.sqrt(S))
    weight_ref[:, 1, 0] = imag * (1.0 / math.sqrt(S))


def call(kernel, outs, *operands, flops=50_000_000, far_in=(), far_out=(), scratch=(), room=24):
    shapes = [jax.ShapeDtypeStruct(shape, kind) for shape, kind in outs]
    operands = [jnp.asarray(x) for x in operands]
    size = sum(math.prod(x.shape) * x.dtype.itemsize for x in operands + shapes)
    near, far = pl.BlockSpec(memory_space=pltpu.VMEM), pl.BlockSpec(memory_space=pltpu.HBM)
    return pl.pallas_call(
        kernel,
        out_shape=shapes,
        in_specs=[far if i in far_in else near for i in range(len(operands))],
        out_specs=[far if i in far_out else near for i in range(len(shapes))],
        scratch_shapes=list(scratch),
        compiler_params=pltpu.CompilerParams(vmem_limit_bytes=room * 1024 * 1024),
        cost_estimate=pl.CostEstimate(flops=flops, bytes_accessed=size, transcendentals=0),
    )(*operands)


def swap(value, axis):
    return lax.all_to_all(value, axis, 0, 0, tiled=True)


def on_device(features, cotangent, spectral_weight, mix_weight, bias_term):
    planes = S * PLANES
    field = features.reshape(planes, CY, N)
    cot = cotangent.reshape(planes, CY, N)
    held = lambda rows: (pltpu.VMEM((GROUPS, rows, N), F32),)
    line = lambda rows: (pltpu.VMEM((GROUPS * rows, N), F32),)
    crossing = []
    for kz in range(M):
        for e in range(GROUPS):
            kx, place = placed(kz, e)
            for h in range(2):
                crossing.append(((2 * kx + h) * GROUPS + kz, (2 * kz + h) * GROUPS + place))
    pairing = [(i, i ^ 1) for i in range(SPACES)]
    cross = lambda v: lax.ppermute(v, ("space", "dp"), crossing)
    cross_home = lambda v: lax.ppermute(v, ("space", "dp"), [(b, a) for a, b in crossing])
    partner = lambda v: lax.ppermute(v, "space", pairing)

    depth_shape = ((M, S, 2 * PLANES, CY), F32)
    short_shape, plane_shape = ((GROUPS, 4, N), F32), ((GROUPS, 8, N), F32)
    space_shape = ((SPACES * 2 * PLANES, CY), F32)
    flat = lambda v: v.reshape(SPACES * 2 * PLANES, CY)

    def over_space(v):
        return swap(v.reshape(SPACES, 2 * PLANES, CY), "space")

    def over_dp(v):
        return swap(v, "dp")

    planes_scratch = pltpu.VMEM((planes, CY, N), BF16)
    (depth,) = call(
        depth_kernel, [depth_shape], field, Z_DOWN, room=60,
    )
    weight = spectral_weight.reshape(M // 2, 2, CO).astype(F32).transpose(1, 0, 2)
    mine = cross(weight)
    got = flat(over_space(depth))
    (plane,) = call(lambda *r: plane_kernel(False, *r), [short_shape], got, X_DOWN_4, scratch=held(4))
    mine, bias, back = call(
        land_kernel, [((2, M // 2, CO), F32), ((8, C), F32), ((CY, CY), BF16)],
        mine, bias_term.reshape(1, C), mix_weight, OWN, OWN_T, flops=5000000000)
    other = partner(mine)
    got = over_dp(plane)
    mixed, coeff = call(
        mix_kernel, [short_shape, ((2 * M, CY), F32)],
        got, mine, other, Y_DOWN_4, Y_UP_4, ROW_COS, ROW_SIN, GROW_IN, SUM_OUT, scratch=line(4),
    )
    got = over_dp(mixed)
    (spread,) = call(lambda *r: spread_kernel(False, *r), [space_shape], got, X_UP_A_4, X_UP_B_4, scratch=held(4) + line(4))
    got = over_space(spread).reshape(M, S, 2 * PLANES, CY)
    wide = ((planes, CY, N), BF16)
    activated, grad, depth = call(
        gelu_kernel, [wide, wide, depth_shape],
        got, field, cot, mix_weight, bias, OWN, OWN_T, Z_UP, Z_DOWN, BLOCK,
    )
    got = flat(over_space(depth))
    (plane,) = call(lambda *r: plane_kernel(True, *r), [plane_shape], got, X_DOWN, scratch=held(8))
    got = over_dp(plane)
    mixed, packed = call(
        back_kernel, [plane_shape, ((2, M, N), F32)],
        got, mine, other, Y_DOWN, Y_UP, ROW_COS, ROW_SIN, GROW_OUT, SUM_IN, PACK, coeff,
    )
    half = ((M, N), F32)
    keep, send = call(part_kernel, [half, half], cross_home(packed), flops=5_000_000_000)
    (activated,) = call(store_kernel, [wide], activated, keep)
    (linear,) = call(linear_kernel, [((S, CY, PLANES * N), F32)], grad, back, keep)
    other = partner(send)
    got = over_dp(mixed)
    (spread,) = call(lambda *r: spread_kernel(True, *r), [space_shape], got, X_UP_A, X_UP_B, scratch=held(8) + line(8))
    got = over_space(spread).reshape(M, S, 2 * PLANES, CY)
    grad_input, grad_mix, grad_bias = call(
        input_kernel, [wide, ((C, C), F32), ((1, C), F32)],
        got, linear, Z_UP, OWN,
    )
    (grad_weight,) = call(outer_kernel, [((M // 2, 2, 1, CO), F32)], keep, other, PAIR_IN, PAIR_OUT)
    return (
        activated.reshape(features.shape),
        grad_input.reshape(features.shape),
        grad_weight,
        grad_mix,
        grad_bias.reshape(C),
    )


def solution(mesh):
    field = P(None, "space", None, "dp", None)
    modes = P("space", None, "dp", None)
    return jax.shard_map(
        on_device,
        mesh=mesh,
        in_specs=(field, field, modes, P(), P()),
        out_specs=(field, field, modes, P(), P()),
        check_vma=False,
    )
```

```python
import math

import jax
import jax.numpy as jnp
import ml_dtypes
import numpy as np
from jax import lax
from jax.experimental import pallas as pl
from jax.experimental.pallas import tpu as pltpu
from jax.sharding import PartitionSpec as P

S, C, N, M = 2, 32, 128, 16
PLANES, ROWS = 4, 8
SPACES, GROUPS = 32, 16
CY = C * ROWS
CO = C * C
BF16, F32 = jnp.bfloat16, jnp.float32
ROOT_HALF = 0.7071067811865476
INV_ROOT_TAU = 0.3989422804014327
SCALE_CELLS = 1.0 / math.sqrt(N * N * N)
SCALE_MODES = 1.0 / math.sqrt(M * M * M)
SCALE_ALL = 1.0 / math.sqrt(N * N * N * S)


def rotation(modes, places):
    phases = modes[:, None] * places[None, :] % N
    angles = phases.astype(np.float32) * np.float32(2.0 * math.pi / N)
    return np.cos(angles.astype(np.float64)), np.sin(angles.astype(np.float64))


def narrow(table):
    return table.astype(np.float32).astype(ml_dtypes.bfloat16)


def halves(table):
    high = narrow(table)
    return high, narrow(table.astype(np.float32) - high.astype(np.float32))


def triple(table):
    high, low = halves(table)
    return np.concatenate([high, high, low], 1)


DEPTH = np.arange(M)
SIGNED = np.where(DEPTH < M // 2, DEPTH, DEPTH - M)
PLACES = np.arange(N)
EYE_XL = np.eye(PLANES)


def z_tables():
    cosine, sine = rotation(DEPTH, PLACES)
    both = np.stack([cosine, -sine], 1).astype(np.float32)
    spread = lambda t: np.einsum("krz,xw->krxwz", t, EYE_XL).reshape(M * 2 * PLANES, PLANES * N)
    forward = spread(narrow(both).astype(np.float32)).astype(ml_dtypes.bfloat16)
    high, low = halves(spread(both))
    return forward, np.concatenate([high, high, low], 0)


def turn(cosine, sine, sign):
    return np.stack([np.stack([cosine, -sign * sine]), np.stack([sign * sine, cosine])])


EYE_CH = np.eye(2)


def x_tables():
    cosine, sine = rotation(SIGNED, PLACES)
    down = turn(cosine, sine, -1).reshape(2, 2, M, SPACES, PLANES) * SCALE_CELLS
    analyse = np.zeros((2, M, 4, 2, SPACES, 2, PLANES))
    for h in range(2):
        for q in range(2):
            analyse[h, :, 2 * q + h, 0] = np.transpose(down[q], (1, 2, 0, 3))
    analyse = analyse[:, :, :, 0].reshape(2, M, 4, SPACES * 2 * PLANES)
    wide = np.zeros((2, M, 8, SPACES * 2 * PLANES))
    wide[:, :, :4] = analyse
    wide = wide.reshape(2, M * 8, -1)
    analyse = np.concatenate([triple(wide[0]), triple(wide[1])], 1)
    up = turn(cosine, sine, 1).reshape(2, 2, M, SPACES, PLANES) * SCALE_MODES
    synth = np.zeros((2, SPACES, 2, PLANES, M, 8))
    for h in range(2):
        for r in range(2):
            synth[h, :, :, :, :, 2 * r + h] = np.transpose(up[:, r], (2, 0, 3, 1))
    synth = synth.reshape(2, SPACES * 2 * PLANES, M * 8)
    return analyse, triple(synth[0]), triple(synth[1])


def y_tables():
    cosine, sine = rotation(SIGNED, np.arange(GROUPS) * ROWS)
    down = turn(cosine, sine, -1)
    analyse = np.zeros((2, 2, M, GROUPS, 8))
    for h in range(2):
        for r in range(2):
            analyse[h, :, :, :, 2 * r + h] = down[:, r]
    analyse = triple(analyse.reshape(2 * 2 * M, GROUPS * 8))
    up = turn(cosine, sine, 1)
    synth = np.zeros((2, GROUPS, 8, 2, M))
    for h in range(2):
        for q in range(2):
            synth[h, :, 2 * q + h] = np.transpose(up[q], (2, 0, 1))
    synth = synth.reshape(2, GROUPS * 8, 2 * M)
    synth = np.concatenate([triple(synth[0]), triple(synth[1])], 1)
    cosine, sine = rotation(SIGNED, np.arange(CY) % ROWS)
    return analyse, synth, cosine.astype(np.float32), sine.astype(np.float32)


def channel_tables():
    first = np.repeat(np.arange(C), ROWS)
    pair_in = np.repeat(np.arange(C), C)
    pair_out = np.tile(np.arange(C), C)
    grow_in = narrow((first[:, None] == pair_in[None, :]).astype(np.float32))
    grow_out = narrow((first[:, None] == pair_out[None, :]).astype(np.float32))
    own = narrow((first[:, None] == np.arange(C)[None, :]).astype(np.float32))
    block = narrow((first[:, None] == first[None, :]).astype(np.float32))
    return grow_in, grow_out, own, block


Z_DOWN, Z_UP = z_tables()
X_DOWN, X_UP_A, X_UP_B = x_tables()
Y_DOWN, Y_UP, ROW_COS, ROW_SIN = y_tables()
GROW_IN, GROW_OUT, OWN, BLOCK = channel_tables()
SUM_IN = np.ascontiguousarray(GROW_IN.T)
SUM_OUT = np.ascontiguousarray(GROW_OUT.T)
PACK = np.zeros((2, C, ROWS, 4 * N // 2), OWN.dtype)
for _c in range(C):
    for _s in range(S):
        for _i in range(2):
            PACK[_i, _c, :, _s * N + (2 * _s + _i) * C + _c] = 1
PACK = PACK.reshape(2 * CY, 2 * N)
PAIR_IN = np.ascontiguousarray(GROW_IN[::ROWS])
PAIR_OUT = np.ascontiguousarray(GROW_OUT[::ROWS])
OWN_T = np.ascontiguousarray(OWN.T)
X_DOWN_4 = X_DOWN.reshape(M, 8, -1)[:, :4].reshape(M * 4, -1)
Y_DOWN_4 = Y_DOWN.reshape(-1, 3, GROUPS, 8)[..., :4].reshape(4 * M, -1)
Y_UP_4 = Y_UP.reshape(GROUPS, 8, -1)[:, :4].reshape(GROUPS * 4, -1)
X_UP_A_4 = X_UP_A.reshape(-1, 3, M, 8)[..., :4].reshape(SPACES * 8, -1)
X_UP_B_4 = X_UP_B.reshape(-1, 3, M, 8)[..., :4].reshape(SPACES * 8, -1)


SIDE = 4


def plane_steps():
    hops = lambda d, n: min(d, n - d)
    steps = [(y, x) for y in range(SIDE) for x in range(SIDE)]
    steps.sort(key=lambda s: -(hops(s[0], SIDE) + hops(s[1], SIDE)))
    places = sorted(range(GROUPS), key=lambda e: hops(e, GROUPS))
    out = [None] * GROUPS
    for place, step in zip(places, steps):
        out[place] = step
    return out


PLANE_STEPS = plane_steps()


def placed(kz, e):
    dy, dx = PLANE_STEPS[e]
    kx = (kz // SIDE + dy) % SIDE * SIDE + (kz % SIDE + dx) % SIDE
    return kx, (kz + e) % GROUPS


def dot(a, b):
    return jnp.dot(a, b, preferred_element_type=F32)


def dot_nt(a, b):
    return lax.dot_general(a, b, (((1,), (1,)), ((), ())), preferred_element_type=F32)


def split(value):
    high = value.astype(BF16)
    return high, (value - high.astype(F32)).astype(BF16)


def stack3(value):
    high, low = split(value)
    return jnp.concatenate([high, low, high], 0)


def apply_exact(value, table):
    high, low = split(value)
    both = dot(jnp.concatenate([high, low], 0), table)
    rows = value.shape[0]
    return both[:rows] + both[rows:]


def row_ids(shape):
    return lax.broadcasted_iota(jnp.int32, shape, len(shape) - 2)


def lane_ids(shape):
    return lax.broadcasted_iota(jnp.int32, shape, len(shape) - 1)


def analyse_depth(planes, table, out_ref, copies=None):
    for s in range(S):
        if copies is not None:
            copies[s].wait()
        field = jnp.concatenate([planes(s, x) for x in range(PLANES)], 1)
        out_ref[:, s] = dot_nt(table, field).reshape(M, 2 * PLANES, CY)


def synth_depth(got_ref, s, table):
    rows = got_ref[:, s].reshape(M * 2 * PLANES, CY)
    high, low = split(rows.T)
    return dot(jnp.concatenate([high, low, high], 1), table)


def sample_copies(source, target, sems, base):
    out = []
    for s in range(S):
        part = pl.ds(s * PLANES, PLANES)
        out.append(pltpu.make_async_copy(source.at[part], target.at[part], sems.at[base + s]))
    return out


def depth_kernel(field_ref, table_ref, out_ref):
    analyse_depth(lambda s, x: field_ref[s * PLANES + x], table_ref[...], out_ref)


def same_row(rows):
    return row_ids((rows, CY)) % ROWS == lane_ids((rows, CY)) % ROWS


def grow_mix(mix_rows, own_t):
    return jnp.where(same_row(CY), dot(mix_rows.astype(BF16), own_t), 0.0).astype(BF16)


def bias_column(bias_ref):
    bias = jnp.broadcast_to(bias_ref[0:1], (CY, C))
    picked = jnp.where(lane_ids((CY, C)) == row_ids((CY, C)) // ROWS, bias, 0.0)
    return jnp.sum(picked, 1, keepdims=True)


def put_blocks(value, blocks_ref):
    rows = blocks_ref.shape[1]
    for i in range(GROUPS):
        blocks_ref[i] = value[i * rows : (i + 1) * rows]


def take_blocks(blocks_ref, flat_ref):
    rows = blocks_ref.shape[1]
    for i in range(GROUPS):
        flat_ref[i * rows : (i + 1) * rows, :] = blocks_ref[i]
    return flat_ref[...]


def plane_kernel(with_sums, got_ref, table_ref, out_ref, held_ref):
    got = got_ref[...]
    data = got
    if with_sums:
        lead = lax.axis_index("space") < S
        spare = (row_ids(got.shape) % (2 * PLANES) >= PLANES) & lead
        data = jnp.where(spare, 0.0, got)
    half = N
    stacked = jnp.concatenate([stack3(data[:, :half]), stack3(data[:, half:])], 0)
    out = dot(table_ref[...], stacked)
    if with_sums:
        total = jnp.sum(got.reshape(SPACES, 2 * PLANES, CY), 0)
        rows = row_ids((8, half))
        pair = []
        for x in range(2):
            own = total[PLANES + x : PLANES + x + 1]
            pair.append(
                jnp.where(rows == 4, own[:, :half], 0.0) + jnp.where(rows == 5, own[:, half:], 0.0)
            )
        pair = jnp.concatenate(pair, 0)
        out = (out.reshape(GROUPS // 2, 16, half) + pair[None]).reshape(GROUPS * 8, half)
    kz = lax.axis_index("space") // 2
    put_blocks(out, held_ref)
    for e in range(GROUPS):
        kx, place = placed(kz, e)
        out_ref[place] = held_ref[kx]


def row_spectrum(got, table_ref, cos_ref, sin_ref):
    flat = dot(table_ref[...], stack3(got))
    real = jnp.concatenate([flat[0:M], flat[2 * M : 3 * M]], 1)
    imag = jnp.concatenate([flat[M : 2 * M], flat[3 * M :]], 1)
    cosine, sine = cos_ref[...], sin_ref[...]
    return real * cosine + imag * sine, imag * cosine - real * sine


def weight_kernel(mine_ref, other_ref, out_ref):
    even = lax.axis_index("space") % 2 == 0
    mine, other = mine_ref[...], other_ref[...]
    out_ref[:, : M // 2] = jnp.where(even, mine, other)
    out_ref[:, M // 2 :] = jnp.where(even, other, mine)


def row_synth(real, imag, table_ref, cos_ref, sin_ref):
    cosine, sine = cos_ref[...], sin_ref[...]
    turned = jnp.concatenate([real * cosine - imag * sine, imag * cosine + real * sine], 0)
    stacked = jnp.concatenate([stack3(turned[:, :N]), stack3(turned[:, N:])], 0)
    return dot(table_ref[...], stacked)


def mix_kernel(got_ref, weight_ref, down_ref, up_ref, cos_ref, sin_ref, grow_ref, sum_ref, out_ref, spectrum_ref, flat_ref):
    real, imag = row_spectrum(take_blocks(got_ref, flat_ref), down_ref, cos_ref, sin_ref)
    spectrum = jnp.concatenate([real, imag], 0)
    spectrum_ref[...] = spectrum
    coeff = apply_exact(spectrum, grow_ref[...])
    cr, ci = coeff[:M], coeff[M:]
    wr, wi = weight_ref[0], weight_ref[1]
    mixed = apply_exact(jnp.concatenate([cr * wr - ci * wi, cr * wi + ci * wr], 0), sum_ref[...])
    put_blocks(row_synth(mixed[:M], mixed[M:], up_ref, cos_ref, sin_ref), out_ref)


def back_kernel(got_ref, weight_ref, down_ref, up_ref, cos_ref, sin_ref, grow_ref, sum_ref, pack_ref, coeff_ref, out_ref, packed_ref):
    real, imag = row_spectrum(got_ref[...].reshape(GROUPS * 8, N), down_ref, cos_ref, sin_ref)
    spectrum = jnp.concatenate([real, imag], 0)
    pack(coeff_ref[...], spectrum, pack_ref[...], packed_ref)
    cot = apply_exact(spectrum, grow_ref[...])
    dr, di = cot[:M], cot[M:]
    wr, wi = weight_ref[0], weight_ref[1]
    back = apply_exact(jnp.concatenate([dr * wr + di * wi, di * wr - dr * wi], 0), sum_ref[...])
    out = row_synth(back[:M], back[M:], up_ref, cos_ref, sin_ref)
    total = jnp.sum(got_ref[...], 0)
    rows = row_ids((8, N))
    extra = jnp.where((rows == 4) | (rows == 5), total, 0.0)
    extra = extra + jnp.where(rows == 6, real[0:1, :N], 0.0) + jnp.where(rows == 7, real[0:1, N:], 0.0)
    out_ref[...] = out.reshape(GROUPS, 8, N) + extra[None]


def pack(coeff, cot, table, out_ref):
    even = lax.axis_index("space") % 2 == 0
    packed = apply_exact(jnp.concatenate([coeff, cot], 1), table)
    packed = jnp.where(even, packed[:, :N], packed[:, N:])
    half = M // 2
    low = jnp.concatenate([packed[:half], packed[M : M + half]], 0)
    high = jnp.concatenate([packed[half:M], packed[M + half :]], 0)
    out_ref[0] = jnp.where(even, low, high)
    out_ref[1] = jnp.where(even, high, low)


def part_kernel(moved_ref, keep_ref, send_ref):
    keep_ref[...] = moved_ref[0]
    send_ref[...] = moved_ref[1]


def spread_kernel(with_sums, got_ref, table_a_ref, table_b_ref, out_ref, held_ref, flat_ref):
    kz = lax.axis_index("space") // 2
    for e in range(GROUPS):
        kx, place = placed(kz, e)
        held_ref[kx] = got_ref[place]
    got = take_blocks(held_ref, flat_ref)
    stacked = stack3(got)
    out_a = dot(table_a_ref[...], stacked)
    out_b = dot(table_b_ref[...], stacked)
    if with_sums:
        lead = lax.axis_index("space") < S
        rows = row_ids((8, N))
        spare = (rows >= PLANES) & lead
        for h, out in enumerate((out_a, out_b)):
            slot = jnp.where(rows == 4, got[4 + h : 5 + h], 0.0)
            slot = slot + jnp.where(rows == 5, got[12 + h : 13 + h], 0.0)
            slot = slot + jnp.where(rows == 6, got[6 + h : 7 + h], 0.0)
            out = jnp.where(spare[None], slot[None], out.reshape(SPACES, 8, N))
            out_ref[:, h * N : (h + 1) * N] = out.reshape(SPACES * 8, N)
    else:
        out_ref[:, :N] = out_a
        out_ref[:, N:] = out_b


def gelu_kernel(got_ref, field_ref, cot_ref, mix_ref, bias_ref, own_ref, own_t_ref, up_ref, down_ref, block_ref, act_ref, grad_ref, out_ref):
    forth = grow_mix(dot_nt(own_ref[...], mix_ref[...]), own_t_ref[...])
    bias, up = bias_column(bias_ref), up_ref[...]
    moments = jnp.zeros((CY, CY), F32)
    for s in range(S):
        spectral = synth_depth(got_ref, s, up)
        field = jnp.concatenate([field_ref[s * PLANES + x] for x in range(PLANES)], 1)
        linear = dot(forth, field)
        grads = []
        for x in range(PLANES):
            at = s * PLANES + x
            lanes = slice(x * N, (x + 1) * N)
            preact = spectral[:, lanes] + linear[:, lanes] + bias
            normal_cdf = 0.5 * (1.0 + lax.erf(preact * ROOT_HALF))
            act_ref[at] = (preact * normal_cdf).astype(BF16)
            slope = normal_cdf + preact * jnp.exp(-0.5 * preact * preact) * INV_ROOT_TAU
            grad = (cot_ref[at].astype(F32) * slope).astype(BF16)
            grad_ref[at] = grad
            grads.append(grad)
        moments = moments + dot_nt(field, jnp.concatenate(grads, 1))
    analyse_depth(lambda s, x: grad_ref[s * PLANES + x], down_ref[...], out_ref)
    same = same_row(CY)
    moments = jnp.sum(jnp.where(same, moments, 0.0).reshape(C, ROWS, CY), 1)
    moments = apply_exact(moments, block_ref[...])
    same = same_row(C)
    moments = jnp.sum(jnp.where(same, moments, 0.0).reshape(C // 8, 8, CY), 1)
    for s in range(S):
        out_ref[0, s, PLANES : PLANES + 2, :] = moments[2 * s : 2 * s + 2]


def store_kernel(held_ref, after_ref, out_ref):
    del after_ref
    out_ref[...] = held_ref[...]


def linear_kernel(grad_ref, back_ref, after_ref, out_ref):
    del after_ref
    for s in range(S):
        grad = jnp.concatenate([grad_ref[s * PLANES + x] for x in range(PLANES)], 1)
        out_ref[s] = dot(back_ref[...], grad)


def input_kernel(got_ref, linear_ref, up_ref, own_ref, out_ref, mix_ref, bias_ref):
    up, own = up_ref[...], own_ref[...]
    for s in range(S):
        spectral = synth_depth(got_ref, s, up)
        total = (spectral + linear_ref[s]).astype(BF16)
        for x in range(PLANES):
            out_ref[s * PLANES + x] = total[:, x * N : (x + 1) * N]
    rows = []
    for s in range(S):
        for x in range(2):
            rows.append(jnp.broadcast_to(got_ref[0, s, PLANES + x : PLANES + x + 1, :], (8, CY)))
    wide = jnp.concatenate(rows, 0)
    same = same_row(C)
    mix_ref[...] = apply_exact(jnp.where(same, wide, 0.0), own) * SCALE_ALL
    lead = got_ref[0, 0, PLANES + 2 : PLANES + 3, :] + got_ref[0, 1, PLANES + 2 : PLANES + 3, :]
    lead = jnp.broadcast_to(lead, (16, CY))
    bias_ref[...] = apply_exact(lead, own)[0:1] * (SCALE_ALL / SCALE_CELLS)


def land_kernel(moved_ref, bias_in_ref, mix_ref, own_ref, own_t_ref, mine_ref, bias_ref, back_ref):
    back_ref[...] = grow_mix(dot(own_ref[...], mix_ref[...]), own_t_ref[...])
    mine_ref[...] = moved_ref[...]
    bias_ref[...] = jnp.broadcast_to(bias_in_ref[...], (8, C))


def outer_kernel(keep_ref, other_ref, grow_in_ref, grow_out_ref, weight_ref):
    packed = keep_ref[...] + other_ref[...]
    part = lambda i: packed[:, i * C : (i + 1) * C]
    coeff = apply_exact(jnp.concatenate([part(0), part(2)], 0), grow_in_ref[...])
    cot = apply_exact(jnp.concatenate([part(1), part(3)], 0), grow_out_ref[...])
    half = M // 2
    real = imag = 0.0
    for s in range(S):
        cr, ci = coeff[s * M : s * M + half], coeff[s * M + half : (s + 1) * M]
        dr, di = cot[s * M : s * M + half], cot[s * M + half : (s + 1) * M]
        real = real + (cr * dr + ci * di)
        imag = imag + (cr * di - ci * dr)
    weight_ref[:, 0, 0] = real * (1.0 / math.sqrt(S))
    weight_ref[:, 1, 0] = imag * (1.0 / math.sqrt(S))


def call(kernel, outs, *operands, flops=50_000_000, far_in=(), far_out=(), scratch=(), room=24):
    shapes = [jax.ShapeDtypeStruct(shape, kind) for shape, kind in outs]
    operands = [jnp.asarray(x) for x in operands]
    size = sum(math.prod(x.shape) * x.dtype.itemsize for x in operands + shapes)
    near, far = pl.BlockSpec(memory_space=pltpu.VMEM), pl.BlockSpec(memory_space=pltpu.HBM)
    return pl.pallas_call(
        kernel,
        out_shape=shapes,
        in_specs=[far if i in far_in else near for i in range(len(operands))],
        out_specs=[far if i in far_out else near for i in range(len(shapes))],
        scratch_shapes=list(scratch),
        compiler_params=pltpu.CompilerParams(vmem_limit_bytes=room * 1024 * 1024),
        cost_estimate=pl.CostEstimate(flops=flops, bytes_accessed=size, transcendentals=0),
    )(*operands)


def swap(value, axis):
    return lax.all_to_all(value, axis, 0, 0, tiled=True)


def on_device(features, cotangent, spectral_weight, mix_weight, bias_term):
    planes = S * PLANES
    field = features.reshape(planes, CY, N)
    cot = cotangent.reshape(planes, CY, N)
    held = lambda rows: (pltpu.VMEM((GROUPS, rows, N), F32),)
    line = lambda rows: (pltpu.VMEM((GROUPS * rows, N), F32),)
    crossing = []
    for kz in range(M):
        for e in range(GROUPS):
            kx, place = placed(kz, e)
            for h in range(2):
                crossing.append(((2 * kx + h) * GROUPS + kz, (2 * kz + h) * GROUPS + place))
    pairing = [(i, i ^ 1) for i in range(SPACES)]
    cross = lambda v: lax.ppermute(v, ("space", "dp"), crossing)
    cross_home = lambda v: lax.ppermute(v, ("space", "dp"), [(b, a) for a, b in crossing])
    partner = lambda v: lax.ppermute(v, "space", pairing)

    depth_shape = ((M, S, 2 * PLANES, CY), F32)
    short_shape, plane_shape = ((GROUPS, 4, N), F32), ((GROUPS, 8, N), F32)
    space_shape = ((SPACES * 2 * PLANES, CY), F32)
    flat = lambda v: v.reshape(SPACES * 2 * PLANES, CY)

    def over_space(v):
        return swap(v.reshape(SPACES, 2 * PLANES, CY), "space")

    def over_dp(v):
        return swap(v, "dp")

    planes_scratch = pltpu.VMEM((planes, CY, N), BF16)
    (depth,) = call(
        depth_kernel, [depth_shape], field, Z_DOWN, room=60,
    )
    weight = spectral_weight.reshape(M // 2, 2, CO).astype(F32).transpose(1, 0, 2)
    mine = cross(weight)
    got = flat(over_space(depth))
    (plane,) = call(lambda *r: plane_kernel(False, *r), [short_shape], got, X_DOWN_4, scratch=held(4))
    mine, bias, back = call(
        land_kernel, [((2, M // 2, CO), F32), ((8, C), F32), ((CY, CY), BF16)],
        mine, bias_term.reshape(1, C), mix_weight, OWN, OWN_T, flops=5000000000)
    (weight,) = call(weight_kernel, [((2, M, CO), F32)], mine, partner(mine))
    got = over_dp(plane)
    mixed, coeff = call(
        mix_kernel, [short_shape, ((2 * M, CY), F32)],
        got, weight, Y_DOWN_4, Y_UP_4, ROW_COS, ROW_SIN, GROW_IN, SUM_OUT, scratch=line(4),
    )
    got = over_dp(mixed)
    (spread,) = call(lambda *r: spread_kernel(False, *r), [space_shape], got, X_UP_A_4, X_UP_B_4, scratch=held(4) + line(4))
    got = over_space(spread).reshape(M, S, 2 * PLANES, CY)
    wide = ((planes, CY, N), BF16)
    activated, grad, depth = call(
        gelu_kernel, [wide, wide, depth_shape],
        got, field, cot, mix_weight, bias, OWN, OWN_T, Z_UP, Z_DOWN, BLOCK,
    )
    got = flat(over_space(depth))
    (plane,) = call(lambda *r: plane_kernel(True, *r), [plane_shape], got, X_DOWN, scratch=held(8))
    got = over_dp(plane)
    mixed, packed = call(
        back_kernel, [plane_shape, ((2, M, N), F32)],
        got, weight, Y_DOWN, Y_UP, ROW_COS, ROW_SIN, GROW_OUT, SUM_IN, PACK, coeff,
    )
    half = ((M, N), F32)
    keep, send = call(part_kernel, [half, half], cross_home(packed), flops=5_000_000_000)
    (activated,) = call(store_kernel, [wide], activated, keep)
    (linear,) = call(linear_kernel, [((S, CY, PLANES * N), F32)], grad, back, keep)
    other = partner(send)
    got = over_dp(mixed)
    (spread,) = call(lambda *r: spread_kernel(True, *r), [space_shape], got, X_UP_A, X_UP_B, scratch=held(8) + line(8))
    got = over_space(spread).reshape(M, S, 2 * PLANES, CY)
    grad_input, grad_mix, grad_bias = call(
        input_kernel, [wide, ((C, C), F32), ((1, C), F32)],
        got, linear, Z_UP, OWN,
    )
    (grad_weight,) = call(outer_kernel, [((M // 2, 2, 1, CO), F32)], keep, other, PAIR_IN, PAIR_OUT)
    return (
        activated.reshape(features.shape),
        grad_input.reshape(features.shape),
        grad_weight,
        grad_mix,
        grad_bias.reshape(C),
    )


def solution(mesh):
    field = P(None, "space", None, "dp", None)
    modes = P("space", None, "dp", None)
    return jax.shard_map(
        on_device,
        mesh=mesh,
        in_specs=(field, field, modes, P(), P()),
        out_specs=(field, field, modes, P(), P()),
        check_vma=False,
    )
```

```python
import math

import jax
import jax.numpy as jnp
import ml_dtypes
import numpy as np
from jax import lax
from jax.experimental import pallas as pl
from jax.experimental.pallas import tpu as pltpu
from jax.sharding import PartitionSpec as P

S, C, N, M = 2, 32, 128, 16
PLANES, ROWS = 4, 8
SPACES, GROUPS = 32, 16
CY = C * ROWS
CO = C * C
BF16, F32 = jnp.bfloat16, jnp.float32
ROOT_HALF = 0.7071067811865476
INV_ROOT_TAU = 0.3989422804014327
SCALE_CELLS = 1.0 / math.sqrt(N * N * N)
SCALE_MODES = 1.0 / math.sqrt(M * M * M)
SCALE_ALL = 1.0 / math.sqrt(N * N * N * S)


def rotation(modes, places):
    phases = modes[:, None] * places[None, :] % N
    angles = phases.astype(np.float32) * np.float32(2.0 * math.pi / N)
    return np.cos(angles.astype(np.float64)), np.sin(angles.astype(np.float64))


def narrow(table):
    return table.astype(np.float32).astype(ml_dtypes.bfloat16)


def halves(table):
    high = narrow(table)
    return high, narrow(table.astype(np.float32) - high.astype(np.float32))


def triple(table):
    high, low = halves(table)
    return np.concatenate([high, high, low], 1)


DEPTH = np.arange(M)
SIGNED = np.where(DEPTH < M // 2, DEPTH, DEPTH - M)
PLACES = np.arange(N)
EYE_XL = np.eye(PLANES)


def z_tables():
    cosine, sine = rotation(DEPTH, PLACES)
    both = np.stack([cosine, -sine], 1).astype(np.float32)
    spread = lambda t: np.einsum("krz,xw->krxwz", t, EYE_XL).reshape(M * 2 * PLANES, PLANES * N)
    forward = spread(narrow(both).astype(np.float32)).astype(ml_dtypes.bfloat16)
    high, low = halves(spread(both))
    return forward, np.concatenate([high, high, low], 0)


def turn(cosine, sine, sign):
    return np.stack([np.stack([cosine, -sign * sine]), np.stack([sign * sine, cosine])])


EYE_CH = np.eye(2)


def x_tables():
    cosine, sine = rotation(SIGNED, PLACES)
    down = turn(cosine, sine, -1).reshape(2, 2, M, SPACES, PLANES) * SCALE_CELLS
    analyse = np.zeros((2, M, 4, 2, SPACES, 2, PLANES))
    for h in range(2):
        for q in range(2):
            analyse[h, :, 2 * q + h, 0] = np.transpose(down[q], (1, 2, 0, 3))
    analyse = analyse[:, :, :, 0].reshape(2, M, 4, SPACES * 2 * PLANES)
    wide = np.zeros((2, M, 8, SPACES * 2 * PLANES))
    wide[:, :, :4] = analyse
    wide = wide.reshape(2, M * 8, -1)
    analyse = np.concatenate([triple(wide[0]), triple(wide[1])], 1)
    up = turn(cosine, sine, 1).reshape(2, 2, M, SPACES, PLANES) * SCALE_MODES
    synth = np.zeros((2, SPACES, 2, PLANES, M, 8))
    for h in range(2):
        for r in range(2):
            synth[h, :, :, :, :, 2 * r + h] = np.transpose(up[:, r], (2, 0, 3, 1))
    synth = synth.reshape(2, SPACES * 2 * PLANES, M * 8)
    return analyse, triple(synth[0]), triple(synth[1])


def y_tables():
    cosine, sine = rotation(SIGNED, np.arange(GROUPS) * ROWS)
    down = turn(cosine, sine, -1)
    analyse = np.zeros((2, 2, M, GROUPS, 8))
    for h in range(2):
        for r in range(2):
            analyse[h, :, :, :, 2 * r + h] = down[:, r]
    analyse = triple(analyse.reshape(2 * 2 * M, GROUPS * 8))
    up = turn(cosine, sine, 1)
    synth = np.zeros((2, GROUPS, 8, 2, M))
    for h in range(2):
        for q in range(2):
            synth[h, :, 2 * q + h] = np.transpose(up[q], (2, 0, 1))
    synth = synth.reshape(2, GROUPS * 8, 2 * M)
    synth = np.concatenate([triple(synth[0]), triple(synth[1])], 1)
    cosine, sine = rotation(SIGNED, np.arange(CY) % ROWS)
    return analyse, synth, cosine.astype(np.float32), sine.astype(np.float32)


def channel_tables():
    first = np.repeat(np.arange(C), ROWS)
    pair_in = np.repeat(np.arange(C), C)
    pair_out = np.tile(np.arange(C), C)
    grow_in = narrow((first[:, None] == pair_in[None, :]).astype(np.float32))
    grow_out = narrow((first[:, None] == pair_out[None, :]).astype(np.float32))
    own = narrow((first[:, None] == np.arange(C)[None, :]).astype(np.float32))
    block = narrow((first[:, None] == first[None, :]).astype(np.float32))
    return grow_in, grow_out, own, block


Z_DOWN, Z_UP = z_tables()
X_DOWN, X_UP_A, X_UP_B = x_tables()
Y_DOWN, Y_UP, ROW_COS, ROW_SIN = y_tables()
GROW_IN, GROW_OUT, OWN, BLOCK = channel_tables()
SUM_IN = np.ascontiguousarray(GROW_IN.T)
SUM_OUT = np.ascontiguousarray(GROW_OUT.T)
PACK = np.zeros((2, C, ROWS, 4 * N // 2), OWN.dtype)
for _c in range(C):
    for _s in range(S):
        for _i in range(2):
            PACK[_i, _c, :, _s * N + (2 * _s + _i) * C + _c] = 1
PACK = PACK.reshape(2 * CY, 2 * N)
PAIR_IN = np.ascontiguousarray(GROW_IN[::ROWS])
PAIR_OUT = np.ascontiguousarray(GROW_OUT[::ROWS])
OWN_T = np.ascontiguousarray(OWN.T)
X_DOWN_4 = X_DOWN.reshape(M, 8, -1)[:, :4].reshape(M * 4, -1)
Y_DOWN_4 = Y_DOWN.reshape(-1, 3, GROUPS, 8)[..., :4].reshape(4 * M, -1)
Y_UP_4 = Y_UP.reshape(GROUPS, 8, -1)[:, :4].reshape(GROUPS * 4, -1)
X_UP_A_4 = X_UP_A.reshape(-1, 3, M, 8)[..., :4].reshape(SPACES * 8, -1)
X_UP_B_4 = X_UP_B.reshape(-1, 3, M, 8)[..., :4].reshape(SPACES * 8, -1)


SIDE = 4


def plane_steps():
    hops = lambda d, n: min(d, n - d)
    steps = [(y, x) for y in range(SIDE) for x in range(SIDE)]
    steps.sort(key=lambda s: -(hops(s[0], SIDE) + hops(s[1], SIDE)))
    places = sorted(range(GROUPS), key=lambda e: hops(e, GROUPS))
    out = [None] * GROUPS
    for place, step in zip(places, steps):
        out[place] = step
    return out


PLANE_STEPS = plane_steps()


def placed(kz, e):
    dy, dx = PLANE_STEPS[e]
    kx = (kz // SIDE + dy) % SIDE * SIDE + (kz % SIDE + dx) % SIDE
    return kx, (kz + e) % GROUPS


def dot(a, b):
    return jnp.dot(a, b, preferred_element_type=F32)


def dot_nt(a, b):
    return lax.dot_general(a, b, (((1,), (1,)), ((), ())), preferred_element_type=F32)


def split(value):
    high = value.astype(BF16)
    return high, (value - high.astype(F32)).astype(BF16)


def stack3(value):
    high, low = split(value)
    return jnp.concatenate([high, low, high], 0)


def apply_exact(value, table):
    high, low = split(value)
    both = dot(jnp.concatenate([high, low], 0), table)
    rows = value.shape[0]
    return both[:rows] + both[rows:]


def row_ids(shape):
    return lax.broadcasted_iota(jnp.int32, shape, len(shape) - 2)


def lane_ids(shape):
    return lax.broadcasted_iota(jnp.int32, shape, len(shape) - 1)


def analyse_depth(planes, table, out_ref, copies=None):
    for s in range(S):
        if copies is not None:
            copies[s].wait()
        field = jnp.concatenate([planes(s, x) for x in range(PLANES)], 1)
        out_ref[:, s] = dot_nt(table, field).reshape(M, 2 * PLANES, CY)


def synth_depth(got_ref, s, table):
    rows = got_ref[:, s].reshape(M * 2 * PLANES, CY)
    high, low = split(rows.T)
    return dot(jnp.concatenate([high, low, high], 1), table)


def sample_copies(source, target, sems, base):
    out = []
    for s in range(S):
        part = pl.ds(s * PLANES, PLANES)
        out.append(pltpu.make_async_copy(source.at[part], target.at[part], sems.at[base + s]))
    return out


def depth_kernel(field_ref, table_ref, out_ref):
    analyse_depth(lambda s, x: field_ref[s * PLANES + x], table_ref[...], out_ref)


def same_row(rows):
    return row_ids((rows, CY)) % ROWS == lane_ids((rows, CY)) % ROWS


def grow_mix(mix_rows, own_t):
    return jnp.where(same_row(CY), dot(mix_rows.astype(BF16), own_t), 0.0).astype(BF16)


def bias_column(bias_ref):
    bias = jnp.broadcast_to(bias_ref[...], (CY, C))
    picked = jnp.where(lane_ids((CY, C)) == row_ids((CY, C)) // ROWS, bias, 0.0)
    return jnp.sum(picked, 1, keepdims=True)


def put_blocks(value, blocks_ref):
    rows = blocks_ref.shape[1]
    for i in range(GROUPS):
        blocks_ref[i] = value[i * rows : (i + 1) * rows]


def take_blocks(blocks_ref, flat_ref):
    rows = blocks_ref.shape[1]
    for i in range(GROUPS):
        flat_ref[i * rows : (i + 1) * rows, :] = blocks_ref[i]
    return flat_ref[...]


def plane_kernel(with_sums, got_ref, table_ref, out_ref, held_ref):
    got = got_ref[...]
    data = got
    if with_sums:
        lead = lax.axis_index("space") < S
        spare = (row_ids(got.shape) % (2 * PLANES) >= PLANES) & lead
        data = jnp.where(spare, 0.0, got)
    half = N
    stacked = jnp.concatenate([stack3(data[:, :half]), stack3(data[:, half:])], 0)
    out = dot(table_ref[...], stacked)
    if with_sums:
        total = jnp.sum(got.reshape(SPACES, 2 * PLANES, CY), 0)
        rows = row_ids((8, half))
        pair = []
        for x in range(2):
            own = total[PLANES + x : PLANES + x + 1]
            pair.append(
                jnp.where(rows == 4, own[:, :half], 0.0) + jnp.where(rows == 5, own[:, half:], 0.0)
            )
        pair = jnp.concatenate(pair, 0)
        out = (out.reshape(GROUPS // 2, 16, half) + pair[None]).reshape(GROUPS * 8, half)
    kz = lax.axis_index("space") // 2
    put_blocks(out, held_ref)
    for e in range(GROUPS):
        kx, place = placed(kz, e)
        out_ref[place] = held_ref[kx]


def row_spectrum(got, table_ref, cos_ref, sin_ref):
    flat = dot(table_ref[...], stack3(got))
    real = jnp.concatenate([flat[0:M], flat[2 * M : 3 * M]], 1)
    imag = jnp.concatenate([flat[M : 2 * M], flat[3 * M :]], 1)
    cosine, sine = cos_ref[...], sin_ref[...]
    return real * cosine + imag * sine, imag * cosine - real * sine


def weight_kernel(mine_ref, other_ref, out_ref):
    even = lax.axis_index("space") % 2 == 0
    mine, other = mine_ref[...], other_ref[...]
    out_ref[:, : M // 2] = jnp.where(even, mine, other)
    out_ref[:, M // 2 :] = jnp.where(even, other, mine)


def row_synth(real, imag, table_ref, cos_ref, sin_ref):
    cosine, sine = cos_ref[...], sin_ref[...]
    turned = jnp.concatenate([real * cosine - imag * sine, imag * cosine + real * sine], 0)
    stacked = jnp.concatenate([stack3(turned[:, :N]), stack3(turned[:, N:])], 0)
    return dot(table_ref[...], stacked)


def mix_kernel(got_ref, weight_ref, down_ref, up_ref, cos_ref, sin_ref, grow_ref, sum_ref, out_ref, spectrum_ref, flat_ref):
    real, imag = row_spectrum(take_blocks(got_ref, flat_ref), down_ref, cos_ref, sin_ref)
    spectrum = jnp.concatenate([real, imag], 0)
    spectrum_ref[...] = spectrum
    coeff = apply_exact(spectrum, grow_ref[...])
    cr, ci = coeff[:M], coeff[M:]
    wr, wi = weight_ref[0], weight_ref[1]
    mixed = apply_exact(jnp.concatenate([cr * wr - ci * wi, cr * wi + ci * wr], 0), sum_ref[...])
    put_blocks(row_synth(mixed[:M], mixed[M:], up_ref, cos_ref, sin_ref), out_ref)


def back_kernel(got_ref, weight_ref, down_ref, up_ref, cos_ref, sin_ref, grow_ref, sum_ref, pack_ref, coeff_ref, out_ref, packed_ref):
    real, imag = row_spectrum(got_ref[...].reshape(GROUPS * 8, N), down_ref, cos_ref, sin_ref)
    spectrum = jnp.concatenate([real, imag], 0)
    pack(coeff_ref[...], spectrum, pack_ref[...], packed_ref)
    cot = apply_exact(spectrum, grow_ref[...])
    dr, di = cot[:M], cot[M:]
    wr, wi = weight_ref[0], weight_ref[1]
    back = apply_exact(jnp.concatenate([dr * wr + di * wi, di * wr - dr * wi], 0), sum_ref[...])
    out = row_synth(back[:M], back[M:], up_ref, cos_ref, sin_ref)
    total = jnp.sum(got_ref[...], 0)
    rows = row_ids((8, N))
    extra = jnp.where((rows == 4) | (rows == 5), total, 0.0)
    extra = extra + jnp.where(rows == 6, real[0:1, :N], 0.0) + jnp.where(rows == 7, real[0:1, N:], 0.0)
    out_ref[...] = out.reshape(GROUPS, 8, N) + extra[None]


def pack(coeff, cot, table, out_ref):
    even = lax.axis_index("space") % 2 == 0
    packed = apply_exact(jnp.concatenate([coeff, cot], 1), table)
    packed = jnp.where(even, packed[:, :N], packed[:, N:])
    half = M // 2
    low = jnp.concatenate([packed[:half], packed[M : M + half]], 0)
    high = jnp.concatenate([packed[half:M], packed[M + half :]], 0)
    out_ref[0] = jnp.where(even, low, high)
    out_ref[1] = jnp.where(even, high, low)


def part_kernel(moved_ref, keep_ref, send_ref):
    keep_ref[...] = moved_ref[0]
    send_ref[...] = moved_ref[1]


def spread_kernel(with_sums, got_ref, table_a_ref, table_b_ref, out_ref, held_ref, flat_ref):
    kz = lax.axis_index("space") // 2
    for e in range(GROUPS):
        kx, place = placed(kz, e)
        held_ref[kx] = got_ref[place]
    got = take_blocks(held_ref, flat_ref)
    stacked = stack3(got)
    out_a = dot(table_a_ref[...], stacked)
    out_b = dot(table_b_ref[...], stacked)
    if with_sums:
        lead = lax.axis_index("space") < S
        rows = row_ids((8, N))
        spare = (rows >= PLANES) & lead
        for h, out in enumerate((out_a, out_b)):
            slot = jnp.where(rows == 4, got[4 + h : 5 + h], 0.0)
            slot = slot + jnp.where(rows == 5, got[12 + h : 13 + h], 0.0)
            slot = slot + jnp.where(rows == 6, got[6 + h : 7 + h], 0.0)
            out = jnp.where(spare[None], slot[None], out.reshape(SPACES, 8, N))
            out_ref[:, h * N : (h + 1) * N] = out.reshape(SPACES * 8, N)
    else:
        out_ref[:, :N] = out_a
        out_ref[:, N:] = out_b


def gelu_kernel(got_ref, field_ref, cot_ref, mix_ref, bias_ref, own_ref, own_t_ref, up_ref, down_ref, block_ref, act_ref, grad_ref, out_ref):
    forth = grow_mix(dot_nt(own_ref[...], mix_ref[...]), own_t_ref[...])
    bias, up = bias_ref[...], up_ref[...]
    moments = jnp.zeros((CY, CY), F32)
    for s in range(S):
        spectral = synth_depth(got_ref, s, up)
        field = jnp.concatenate([field_ref[s * PLANES + x] for x in range(PLANES)], 1)
        linear = dot(forth, field)
        grads = []
        for x in range(PLANES):
            at = s * PLANES + x
            lanes = slice(x * N, (x + 1) * N)
            preact = spectral[:, lanes] + linear[:, lanes] + bias
            normal_cdf = 0.5 * (1.0 + lax.erf(preact * ROOT_HALF))
            act_ref[at] = (preact * normal_cdf).astype(BF16)
            slope = normal_cdf + preact * jnp.exp(-0.5 * preact * preact) * INV_ROOT_TAU
            grad = (cot_ref[at].astype(F32) * slope).astype(BF16)
            grad_ref[at] = grad
            grads.append(grad)
        moments = moments + dot_nt(field, jnp.concatenate(grads, 1))
    analyse_depth(lambda s, x: grad_ref[s * PLANES + x], down_ref[...], out_ref)
    same = same_row(CY)
    moments = jnp.sum(jnp.where(same, moments, 0.0).reshape(C, ROWS, CY), 1)
    moments = apply_exact(moments, block_ref[...])
    same = same_row(C)
    moments = jnp.sum(jnp.where(same, moments, 0.0).reshape(C // 8, 8, CY), 1)
    for s in range(S):
        out_ref[0, s, PLANES : PLANES + 2, :] = moments[2 * s : 2 * s + 2]


def store_kernel(held_ref, after_ref, out_ref):
    del after_ref
    out_ref[...] = held_ref[...]


def linear_kernel(grad_ref, back_ref, after_ref, out_ref):
    del after_ref
    for s in range(S):
        grad = jnp.concatenate([grad_ref[s * PLANES + x] for x in range(PLANES)], 1)
        out_ref[s] = dot(back_ref[...], grad)


def input_kernel(got_ref, linear_ref, up_ref, own_ref, out_ref, mix_ref, bias_ref):
    up, own = up_ref[...], own_ref[...]
    for s in range(S):
        spectral = synth_depth(got_ref, s, up)
        total = (spectral + linear_ref[s]).astype(BF16)
        for x in range(PLANES):
            out_ref[s * PLANES + x] = total[:, x * N : (x + 1) * N]
    rows = []
    for s in range(S):
        for x in range(2):
            rows.append(jnp.broadcast_to(got_ref[0, s, PLANES + x : PLANES + x + 1, :], (8, CY)))
    wide = jnp.concatenate(rows, 0)
    same = same_row(C)
    mix_ref[...] = apply_exact(jnp.where(same, wide, 0.0), own) * SCALE_ALL
    lead = got_ref[0, 0, PLANES + 2 : PLANES + 3, :] + got_ref[0, 1, PLANES + 2 : PLANES + 3, :]
    lead = jnp.broadcast_to(lead, (16, CY))
    bias_ref[...] = apply_exact(lead, own)[0:1] * (SCALE_ALL / SCALE_CELLS)


def land_kernel(moved_ref, bias_in_ref, mix_ref, own_ref, own_t_ref, mine_ref, bias_ref, back_ref):
    back_ref[...] = grow_mix(dot(own_ref[...], mix_ref[...]), own_t_ref[...])
    mine_ref[...] = moved_ref[...]
    bias_ref[...] = jnp.broadcast_to(bias_column(bias_in_ref), (CY, N))


def outer_kernel(keep_ref, other_ref, grow_in_ref, grow_out_ref, weight_ref):
    packed = keep_ref[...] + other_ref[...]
    part = lambda i: packed[:, i * C : (i + 1) * C]
    coeff = apply_exact(jnp.concatenate([part(0), part(2)], 0), grow_in_ref[...])
    cot = apply_exact(jnp.concatenate([part(1), part(3)], 0), grow_out_ref[...])
    half = M // 2
    real = imag = 0.0
    for s in range(S):
        cr, ci = coeff[s * M : s * M + half], coeff[s * M + half : (s + 1) * M]
        dr, di = cot[s * M : s * M + half], cot[s * M + half : (s + 1) * M]
        real = real + (cr * dr + ci * di)
        imag = imag + (cr * di - ci * dr)
    weight_ref[:, 0, 0] = real * (1.0 / math.sqrt(S))
    weight_ref[:, 1, 0] = imag * (1.0 / math.sqrt(S))


def call(kernel, outs, *operands, flops=50_000_000, far_in=(), far_out=(), scratch=(), room=24):
    shapes = [jax.ShapeDtypeStruct(shape, kind) for shape, kind in outs]
    operands = [jnp.asarray(x) for x in operands]
    size = sum(math.prod(x.shape) * x.dtype.itemsize for x in operands + shapes)
    near, far = pl.BlockSpec(memory_space=pltpu.VMEM), pl.BlockSpec(memory_space=pltpu.HBM)
    return pl.pallas_call(
        kernel,
        out_shape=shapes,
        in_specs=[far if i in far_in else near for i in range(len(operands))],
        out_specs=[far if i in far_out else near for i in range(len(shapes))],
        scratch_shapes=list(scratch),
        compiler_params=pltpu.CompilerParams(vmem_limit_bytes=room * 1024 * 1024),
        cost_estimate=pl.CostEstimate(flops=flops, bytes_accessed=size, transcendentals=0),
    )(*operands)


def swap(value, axis):
    return lax.all_to_all(value, axis, 0, 0, tiled=True)


def on_device(features, cotangent, spectral_weight, mix_weight, bias_term):
    planes = S * PLANES
    field = features.reshape(planes, CY, N)
    cot = cotangent.reshape(planes, CY, N)
    held = lambda rows: (pltpu.VMEM((GROUPS, rows, N), F32),)
    line = lambda rows: (pltpu.VMEM((GROUPS * rows, N), F32),)
    crossing = []
    for kz in range(M):
        for e in range(GROUPS):
            kx, place = placed(kz, e)
            for h in range(2):
                crossing.append(((2 * kx + h) * GROUPS + kz, (2 * kz + h) * GROUPS + place))
    pairing = [(i, i ^ 1) for i in range(SPACES)]
    cross = lambda v: lax.ppermute(v, ("space", "dp"), crossing)
    cross_home = lambda v: lax.ppermute(v, ("space", "dp"), [(b, a) for a, b in crossing])
    partner = lambda v: lax.ppermute(v, "space", pairing)

    depth_shape = ((M, S, 2 * PLANES, CY), F32)
    short_shape, plane_shape = ((GROUPS, 4, N), F32), ((GROUPS, 8, N), F32)
    space_shape = ((SPACES * 2 * PLANES, CY), F32)
    flat = lambda v: v.reshape(SPACES * 2 * PLANES, CY)

    def over_space(v):
        return swap(v.reshape(SPACES, 2 * PLANES, CY), "space")

    def over_dp(v):
        return swap(v, "dp")

    planes_scratch = pltpu.VMEM((planes, CY, N), BF16)
    (depth,) = call(
        depth_kernel, [depth_shape], field, Z_DOWN, room=60,
    )
    weight = spectral_weight.reshape(M // 2, 2, CO).astype(F32).transpose(1, 0, 2)
    mine = cross(weight)
    got = flat(over_space(depth))
    (plane,) = call(lambda *r: plane_kernel(False, *r), [short_shape], got, X_DOWN_4, scratch=held(4))
    mine, bias, back = call(
        land_kernel, [((2, M // 2, CO), F32), ((CY, N), F32), ((CY, CY), BF16)],
        mine, bias_term.reshape(1, C), mix_weight, OWN, OWN_T, flops=5000000000)
    (weight,) = call(weight_kernel, [((2, M, CO), F32)], mine, partner(mine))
    got = over_dp(plane)
    mixed, coeff = call(
        mix_kernel, [short_shape, ((2 * M, CY), F32)],
        got, weight, Y_DOWN_4, Y_UP_4, ROW_COS, ROW_SIN, GROW_IN, SUM_OUT, scratch=line(4),
    )
    got = over_dp(mixed)
    (spread,) = call(lambda *r: spread_kernel(False, *r), [space_shape], got, X_UP_A_4, X_UP_B_4, scratch=held(4) + line(4))
    got = over_space(spread).reshape(M, S, 2 * PLANES, CY)
    wide = ((planes, CY, N), BF16)
    activated, grad, depth = call(
        gelu_kernel, [wide, wide, depth_shape],
        got, field, cot, mix_weight, bias, OWN, OWN_T, Z_UP, Z_DOWN, BLOCK,
    )
    got = flat(over_space(depth))
    (plane,) = call(lambda *r: plane_kernel(True, *r), [plane_shape], got, X_DOWN, scratch=held(8))
    got = over_dp(plane)
    mixed, packed = call(
        back_kernel, [plane_shape, ((2, M, N), F32)],
        got, weight, Y_DOWN, Y_UP, ROW_COS, ROW_SIN, GROW_OUT, SUM_IN, PACK, coeff,
    )
    half = ((M, N), F32)
    keep, send = call(part_kernel, [half, half], cross_home(packed), flops=5_000_000_000)
    (activated,) = call(store_kernel, [wide], activated, keep)
    (linear,) = call(linear_kernel, [((S, CY, PLANES * N), F32)], grad, back, keep)
    other = partner(send)
    got = over_dp(mixed)
    (spread,) = call(lambda *r: spread_kernel(True, *r), [space_shape], got, X_UP_A, X_UP_B, scratch=held(8) + line(8))
    got = over_space(spread).reshape(M, S, 2 * PLANES, CY)
    grad_input, grad_mix, grad_bias = call(
        input_kernel, [wide, ((C, C), F32), ((1, C), F32)],
        got, linear, Z_UP, OWN,
    )
    (grad_weight,) = call(outer_kernel, [((M // 2, 2, 1, CO), F32)], keep, other, PAIR_IN, PAIR_OUT)
    return (
        activated.reshape(features.shape),
        grad_input.reshape(features.shape),
        grad_weight,
        grad_mix,
        grad_bias.reshape(C),
    )


def solution(mesh):
    field = P(None, "space", None, "dp", None)
    modes = P("space", None, "dp", None)
    return jax.shard_map(
        on_device,
        mesh=mesh,
        in_specs=(field, field, modes, P(), P()),
        out_specs=(field, field, modes, P(), P()),
        check_vma=False,
    )
```
